32 devices in a mesh: row: 4 (over y, x), seq: 8 (over z, core).
Axes of the slice: x: 2, y: 2, z: 4, core: 2. Of those that a mesh axis runs over, the one named last changes fastest.
Arguments:
- hidden_in: bfloat16 [8, 2048, 1024], P('row', 'seq'), may hold values from -6 to 6
- lengths: int32 [8, 8], P('row'), may hold values from 1 to 2041, as said below
- norm1_gain: bfloat16 [1024], replicated, may hold values from 0.5 to 1.5
- w_qkv: bfloat16 [1024, 5120], replicated, may hold values from -0.1875 to 0.1875
- conv_w: bfloat16 [5120, 4], replicated, may hold values from -3 to 3
- w_rates: bfloat16 [1024, 24], replicated, may hold values from -0.1875 to 0.1875
- a_log: float32 [8], replicated, may hold values from -6.5 to -2.5
- dt_bias: float32 [8], replicated, may hold values from -1 to 1
- w_gate: bfloat16 [1024, 1024], replicated, may hold values from -0.1875 to 0.1875
- out_gain: bfloat16 [128], replicated, may hold values from 0.5 to 1.5
- w_out: bfloat16 [1024, 1024], replicated, may hold values from -0.25 to 0.25
- norm2_gain: bfloat16 [1024], replicated, may hold values from 0.5 to 1.5
- w_up: bfloat16 [1024, 5632], replicated, may hold values from -0.1875 to 0.1875
- w_down: bfloat16 [2816, 1024], replicated, may hold values from -0.15625 to 0.15625
- cotangent: bfloat16 [8, 2048, 1024], P('row', 'seq'), may hold values from -6 to 6
Outputs:
- layer_out: bfloat16 [8, 2048, 1024], P('row', 'seq')
- grad_x: bfloat16 [8, 2048, 1024], P('row', 'seq')
- grad_norm1_gain: float32 [1024], P('seq')
- grad_w_qkv: float32 [1024, 5120], P('seq')
- grad_conv_w: float32 [5120, 4], P('seq')
- grad_w_rates: float32 [1024, 24], P('seq')
- grad_a_log: float32 [8], replicated
- grad_dt_bias: float32 [8], replicated
- grad_w_gate: float32 [1024, 1024], P('seq')
- grad_out_gain: float32 [128], replicated
- grad_w_out: float32 [1024, 1024], P('seq')
- grad_norm2_gain: float32 [1024], P('seq')
- grad_w_up: float32 [1024, 5632], P('seq')
- grad_w_down: float32 [2816, 1024], P('seq')
The draws below stay inside these ranges and needn't reach their ends.
Inputs may be any that keep to these rules, and one draw needn't show every extreme that they name: Each row's 8 lengths are positive and sum to 2048; documents are laid end to end in the order given.
All inputs are finite; a program needn't handle non-finite values.
Results may differ from the reference program's by a relative error of at most 0.02.
Values may be sent and summed in bfloat16 or wider, within the bound.
No kernel may reach another device: no remote copies, remote signals or barrier semaphores. Data moves between devices by JAX's collectives and lax.ppermute only.
A program may use at most 384 MiB of HBM per device.

```python
import jax
import jax.numpy as jnp
from jax import lax

D = 1024
HEADS = 8
HDIM = 128
NH = 2
FF = 2816
CONV = 4
BLOCK = 64
TOK_SEQ = 256
ROWS_DEV = 2
NDOC = 8
ROW_LEN = 2048
ROWS = 8
QKV = 5120
RATES = 24


def draw_lengths(key, part):
    key = jax.random.fold_in(key, 7)
    cut_key, head_key, tail_key, pick_key, long_key, slot_key = jax.random.split(key, 6)
    row_keys = jax.random.split(cut_key, ROWS)

    def cut_row(row_key):
        picked = jax.random.permutation(row_key, ROW_LEN - 1)[:NDOC - 1] + 1
        bounds = jnp.concatenate([jnp.zeros((1,), jnp.int32), jnp.sort(picked).astype(jnp.int32), jnp.full((1,), ROW_LEN, jnp.int32)])
        return bounds[1:] - bounds[:-1]
    spread = jax.vmap(cut_row)(row_keys)
    first = jax.random.randint(head_key, (ROWS, 1), 1, TOK_SEQ // 2 + 1)
    tail_docs = jax.random.randint(tail_key, (ROWS, NDOC - 2), 1, TOK_SEQ // (2 * NDOC) + 1)
    middle = ROW_LEN - first - jnp.sum(tail_docs, axis=1, keepdims=True)
    spanning = jnp.concatenate([first, middle, tail_docs], axis=1)
    chosen = jax.random.randint(pick_key, (ROWS // ROWS_DEV,), 0, ROWS_DEV)
    picked_rows = jnp.arange(ROWS) % ROWS_DEV == jnp.repeat(chosen, ROWS_DEV)
    mixed_rows = jnp.where(picked_rows[:, None], spanning, spread)
    long_row = jax.random.randint(long_key, (), 0, ROWS)
    long_slot = jax.random.randint(slot_key, (), 0, NDOC)
    long_lengths = jnp.where(jnp.arange(NDOC) == long_slot, ROW_LEN - NDOC + 1, 1)
    result = jnp.where((jnp.arange(ROWS) == long_row)[:, None], long_lengths[None, :], mixed_rows)
    return result.astype(jnp.int32)


def block_scale(rng, dims, cuts, smallest, largest):
    factor_of, own = 1.0, jax.random.fold_in(rng, 6)
    for dim, shards_of in cuts:
        draws = jnp.exp(jax.random.uniform(jax.random.fold_in(own, dim), (shards_of,), jnp.float32, smallest / len(cuts), largest / len(cuts)))
        factor_of = factor_of * jnp.repeat(draws, dims[dim] // shards_of).reshape([-1 if axis == dim else 1 for axis in range(len(dims))])
    return factor_of


def centred(key, shape, scale, limit, cuts=(), kind=jnp.bfloat16):
    values = scale * jax.random.normal(key, shape, jnp.float32)
    if cuts:
        values = values * block_scale(key, shape, cuts, -0.22, 0.18)
    return jnp.clip(values, -limit, limit).astype(kind)


def setup_inputs(seed: int = 0) -> dict:
    arg_keys = jax.random.split(jax.random.key(seed), 16)
    hidden_in = centred(arg_keys[0], (ROWS, ROW_LEN, D), 1.0, 6.0, ((0, 4), (1, 8)))
    lengths = draw_lengths(jax.random.fold_in(arg_keys[15], 71), 0)
    norm1_gain = jnp.clip(1.0 + 0.1 * jax.random.normal(arg_keys[2], (D,), jnp.float32), 0.5, 1.5).astype(jnp.bfloat16)
    w_qkv = centred(arg_keys[3], (D, QKV), D ** -0.5, 0.1875)
    conv_w = centred(arg_keys[4], (QKV, CONV), 0.5, 3.0)
    w_rates = centred(arg_keys[5], (D, RATES), D ** -0.5, 0.1875)
    a_log = jnp.clip(jax.random.uniform(arg_keys[6], (HEADS,), jnp.float32, -6.5, -2.5), -6.5, -2.5)
    dt_bias = jnp.clip(jax.random.uniform(arg_keys[7], (HEADS,), jnp.float32, -1.0, 1.0), -1.0, 1.0)
    w_gate = centred(arg_keys[8], (D, D), D ** -0.5, 0.1875)
    out_gain = jnp.clip(1.0 + 0.1 * jax.random.normal(arg_keys[9], (HDIM,), jnp.float32), 0.5, 1.5).astype(jnp.bfloat16)
    w_out = centred(arg_keys[10], (D, D), (D // 2) ** -0.5, 0.25)
    norm2_gain = jnp.clip(1.0 + 0.1 * jax.random.normal(arg_keys[11], (D,), jnp.float32), 0.5, 1.5).astype(jnp.bfloat16)
    w_up = centred(arg_keys[12], (D, 2 * FF), D ** -0.5, 0.1875)
    w_down = centred(arg_keys[13], (FF, D), (FF // 2) ** -0.5, 0.15625)
    cotangent = centred(arg_keys[14], (ROWS, ROW_LEN, D), 1.0, 6.0, ((0, 4), (1, 8)))
    return {"hidden_in": hidden_in, "lengths": lengths, "norm1_gain": norm1_gain, "w_qkv": w_qkv, "conv_w": conv_w, "w_rates": w_rates, "a_log": a_log, "dt_bias": dt_bias, "w_gate": w_gate, "out_gain": out_gain, "w_out": w_out, "norm2_gain": norm2_gain, "w_up": w_up, "w_down": w_down, "cotangent": cotangent}


@jax.custom_vjp
def low(v):
    return lax.optimization_barrier(v.astype(jnp.bfloat16)).astype(jnp.float32)

@jax.custom_vjp
def low_back(v):
    return v

def low_keep(v):
    return (low(v), None)

def low_pass(kept, grad):
    return (grad,)

def back_keep(v):
    return (v, None)

def back_low(kept, grad):
    return (low(grad),)
low.defvjp(low_keep, low_pass)
low_back.defvjp(back_keep, back_low)
EPSILON = 1e-06
HIGHEST = lax.Precision.HIGHEST

def full_product(formula, former, latter):
    return jnp.einsum(formula, former, latter, precision=HIGHEST)

def matmul(former, latter):
    return jnp.dot(former.astype(jnp.float32), latter.astype(jnp.float32), precision=HIGHEST, preferred_element_type=jnp.float32)

def rms_norm(tensor, gain):
    return tensor * lax.rsqrt(lax.optimization_barrier(jnp.mean(tensor * tensor, axis=-1, keepdims=True)) + EPSILON) * gain

def unit_rows(tensor):
    return tensor * lax.rsqrt(lax.optimization_barrier(jnp.sum(tensor * tensor, axis=-1, keepdims=True)) + EPSILON)

def find_docs(lengths_row, positions):
    doc_ends = jnp.cumsum(lengths_row)
    return lax.optimization_barrier(jnp.sum((positions[:, None] >= doc_ends[None, :]).astype(jnp.int32), axis=1)).astype(jnp.int32)

def block_step(state, block_pair):
    query, key_rows, values, beta_rows, log_decay, doc_block, doc_before = block_pair
    span_len = key_rows.shape[0]
    key_heads = jnp.swapaxes(key_rows, 0, 1)
    value_heads = jnp.swapaxes(values, 0, 1)
    query_heads = jnp.swapaxes(query, 0, 1)
    beta_heads = beta_rows.T
    summed_log = jnp.cumsum(log_decay.T, axis=1)
    indices = jnp.arange(span_len)
    same_doc = doc_block[:, None] == doc_block[None, :]
    lower_mask = indices[:, None] >= indices[None, :]
    strict_mask = (indices[:, None] > indices[None, :]).astype(jnp.float32)
    decay = jnp.exp(jnp.where(same_doc & lower_mask, summed_log[:, :, None] - summed_log[:, None, :], -jnp.inf))
    start_decay = jnp.exp(summed_log) * (doc_block == doc_before).astype(jnp.float32)[None, :]
    weighted = beta_heads[:, :, None] * key_heads
    mixing = full_product('htk,hsk->hts', weighted, key_heads) * decay * strict_mask
    right_side = jnp.concatenate([start_decay[:, :, None] * weighted, beta_heads[:, :, None] * value_heads], axis=-1)
    solved = jax.scipy.linalg.solve_triangular(mixing, right_side, lower=True, unit_diagonal=True)
    wide_keys = solved[..., :HDIM]
    fresh_values = solved[..., HDIM:]
    delta_rows = fresh_values - full_product('hsk,hvk->hsv', wide_keys, state)
    scores = full_product('htk,hsk->hts', query_heads, key_heads) * decay[:, NH - 1::NH, :]
    output = start_decay[:, NH - 1::NH, None] * full_product('htk,hvk->htv', query_heads, state)
    output = output + full_product('hts,hsv->htv', scores, delta_rows)
    tail_keys = decay[:, -1, :, None] * key_heads
    new_state = start_decay[:, -1, None, None] * state + full_product('hsv,hsk->hvk', delta_rows, tail_keys)
    return (new_state, jnp.swapaxes(output, 0, 1))

def mix_row(query, key_rows, values, beta_rows, log_decay, doc_virtual):
    length = query.shape[0]
    block_count = length // BLOCK
    span_len = NH * BLOCK
    doc_before = jnp.concatenate([jnp.full((1,), -1, jnp.int32), doc_virtual[span_len - 1::span_len][:block_count - 1]])
    inputs = (query.reshape(block_count, BLOCK, HEADS, HDIM), key_rows.reshape(block_count, span_len, HEADS, HDIM), values.reshape(block_count, span_len, HEADS, HDIM), beta_rows.reshape(block_count, span_len, HEADS), log_decay.reshape(block_count, span_len, HEADS), doc_virtual.reshape(block_count, span_len), doc_before)
    state = jnp.zeros((HEADS, HDIM, HDIM), jnp.float32)
    state, outputs = lax.scan(jax.checkpoint(block_step), state, inputs)
    return outputs.reshape(length, HEADS, HDIM)

def layer(hidden_in, params, doc_tokens):
    norm1_gain, w_qkv, conv_w, w_rates, a_log, dt_bias, w_gate, out_gain, w_out, norm2_gain, w_up, w_down = params
    length = hidden_in.shape[0]
    normed = low(rms_norm(hidden_in, norm1_gain))
    projected = low_back(low(matmul(normed, w_qkv)))
    padded = jnp.pad(projected, ((CONV - 1, 0), (0, 0)))
    doc_padded = jnp.concatenate([jnp.full((CONV - 1,), -1, jnp.int32), doc_tokens])
    summed = jnp.zeros_like(projected)
    for offset in range(CONV):
        keep_taps = (doc_padded[offset:offset + length] == doc_tokens).astype(jnp.float32)
        summed = summed + padded[offset:offset + length] * keep_taps[:, None] * conv_w[:, offset]
    active = jax.nn.silu(summed)
    query = low_back(low(unit_rows(active[:, :D].reshape(length, HEADS, HDIM))))
    key_rows = low_back(low(unit_rows(active[:, D:D + NH * D].reshape(length * NH, HEADS, HDIM))))
    values = low_back(low(active[:, D + NH * D:].reshape(length * NH, HEADS, HDIM)))
    rate_logits = low_back(matmul(normed, w_rates))
    beta_rows = jax.nn.sigmoid(rate_logits[:, :NH * HEADS]).reshape(length * NH, HEADS)
    log_rate = -jnp.exp(a_log) * jax.nn.softplus(rate_logits[:, NH * HEADS:] + dt_bias)
    padding = jnp.zeros((length, NH - 1, HEADS), jnp.float32)
    log_decay = jnp.concatenate([log_rate[:, None, :], padding], axis=1).reshape(length * NH, HEADS)
    doc_virtual = jnp.repeat(doc_tokens, NH)
    mixed = mix_row(query, key_rows, values, beta_rows, log_decay, doc_virtual)
    gate_logits = low_back(matmul(normed, w_gate)).reshape(length, HEADS, HDIM)
    branch = rms_norm(mixed, out_gain) * jax.nn.silu(gate_logits)
    attended = low_back(matmul(low(branch.reshape(length, D)), w_out))
    hidden = hidden_in + attended
    normed2 = low(rms_norm(hidden, norm2_gain))
    gate_up = low_back(matmul(normed2, w_up))
    activated = low(jax.nn.silu(gate_up[:, :FF]) * gate_up[:, FF:])
    return hidden + matmul(activated, w_down)

def reference(hidden_in, lengths, norm1_gain, w_qkv, conv_w, w_rates, a_log, dt_bias, w_gate, out_gain, w_out, norm2_gain, w_up, w_down, cotangent):
    params = tuple((member.astype(jnp.float32) for member in (norm1_gain, w_qkv, conv_w, w_rates, a_log, dt_bias, w_gate, out_gain, w_out, norm2_gain, w_up, w_down)))
    positions = jnp.arange(ROW_LEN, dtype=jnp.int32)

    def one_row(totals, row_data):
        input_row, length_row, tangent_row = row_data
        doc_tokens = find_docs(length_row, positions)

        def row_layer(input_float, weights):
            return layer(input_float, weights, doc_tokens)
        output, pullback = jax.vjp(row_layer, input_row.astype(jnp.float32), params)
        grad_row, grad_params = pullback(tangent_row.astype(jnp.float32))
        totals = jax.tree.map(jnp.add, totals, grad_params)
        return (totals, (output.astype(jnp.bfloat16), grad_row.astype(jnp.bfloat16)))
    zeros = tuple((jnp.zeros(member.shape, jnp.float32) for member in params))
    grads, (outputs, grad_inputs) = lax.scan(one_row, zeros, (hidden_in, lengths, cotangent))
    return (outputs, grad_inputs, grads[0], grads[1], grads[2], grads[3], grads[4], grads[5], grads[6], grads[7], grads[8], grads[9], grads[10], grads[11])
```

```python
from functools import partial

import jax
import jax.numpy as jnp
from jax import lax
from jax.experimental import pallas as pl
from jax.experimental.pallas import tpu as pltpu
from jax.sharding import PartitionSpec as P

D = 1024
HEADS = 8
HDIM = 128
NH = 2
FF = 2816
CHUNK = 128
VIRT = NH * CHUNK
GROUPS = 1 + 2 * NH
EPSILON = 1e-06
F32 = jnp.float32
BF16 = jnp.bfloat16
HIGHEST = lax.Precision.HIGHEST
VMEM_LIMIT = 48 * 1024 * 1024


def mm(former, latter, over=(1, 0)):
    return lax.dot_general(
        former.astype(BF16),
        latter.astype(BF16),
        (((over[0],), (over[1],)), ((), ())),
        preferred_element_type=F32,
    )


def exact_mm(former, latter):
    return jnp.dot(former, latter, precision=HIGHEST, preferred_element_type=F32)


def sigmoid(tensor):
    return 1.0 / (1.0 + jnp.exp(-tensor))


def iota2(shape, dim):
    return lax.broadcasted_iota(jnp.int32, shape, dim)


def params(*semantics):
    return pltpu.CompilerParams(
        dimension_semantics=semantics or None, vmem_limit_bytes=VMEM_LIMIT
    )


def front_kernel(x_ref, gain_ref, w_ref, lanes_ref, flags_ref, normed_ref, col_ref, row_ref):
    x = x_ref[0].astype(F32)
    length = x.shape[0]
    scale = lax.rsqrt(jnp.mean(x * x, axis=-1, keepdims=True) + EPSILON)
    normed = (x * scale * gain_ref[...]).astype(BF16)
    normed_ref[0] = normed
    rates = jnp.dot(normed, w_ref[...], preferred_element_type=F32)
    shifted = rates + lanes_ref[1:2]
    soft = jnp.maximum(shifted, 0.0) + jnp.log(1.0 + jnp.exp(-jnp.abs(shifted)))
    log_decay = lanes_ref[0:1] * soft
    shape = (length, length)
    here, there = iota2(shape, 0), iota2(shape, 1)
    lower = ((here >= there) & (here // CHUNK == there // CHUNK)).astype(F32)
    summed = exact_mm(lower, log_decay)
    last = jnp.concatenate(
        [
            jnp.broadcast_to(summed[at + CHUNK - 1 : at + CHUNK], (CHUNK, HDIM))
            for at in range(0, length, CHUNK)
        ],
        axis=0,
    )
    flags = flags_ref[0]
    start = jnp.exp(summed) * flags[:, 0:1]
    tail = jnp.exp(last - summed) * flags[:, 1:2]
    lane = iota2((length, HDIM), 1)
    packed = jnp.zeros((length, HDIM), F32)
    for limit, member, shift in (
        (56, log_decay, 32),
        (48, sigmoid(shifted), 24),
        (40, tail, 16),
        (32, start, 8),
        (24, summed, 0),
        (16, sigmoid(rates), 0),
    ):
        member = pltpu.roll(member, shift, 1) if shift else member
        packed = jnp.where(lane < limit, member, packed)
    col_ref[0] = packed
    row_ref[0] = packed.T


def front(hidden_in, gain, w_rates, a_log, dt_bias, flags):
    rows, length = hidden_in.shape[:2]
    w_padded = jnp.pad(w_rates, ((0, 0), (0, HDIM - w_rates.shape[1])))
    first = NH * HEADS
    lanes = jnp.pad(
        jnp.stack([-jnp.exp(a_log), dt_bias]), ((0, 0), (first, HDIM - first - HEADS))
    )
    return pl.pallas_call(
        front_kernel,
        grid=(rows,),
        in_specs=[
            pl.BlockSpec((1, length, D), lambda r: (r, 0, 0)),
            pl.BlockSpec((1, D), lambda r: (0, 0)),
            pl.BlockSpec((D, HDIM), lambda r: (0, 0)),
            pl.BlockSpec((2, HDIM), lambda r: (0, 0)),
            pl.BlockSpec((1, length, 2), lambda r: (r, 0, 0)),
        ],
        out_specs=[
            pl.BlockSpec((1, length, D), lambda r: (r, 0, 0)),
            pl.BlockSpec((1, length, HDIM), lambda r: (r, 0, 0)),
            pl.BlockSpec((1, HDIM, length), lambda r: (r, 0, 0)),
        ],
        out_shape=[
            jax.ShapeDtypeStruct((rows, length, D), BF16),
            jax.ShapeDtypeStruct((rows, length, HDIM), F32),
            jax.ShapeDtypeStruct((rows, HDIM, length), F32),
        ],
        compiler_params=params("arbitrary"),
        name="front",
    )(hidden_in, gain.astype(F32)[None], w_padded, lanes, flags)


def convolved(x_ref, halo_ref, taps_ref, keep_ref, ext_ref):
    length = x_ref.shape[1]
    ext_ref[0:8] = halo_ref[0].astype(F32)
    x = x_ref[0].astype(F32)
    ext_ref[8 : 8 + length] = x
    summed = x * taps_ref[3:4]
    for tap in range(3):
        summed = summed + ext_ref[5 + tap : 5 + tap + length] * keep_ref[0, tap] * taps_ref[
            tap : tap + 1
        ]
    return summed


def head_columns(col_ref, head):
    return pltpu.roll(col_ref[0], (HDIM - head) % HDIM, 1)


def both(tensor):
    return jnp.concatenate([tensor, tensor], axis=0)


def decay_matrix(cols, row_ref, mask_ref, head, chunk):
    at = chunk * CHUNK
    own = iota2((HEADS, CHUNK), 0) == head
    across = row_ref[0, 16:24, at : at + CHUNK]
    across = jnp.sum(jnp.where(own, across, 0.0), axis=0, keepdims=True)
    down = cols[at : at + CHUNK, 16:17]
    return jnp.exp(down - across + mask_ref[0, chunk])


def maps_kernel(*refs):
    xs, halos, taps = refs[0:5], refs[5:10], refs[10:15]
    keep_ref, col_ref, row_ref, mask_ref, level_ref = refs[15:20]
    q_ref, k_ref, v_ref, t_ref, wu_ref, p_ref, m_ref, dev_ref, ext_ref = refs[20:]
    head = pl.program_id(1)
    length = xs[0].shape[1]
    chunks = length // CHUNK
    cols = head_columns(col_ref, head)
    parts = []
    for group in range(GROUPS):
        summed = convolved(
            xs[group], halos[group], taps[group], keep_ref, ext_ref.at[group]
        )
        active = summed * sigmoid(summed)
        if group < 1 + NH:
            active = active * lax.rsqrt(
                jnp.sum(active * active, axis=-1, keepdims=True) + EPSILON
            )
        parts.append(active.astype(BF16))
    q_ref[0, 0] = parts[0]
    level = level_ref[...]
    eye = (iota2((HDIM, HDIM), 0) == iota2((HDIM, HDIM), 1)).astype(F32)
    eye_wide = (iota2((VIRT, VIRT), 0) == iota2((VIRT, VIRT), 1)).astype(F32)
    data = []
    for chunk in range(chunks):
        at = chunk * CHUNK
        rows = slice(at, at + CHUNK)
        query = parts[0][rows]
        keys = jnp.concatenate([parts[1][rows], parts[2][rows]], axis=0)
        values = jnp.concatenate([parts[3][rows], parts[4][rows]], axis=0)
        k_ref[0, 0, chunk] = keys
        v_ref[0, 0, chunk] = values
        decay = decay_matrix(cols, row_ref, mask_ref, head, chunk)
        wide_decay = jnp.concatenate([decay, decay], axis=1)
        beta = jnp.concatenate([cols[rows, 0:1], cols[rows, 8:9]], axis=0)
        mixing = (mm(keys, keys, (1, 1)) * both(wide_decay) * beta).astype(BF16).astype(F32)
        p_ref[0, 0, chunk] = (mm(query, keys, (1, 1)) * wide_decay).astype(BF16)
        inverse = (eye_wide - jnp.where(level == 0, mixing, 0.0)).astype(BF16)
        data.append((keys, values, beta, mixing, inverse))
    for step in range(1, 8):
        mids = [
            mm(jnp.where(level == step, mixing, 0.0), inverse)
            for keys, values, beta, mixing, inverse in data
        ]
        data = [
            (keys, values, beta, mixing, inverse - mm(inverse, mid).astype(BF16))
            for (keys, values, beta, mixing, inverse), mid in zip(data, mids)
        ]
    device_m, device_b = None, None
    for chunk, (keys, values, beta, mixing, inverse) in enumerate(data):
        at = chunk * CHUNK
        rows = slice(at, at + CHUNK)
        t_ref[0, 0, chunk] = inverse
        keys_float = keys.astype(F32)
        right = jnp.concatenate(
            [keys_float * (both(cols[rows, 24:25]) * beta), values.astype(F32) * beta], axis=1
        )
        solved = mm(inverse, right).astype(BF16)
        wu_ref[0, 0, chunk] = solved
        tail_keys = keys_float * both(cols[rows, 32:33])
        pair = mm(solved, tail_keys, (0, 0))
        block_m = cols[at + CHUNK - 1 : at + CHUNK, 24:25] * eye - pair[:HDIM]
        block_b = pair[HDIM:]
        m_ref[0, 0, chunk] = block_m.astype(BF16)
        if device_m is None:
            device_m, device_b = block_m, block_b
        else:
            chained = mm(jnp.concatenate([device_m, device_b], axis=0), block_m)
            device_m, device_b = chained[:HDIM], chained[HDIM:] + block_b
    dev_ref[0, 0, 0] = device_m.astype(BF16)
    dev_ref[1, 0, 0] = device_b.astype(BF16)


def group_specs(block, index):
    return [
        pl.BlockSpec(block, partial(lambda g, r, h: index(r, g * HEADS + h), g))
        for g in range(GROUPS)
    ]


def head_spec(*block):
    return pl.BlockSpec(
        (1, 1) + block, lambda r, h: (r, h) + (0,) * len(block)
    )


def conv_specs(length):
    return (
        group_specs((1, length, HDIM), lambda r, c: (r, 0, c))
        + group_specs((1, 8, HDIM), lambda r, c: (r, 0, c))
        + group_specs((4, HDIM), lambda r, c: (0, c))
        + [pl.BlockSpec((1, 3, length, HDIM), lambda r, h: (r, 0, 0, 0))]
    )


def rate_specs(length):
    return [
        pl.BlockSpec((1, length, HDIM), lambda r, h: (r, 0, 0)),
        pl.BlockSpec((1, HDIM, length), lambda r, h: (r, 0, 0)),
        pl.BlockSpec((1, length // CHUNK, CHUNK, CHUNK), lambda r, h: (r, 0, 0, 0)),
    ]


def levels():
    place = jnp.arange(VIRT)
    place = NH * (place % CHUNK) + place // CHUNK
    differ = place[:, None] ^ place[None, :]
    level = sum((differ >= (1 << bit)).astype(jnp.int32) for bit in range(1, 8))
    return jnp.where(place[:, None] > place[None, :], level, -1)


def maps(projected, halo, taps, keep, col, row, mask, level):
    rows, length = projected.shape[:2]
    chunks = length // CHUNK
    shape = lambda *tail: jax.ShapeDtypeStruct((rows, HEADS) + tail, BF16)
    wide = pl.BlockSpec((VIRT, VIRT), lambda r, h: (0, 0))
    return pl.pallas_call(
        maps_kernel,
        grid=(rows, HEADS),
        in_specs=conv_specs(length) + rate_specs(length) + [wide],
        out_specs=[
            head_spec(length, HDIM),
            head_spec(chunks, VIRT, HDIM),
            head_spec(chunks, VIRT, HDIM),
            head_spec(chunks, VIRT, VIRT),
            head_spec(chunks, VIRT, VIRT),
            head_spec(chunks, CHUNK, VIRT),
            head_spec(chunks, HDIM, HDIM),
            pl.BlockSpec((2, 1, 1, HDIM, HDIM), lambda r, h: (0, r, h, 0, 0)),
        ],
        out_shape=[
            shape(length, HDIM),
            shape(chunks, VIRT, HDIM),
            shape(chunks, VIRT, HDIM),
            shape(chunks, VIRT, VIRT),
            shape(chunks, VIRT, VIRT),
            shape(chunks, CHUNK, VIRT),
            shape(chunks, HDIM, HDIM),
            jax.ShapeDtypeStruct((2, rows, HEADS, HDIM, HDIM), BF16),
        ],
        scratch_shapes=[pltpu.VMEM((GROUPS, length + 8, HDIM), F32)],
        compiler_params=params("arbitrary", "arbitrary"),
        name="maps",
    )(*([projected] * 5 + [halo] * 5 + [taps] * 5), keep, col, row, mask, level)


def mixed_kernel(
    q_ref, k_ref, wu_ref, p_ref, col_ref, state_ref, gate_ref, gain_ref,
    branch_ref, mixed_ref, states_ref, delta_ref,
):
    head = pl.program_id(1)
    cols = head_columns(col_ref, head)
    state = state_ref[0, 0].astype(F32)
    chunks = k_ref.shape[2]
    outputs = []
    for chunk in range(chunks):
        at = chunk * CHUNK
        rows = slice(at, at + CHUNK)
        solved = wu_ref[0, 0, chunk]
        states_ref[0, 0, chunk] = state.astype(BF16)
        seen = mm(
            jnp.concatenate([solved[:, :HDIM], q_ref[0, 0, rows]], axis=0), state, (1, 1)
        )
        delta = (solved[:, HDIM:].astype(F32) - seen[:VIRT]).astype(BF16)
        delta_ref[0, 0, chunk] = delta
        outputs.append(cols[rows, 24:25] * seen[VIRT:] + mm(p_ref[0, 0, chunk], delta))
        if chunk + 1 < chunks:
            tail_keys = k_ref[0, 0, chunk].astype(F32) * both(cols[rows, 32:33])
            state = cols[at + CHUNK - 1 : at + CHUNK, 24:25] * state + mm(
                delta, tail_keys, (0, 0)
            )
    mixed = jnp.concatenate(outputs, axis=0)
    mixed_ref[0] = mixed
    scale = lax.rsqrt(jnp.mean(mixed * mixed, axis=-1, keepdims=True) + EPSILON)
    gate = gate_ref[0]
    branch_ref[0] = (mixed * scale * gain_ref[...] * (gate * sigmoid(gate))).astype(BF16)


def column_spec(length):
    return pl.BlockSpec((1, length, HDIM), lambda r, h: (r, 0, h))


def mix(q, k, wu, p, col, state_in, gate, gain):
    rows, _, length = q.shape[:3]
    chunks = length // CHUNK
    return pl.pallas_call(
        mixed_kernel,
        grid=(rows, HEADS),
        in_specs=[
            head_spec(length, HDIM),
            head_spec(chunks, VIRT, HDIM),
            head_spec(chunks, VIRT, VIRT),
            head_spec(chunks, CHUNK, VIRT),
            rate_specs(length)[0],
            head_spec(HDIM, HDIM),
            column_spec(length),
            pl.BlockSpec((1, HDIM), lambda r, h: (0, 0)),
        ],
        out_specs=[
            column_spec(length),
            column_spec(length),
            head_spec(chunks, HDIM, HDIM),
            head_spec(chunks, VIRT, HDIM),
        ],
        out_shape=[
            jax.ShapeDtypeStruct((rows, length, D), BF16),
            jax.ShapeDtypeStruct((rows, length, D), F32),
            jax.ShapeDtypeStruct((rows, HEADS, chunks, HDIM, HDIM), BF16),
            jax.ShapeDtypeStruct((rows, HEADS, chunks, VIRT, HDIM), BF16),
        ],
        compiler_params=params("arbitrary", "arbitrary"),
        name="mix",
    )(q, k, wu, p, col, state_in, gate, gain.astype(F32)[None])


def adjoint_kernel(
    up_ref, mixed_ref, gate_ref, gain_ref, q_ref, wu_ref, p_ref, m_ref, col_ref,
    grad_mixed_ref, grad_gate_ref, grad_gain_ref, own_ref,
):
    head = pl.program_id(1)
    cols = head_columns(col_ref, head)
    chunks = p_ref.shape[2]
    upstream, mixed, gate, gain = up_ref[0], mixed_ref[0], gate_ref[0], gain_ref[...]
    sig = sigmoid(gate)
    scale = lax.rsqrt(jnp.mean(mixed * mixed, axis=-1, keepdims=True) + EPSILON)
    unit = mixed * scale
    grad_gate_ref[0] = (
        upstream * unit * gain * (sig * (1.0 + gate * (1.0 - sig)))
    ).astype(BF16)
    upstream = upstream * (gate * sig)
    partial_gain = upstream * unit
    grad_gain_ref[0, 0] = jnp.sum(
        partial_gain.reshape(partial_gain.shape[0] // 8, 8, HDIM), axis=0
    )
    weighted = gain * upstream
    grad_mixed = scale * (weighted - unit * jnp.mean(unit * weighted, axis=-1, keepdims=True))
    low = grad_mixed.astype(BF16)
    grad_mixed_ref[0] = low
    grad_state = None
    for chunk in reversed(range(chunks)):
        at = chunk * CHUNK
        rows = slice(at, at + CHUNK)
        own_delta = mm(p_ref[0, 0, chunk], low[rows], (0, 0))
        left = jnp.concatenate(
            [(grad_mixed[rows] * cols[rows, 24:25]).astype(BF16), (-own_delta).astype(BF16)],
            axis=0,
        )
        right = jnp.concatenate([q_ref[0, 0, rows], wu_ref[0, 0, chunk, :, :HDIM]], axis=0)
        own = mm(left, right, (0, 0))
        if grad_state is not None:
            own = own + mm(grad_state, m_ref[0, 0, chunk], (1, 1))
        grad_state = own
    own_ref[0, 0] = grad_state.astype(BF16)


def adjoint(upstream, mixed, gate, gain, q, wu, p, m, col):
    rows, _, length = q.shape[:3]
    chunks = length // CHUNK
    return pl.pallas_call(
        adjoint_kernel,
        grid=(rows, HEADS),
        in_specs=[
            column_spec(length),
            column_spec(length),
            column_spec(length),
            pl.BlockSpec((1, HDIM), lambda r, h: (0, 0)),
            head_spec(length, HDIM),
            head_spec(chunks, VIRT, VIRT),
            head_spec(chunks, CHUNK, VIRT),
            head_spec(chunks, HDIM, HDIM),
            rate_specs(length)[0],
        ],
        out_specs=[
            column_spec(length),
            column_spec(length),
            head_spec(8, HDIM),
            head_spec(HDIM, HDIM),
        ],
        out_shape=[
            jax.ShapeDtypeStruct((rows, length, D), BF16),
            jax.ShapeDtypeStruct((rows, length, D), BF16),
            jax.ShapeDtypeStruct((rows, HEADS, 8, HDIM), F32),
            jax.ShapeDtypeStruct((rows, HEADS, HDIM, HDIM), BF16),
        ],
        compiler_params=params("arbitrary", "arbitrary"),
        name="adjoint",
    )(upstream, mixed, gate, gain.astype(F32)[None], q, wu, p, m, col)


def back_kernel(*refs):
    xs, halos, taps = refs[0:5], refs[5:10], refs[10:15]
    keep_ref, col_ref, row_ref, mask_ref, level_ref = refs[15:20]
    q_ref, k_ref, v_ref, t_ref, wu_ref, p_ref, states_ref, delta_ref = refs[20:28]
    grad_mixed_ref, state_ref = refs[28:30]
    gp_ref, gh_ref, gw_ref, stats_ref, ext_ref, shift_ref = refs[30:]
    head = pl.program_id(1)
    length = xs[0].shape[1]
    chunks = length // CHUNK
    cols = head_columns(col_ref, head)
    strict = level_ref[...] >= 0
    lane = iota2((CHUNK, CHUNK), 1)
    last_row = iota2((CHUNK, 1), 0) == CHUNK - 1
    own_row = iota2((HEADS, CHUNK), 0) == head
    grad_next = state_ref[0, 0].astype(F32)
    grads = [[None] * chunks for _ in range(GROUPS)]
    for chunk in reversed(range(chunks)):
        at = chunk * CHUNK
        rows = slice(at, at + CHUNK)
        query = q_ref[0, 0, rows]
        query_float = query.astype(F32)
        keys, values = k_ref[0, 0, chunk], v_ref[0, 0, chunk]
        keys_float, values_float = keys.astype(F32), values.astype(F32)
        solved, scores = wu_ref[0, 0, chunk], p_ref[0, 0, chunk]
        state, delta = states_ref[0, 0, chunk], delta_ref[0, 0, chunk]
        grad_out = grad_mixed_ref[0, rows]
        beta = jnp.concatenate([cols[rows, 0:1], cols[rows, 8:9]], axis=0)
        start, tail = cols[rows, 24:25], cols[rows, 32:33]
        start_wide, tail_wide = both(start), both(tail)
        end = cols[at + CHUNK - 1 : at + CHUNK, 24:25]
        decay = decay_matrix(cols, row_ref, mask_ref, head, chunk)
        wide_decay = jnp.concatenate([decay, decay], axis=1)
        full_decay = jnp.where(strict, both(wide_decay), 0.0)
        next_low = grad_next.astype(BF16)
        tail_keys = (keys_float * tail_wide).astype(BF16)
        grad_delta = mm(scores, grad_out, (0, 0)) + mm(tail_keys, next_low, (1, 1))
        delta_low = grad_delta.astype(BF16)
        grad_scores = mm(grad_out, delta, (1, 1))
        weighted_scores = grad_scores * scores.astype(F32)
        grad_raw = (grad_scores * wide_decay).astype(BF16)
        seen = mm(jnp.concatenate([grad_out, delta_low], axis=0), state)
        grad_query = start * seen[:CHUNK] + mm(grad_raw, keys)
        grad_start = jnp.sum(seen[:CHUNK] * query_float, axis=1, keepdims=True)
        grad_wide = jnp.concatenate([-seen[CHUNK:], grad_delta], axis=1).astype(BF16)
        grad_end = jnp.sum(
            jnp.sum(grad_next * state.astype(F32), axis=1, keepdims=True), axis=0, keepdims=True
        )
        grad_tail_keys = mm(delta, next_low)
        left = jnp.concatenate(
            [(grad_out.astype(F32) * start).astype(BF16), (-grad_delta).astype(BF16)], axis=0
        )
        grad_next = end * grad_next + mm(
            left, jnp.concatenate([query, solved[:, :HDIM]], axis=0), (0, 0)
        )
        grad_right = mm(t_ref[0, 0, chunk], grad_wide, (0, 0))
        right_keys, right_values = grad_right[:, :HDIM], grad_right[:, HDIM:]
        grad_mixing = -mm(grad_right, solved, (1, 1))
        gram = mm(keys, keys, (1, 1))
        decayed = grad_mixing * full_decay
        weighted = decayed * gram
        grad_gram = (decayed * beta).astype(BF16)
        by_keys = jnp.sum(keys_float * right_keys, axis=1, keepdims=True)
        by_values = jnp.sum(values_float * right_values, axis=1, keepdims=True)
        by_mixing = jnp.sum(weighted, axis=1, keepdims=True)
        grad_beta = start_wide * by_keys + by_values + by_mixing
        grad_keys = (
            (start_wide * beta) * right_keys
            + tail_wide * grad_tail_keys
            + mm(grad_raw, query, (0, 0))
            + mm(grad_gram, keys)
            + mm(grad_gram, keys, (0, 0))
        )
        grad_values = beta * right_values
        fold = lambda tensor: tensor[:CHUNK] + tensor[CHUNK:]
        across = jnp.sum(beta * weighted, axis=0, keepdims=True) + jnp.sum(
            weighted_scores, axis=0, keepdims=True
        )
        across = across[:, :CHUNK] + across[:, CHUNK:]
        tail_part = (
            fold(jnp.sum(keys_float * grad_tail_keys, axis=1, keepdims=True)) * tail
        )
        down = (
            fold(beta * by_mixing)
            + jnp.sum(weighted_scores, axis=1, keepdims=True)
            + (grad_start + fold(beta * by_keys)) * start
            - tail_part
        )
        at_end = jnp.sum(tail_part, axis=0, keepdims=True) + grad_end * end
        down = down + jnp.where(last_row, at_end, 0.0)
        columns = jnp.where(
            lane == 0, grad_beta[:CHUNK], jnp.where(lane == 1, grad_beta[CHUNK:], down)
        )
        turned = columns.T
        for place, member in enumerate((turned[0:1], turned[1:2], turned[2:3] - across)):
            spot = slice(place * HEADS, place * HEADS + HEADS)
            stats_ref[0, spot, rows] = jnp.where(own_row, member, stats_ref[0, spot, rows])
        for group, member in enumerate(
            (grad_query, grad_keys[:CHUNK], grad_keys[CHUNK:], grad_values[:CHUNK], grad_values[CHUNK:])
        ):
            grads[group][chunk] = member
    for tap in range(3):
        shift_ref[tap, 0:8] = jnp.zeros((8, HDIM), F32)
        shift_ref[tap, 8 + length : 16 + length] = jnp.zeros((8, HDIM), F32)
    for group in range(GROUPS):
        ext = ext_ref.at[group]
        summed = convolved(xs[group], halos[group], taps[group], keep_ref, ext)
        sig = sigmoid(summed)
        active = summed * sig
        grad = jnp.concatenate(grads[group], axis=0).astype(BF16).astype(F32)
        if group < 1 + NH:
            scale = lax.rsqrt(jnp.sum(active * active, axis=-1, keepdims=True) + EPSILON)
            unit = active * scale
            grad = scale * (grad - unit * jnp.sum(unit * grad, axis=-1, keepdims=True))
        grad = grad * (sig * (1.0 + summed * (1.0 - sig)))
        total = grad * taps[group][3:4]
        before = None
        weight_rows = []
        for tap in range(3):
            kept = grad * keep_ref[0, tap]
            weight_rows.append(
                jnp.sum(kept * ext[5 + tap : 5 + tap + length], axis=0, keepdims=True)
            )
            shift_ref[tap, 8 : 8 + length] = kept * taps[group][tap : tap + 1]
            total = total + shift_ref[tap, 11 - tap : 11 - tap + length]
            early = shift_ref[tap, 3 - tap : 11 - tap]
            before = early if before is None else before + early
        weight_rows.append(
            jnp.sum(grad * ext[8 : 8 + length], axis=0, keepdims=True)
        )
        gp_ref[group, 0] = total.astype(BF16)
        gh_ref[group, 0] = before.astype(BF16)
        gw_ref[0, group, 0] = jnp.concatenate(
            weight_rows + [jnp.zeros((4, HDIM), F32)], axis=0
        )


def back(projected, halo, taps, keep, col, row, mask, level, saved, grad_mixed, adjoint_in):
    rows, length = projected.shape[:2]
    chunks = length // CHUNK
    wide = pl.BlockSpec((VIRT, VIRT), lambda r, h: (0, 0))
    return pl.pallas_call(
        back_kernel,
        grid=(rows, HEADS),
        in_specs=conv_specs(length)
        + rate_specs(length)
        + [wide]
        + [
            head_spec(length, HDIM),
            head_spec(chunks, VIRT, HDIM),
            head_spec(chunks, VIRT, HDIM),
            head_spec(chunks, VIRT, VIRT),
            head_spec(chunks, VIRT, VIRT),
            head_spec(chunks, CHUNK, VIRT),
            head_spec(chunks, HDIM, HDIM),
            head_spec(chunks, VIRT, HDIM),
            column_spec(length),
            head_spec(HDIM, HDIM),
        ],
        out_specs=[
            pl.BlockSpec((GROUPS, 1, length, HDIM), lambda r, h: (0, r, 0, h)),
            pl.BlockSpec((GROUPS, 1, 8, HDIM), lambda r, h: (0, r, 0, h)),
            pl.BlockSpec((1, GROUPS, 1, 8, HDIM), lambda r, h: (r, 0, h, 0, 0)),
            pl.BlockSpec((1, 24, length), lambda r, h: (r, 0, 0)),
        ],
        out_shape=[
            jax.ShapeDtypeStruct((GROUPS, rows, length, D), BF16),
            jax.ShapeDtypeStruct((GROUPS, rows, 8, D), BF16),
            jax.ShapeDtypeStruct((rows, GROUPS, HEADS, 8, HDIM), F32),
            jax.ShapeDtypeStruct((rows, 24, length), F32),
        ],
        scratch_shapes=[
            pltpu.VMEM((GROUPS, length + 8, HDIM), F32),
            pltpu.VMEM((3, length + 16, HDIM), F32),
        ],
        compiler_params=params("arbitrary", "arbitrary"),
        name="back",
    )(
        *([projected] * 5 + [halo] * 5 + [taps] * 5),
        keep, col, row, mask, level, *saved, grad_mixed, adjoint_in,
    )


def rates_kernel(stats_ref, row_ref, nega_ref, rates_ref, sums_ref):
    rows, _, length = stats_ref.shape
    shape = (length, length)
    here, there = iota2(shape, 0), iota2(shape, 1)
    lower = ((here >= there) & (here // CHUNK == there // CHUNK)).astype(F32)
    lane = iota2((HEADS, HDIM), 1)
    total = jnp.zeros((HEADS, HDIM), F32)
    for r in range(rows):
        beta = row_ref[r, 0:16]
        grad_log = exact_mm(stats_ref[r, 16:24], lower)
        grad_bias = grad_log * nega_ref[:, 0:1] * row_ref[r, 40:48]
        rates_ref[r, 0:16] = (stats_ref[r, 0:16] * beta * (1.0 - beta)).astype(BF16)
        rates_ref[r, 16:24] = grad_bias.astype(BF16)
        rates_ref[r, 24:32] = jnp.zeros((8, length), BF16)
        by_log = jnp.sum(grad_log * row_ref[r, 48:56], axis=1, keepdims=True)
        by_bias = jnp.sum(grad_bias, axis=1, keepdims=True)
        total = total + jnp.where(lane == 0, by_log, jnp.where(lane == 1, by_bias, 0.0))
    sums_ref[...] = total


def rates_back(stats, row, a_log):
    rows, _, length = stats.shape
    nega = jnp.broadcast_to(-jnp.exp(a_log)[:, None], (HEADS, HDIM))
    return pl.pallas_call(
        rates_kernel,
        out_shape=[
            jax.ShapeDtypeStruct((rows, 32, length), BF16),
            jax.ShapeDtypeStruct((HEADS, HDIM), F32),
        ],
        compiler_params=params(),
        name="rates_back",
    )(stats, row, nega)


def to_core(value):
    count = lax.axis_size("seq")
    return lax.ppermute(value, "seq", [(at, at ^ 1) for at in range(count)])


def to_chip(value, step):
    count = lax.axis_size("seq")
    pairs = [(at, at + 2 * step) for at in range(count) if 0 <= at + 2 * step < count]
    return lax.ppermute(value, "seq", pairs)


def along(value, step):
    count = lax.axis_size("seq")
    pairs = [(at, at + step) for at in range(count) if 0 <= at + step < count]
    return lax.ppermute(value, "seq", pairs)


def chain(former, latter, transposed):
    formula = "rhva,rhba->rhvb" if transposed else "rhva,rhab->rhvb"
    return jnp.einsum(formula, former.astype(BF16), latter.astype(BF16), preferred_element_type=F32)


def carried(device_m, device_b, step):
    transposed = step < 0
    core = lax.axis_index("seq") % 2
    half = device_b.shape[0] // 2
    mine = lambda tensor, which: lax.dynamic_slice_in_dim(tensor, which * half, half, 0)
    own_m, own_b = mine(device_m, core), mine(device_b, core)
    other_m, other_b = to_core((mine(device_m, 1 - core), mine(device_b, 1 - core)))
    own_first = core == (0 if step > 0 else 1)
    first_m = jnp.where(own_first, own_m, other_m)
    first_b = jnp.where(own_first, own_b, other_b)
    second_m = jnp.where(own_first, other_m, own_m)
    second_b = jnp.where(own_first, other_b, own_b)
    if transposed:
        chip_m = chain(second_m, first_m, False).astype(BF16)
    else:
        chip_m = chain(first_m, second_m, False).astype(BF16)
    chip_b = chain(first_b, second_m, transposed) + second_b.astype(F32)
    leaving = chip_b.astype(BF16)
    entering = jnp.zeros_like(leaving)
    steps = lax.axis_size("seq") // 2 - 1
    for at in range(steps):
        entering = to_chip(leaving, step)
        if at + 1 < steps:
            leaving = (chain(entering, chip_m, transposed) + chip_b).astype(BF16)
    between = (chain(entering, first_m, transposed) + first_b.astype(F32)).astype(BF16)
    keep = jnp.where(own_first, entering, between)
    give = jnp.where(own_first, between, entering)
    got = to_core(give)
    low = jnp.where(core == 0, keep, got)
    high = jnp.where(core == 0, got, keep)
    return jnp.concatenate([low, high], axis=0)


def half_product(formula, former, latter):
    return jnp.einsum(formula, former, latter, preferred_element_type=F32)


def shortened(value):
    return jax.tree.map(lambda part: part.astype(BF16), value)


def rms_norm(tensor, gain):
    return tensor * lax.rsqrt(jnp.mean(tensor * tensor, axis=-1, keepdims=True) + EPSILON) * gain


def swiglu(gate_up):
    return jax.nn.silu(gate_up[..., :FF]) * gate_up[..., FF:]


def find_docs(doc_ends, places):
    found = jnp.sum((places[None, :, None] >= doc_ends[:, None, :]).astype(jnp.int32), axis=2)
    return jnp.where(places[None, :] >= 0, found, -1)


def doc_masks(lengths, length):
    anchor = lax.axis_index("seq") * length
    doc_ends = jnp.cumsum(lengths, axis=1)
    extended = find_docs(doc_ends, anchor + jnp.arange(-3, length, dtype=jnp.int32))
    docs = extended[:, 3:]
    rows = docs.shape[0]
    keep = jnp.stack([extended[:, tap : tap + length] == docs for tap in range(3)], axis=1)
    keep = jnp.broadcast_to(keep.astype(F32)[..., None], keep.shape + (HDIM,))
    chunks = length // CHUNK
    blocks = docs.reshape(rows, chunks, CHUNK)
    before = find_docs(doc_ends, anchor + jnp.arange(0, length, CHUNK, dtype=jnp.int32) - 1)
    carry = blocks == before[..., None]
    same_last = blocks == blocks[..., -1:]
    flags = jnp.stack([carry, same_last], axis=-1).astype(F32).reshape(rows, length, 2)
    places = jnp.arange(CHUNK)
    allowed = (blocks[..., :, None] == blocks[..., None, :]) & (places[:, None] >= places)
    return keep, flags, jnp.where(allowed, 0.0, -1e30).astype(F32)


def local(
    hidden_in, lengths, norm1_gain, w_qkv, conv_w, w_rates, a_log, dt_bias,
    w_gate, out_gain, w_out, norm2_gain, w_up, w_down, cotangent,
):
    row_count, length = hidden_in.shape[:2]
    keep, flags, mask = doc_masks(lengths, length)
    level = levels()
    taps = conv_w.astype(F32).T
    input_float = hidden_in.astype(F32)
    normed, col, row = front(hidden_in, norm1_gain, w_rates, a_log, dt_bias, flags)
    projected = half_product("rld,de->rle", normed, w_qkv).astype(BF16)
    halo = along(projected[:, length - 8 :], 1)
    q, k, v, t, wu, p, m, device = maps(projected, halo, taps, keep, col, row, mask, level)
    gate = half_product("rld,de->rle", normed, w_gate)
    state_in = carried(device[0], device[1], 1)
    branch, mixed, states, delta = mix(q, k, wu, p, col, state_in, gate, out_gain)
    hidden = input_float + half_product("rld,de->rle", branch, w_out)
    normed2_float, norm2_back = jax.vjp(rms_norm, hidden, norm2_gain.astype(F32))
    normed2 = normed2_float.astype(BF16)
    gate_up = half_product("rld,de->rle", normed2, w_up)
    activated_float, swiglu_back = jax.vjp(swiglu, gate_up)
    activated = activated_float.astype(BF16)
    layer_out = (hidden + half_product("rlf,fd->rld", activated, w_down)).astype(BF16)
    grad_w_down = half_product("rlf,rld->fd", activated, cotangent)
    grad_act = half_product("rld,fd->rlf", cotangent, w_down)
    grad_gate_up = swiglu_back(grad_act)[0].astype(BF16)
    grad_w_up = half_product("rld,rle->de", normed2, grad_gate_up)
    grad_normed2 = half_product("rle,de->rld", grad_gate_up, w_up)
    grad_hidden_part, grad_norm2_gain = norm2_back(grad_normed2)
    grad_hidden = cotangent.astype(F32) + grad_hidden_part
    grad_attended = grad_hidden.astype(BF16)
    grad_w_out = half_product("rld,rle->de", branch, grad_attended)
    grad_branch = half_product("rle,de->rld", grad_attended, w_out)
    grad_mixed, grad_gate, gain_parts, own = adjoint(
        grad_branch, mixed, gate, out_gain, q, wu, p, m, col
    )
    grad_out_gain = jnp.sum(gain_parts, axis=(0, 1, 2))
    adjoint_in = carried(device[0], own, -1)
    gp, gh, gw, stats = back(
        projected, halo, taps, keep, col, row, mask, level,
        (q, k, v, t, wu, p, states, delta), grad_mixed, adjoint_in,
    )
    returned = along(gh, -1)
    grad_projected = jnp.moveaxis(gp, 0, 2).reshape(row_count, length, GROUPS * D)
    returned = jnp.moveaxis(returned, 0, 2).reshape(row_count, 8, GROUPS * D)
    tail = (grad_projected[:, length - 8 :].astype(F32) + returned.astype(F32)).astype(BF16)
    grad_projected = lax.dynamic_update_slice_in_dim(grad_projected, tail, length - 8, 1)
    grad_conv_w = jnp.moveaxis(jnp.sum(gw, axis=0)[:, :, :4], 2, 3).reshape(GROUPS * D, 4)
    grad_rates, rate_sums = rates_back(stats, row, a_log)
    grad_rates = grad_rates[:, :24]
    grad_w_qkv = half_product("rld,rle->de", normed, grad_projected)
    grad_w_rates = half_product("rld,rel->de", normed, grad_rates)
    grad_w_gate = half_product("rld,rle->de", normed, grad_gate)
    grad_normed = half_product("rle,de->rld", grad_projected, w_qkv)
    grad_normed = grad_normed + half_product("rel,de->rld", grad_rates, w_rates)
    grad_normed = grad_normed + half_product("rle,de->rld", grad_gate, w_gate)
    _, norm1_back = jax.vjp(rms_norm, input_float, norm1_gain.astype(F32))
    grad_input_part, grad_norm1_gain = norm1_back(grad_normed)
    grad_x = (grad_hidden + grad_input_part).astype(BF16)
    mlp_terms = (grad_norm2_gain, grad_w_up, grad_w_down)
    mixer_terms = (grad_norm1_gain, grad_w_qkv, grad_conv_w, grad_w_rates, grad_w_gate, grad_w_out)
    small_sums = lax.psum((rate_sums[:, 0], rate_sums[:, 1], grad_out_gain), ("row", "seq"))
    shards = jax.tree.map(
        lambda part: part.astype(F32),
        lax.psum_scatter(
            shortened(mlp_terms + mixer_terms), "seq", scatter_dimension=0, tiled=True
        ),
    )
    totals = jax.tree.map(lambda part: part.astype(F32), lax.psum(shortened(shards), "row"))
    return (
        layer_out,
        grad_x,
        totals[3],
        totals[4],
        totals[5],
        totals[6],
        small_sums[0],
        small_sums[1],
        totals[7],
        small_sums[2],
        totals[8],
        totals[0],
        totals[1],
        totals[2],
    )


def solution(mesh):
    return jax.shard_map(
        local,
        mesh=mesh,
        in_specs=(
            P("row", "seq", None),
            P("row", None),
            P(),
            P(),
            P(),
            P(),
            P(),
            P(),
            P(),
            P(),
            P(),
            P(),
            P(),
            P(),
            P("row", "seq", None),
        ),
        out_specs=(
            P("row", "seq", None),
            P("row", "seq", None),
            P("seq"),
            P("seq", None),
            P("seq", None),
            P("seq", None),
            P(),
            P(),
            P("seq", None),
            P(),
            P("seq", None),
            P("seq"),
            P("seq", None),
            P("seq", None),
        ),
        check_vma=False,
    )
```

```python
from functools import partial

import jax
import jax.numpy as jnp
from jax import lax
from jax.experimental import pallas as pl
from jax.experimental.pallas import tpu as pltpu
from jax.sharding import PartitionSpec as P

D = 1024
HEADS = 8
HDIM = 128
NH = 2
FF = 2816
CHUNK = 128
VIRT = NH * CHUNK
GROUPS = 1 + 2 * NH
PAIR = 2
EPSILON = 1e-06
F32 = jnp.float32
BF16 = jnp.bfloat16
HIGHEST = lax.Precision.HIGHEST
VMEM_LIMIT = 60 * 1024 * 1024
VMEM_SMALL = 60 * 1024 * 1024
FLOPS_A_US = 1000000000
LONG = 200.0


def mm(former, latter, over=(1, 0)):
    return lax.dot_general(
        former.astype(BF16),
        latter.astype(BF16),
        (((over[0],), (over[1],)), ((), ())),
        preferred_element_type=F32,
    )


def exact_mm(former, latter):
    return jnp.dot(former, latter, precision=HIGHEST, preferred_element_type=F32)


def sigmoid(tensor):
    return 1.0 / (1.0 + jnp.exp(-tensor))


def iota2(shape, dim):
    return lax.broadcasted_iota(jnp.int32, shape, dim)


def params(*semantics, limit=VMEM_LIMIT):
    return pltpu.CompilerParams(dimension_semantics=semantics or None, vmem_limit_bytes=limit)


def pinned(kernel, inputs, pins):
    return lambda *refs: kernel(*refs[:inputs], *refs[inputs + len(pins) :])


def pin_specs(pins):
    return [pl.BlockSpec(memory_space=pl.ANY)] * len(pins)


def core_index():
    return (lax.axis_index("seq") % 2).astype(jnp.int32).reshape(1)


class Order:
    def __init__(self):
        self.last = ()

    def then(self, outputs):
        self.last = (jax.tree.leaves(outputs)[0],)
        return outputs


def call_with_core(
    kernel, grid, in_specs, out_specs, out_shape, args, scratch=(), order=None, name=None, scalar=None,
    limit=VMEM_LIMIT, cost=1.0,
):
    pins = order.last if order else ()
    outputs = pl.pallas_call(
        pinned(kernel, 1 + len(args), pins),
        grid_spec=pltpu.PrefetchScalarGridSpec(
            num_scalar_prefetch=1,
            grid=grid,
            in_specs=list(in_specs) + pin_specs(pins),
            out_specs=out_specs,
            scratch_shapes=list(scratch),
        ),
        out_shape=out_shape,
        compiler_params=params(*["arbitrary"] * len(grid), limit=limit),
        cost_estimate=pl.CostEstimate(
            flops=int(cost * FLOPS_A_US), bytes_accessed=1, transcendentals=0
        ),
        name=name,
    )(core_index() if scalar is None else scalar, *args, *pins)
    return order.then(outputs) if order else outputs


def front_kernel(x_ref, gain_ref, w_ref, lanes_ref, flags_ref, normed_ref, col_ref, row_ref):
    x = x_ref[0].astype(F32)
    length = x.shape[0]
    scale = lax.rsqrt(jnp.mean(x * x, axis=-1, keepdims=True) + EPSILON)
    normed = (x * scale * gain_ref[...]).astype(BF16)
    normed_ref[0] = normed
    rates = jnp.dot(normed, w_ref[...], preferred_element_type=F32)
    shifted = rates + lanes_ref[1:2]
    soft = jnp.maximum(shifted, 0.0) + jnp.log(1.0 + jnp.exp(-jnp.abs(shifted)))
    log_decay = lanes_ref[0:1] * soft
    shape = (length, length)
    here, there = iota2(shape, 0), iota2(shape, 1)
    lower = ((here >= there) & (here // CHUNK == there // CHUNK)).astype(F32)
    summed = exact_mm(lower, log_decay)
    last = jnp.concatenate(
        [
            jnp.broadcast_to(summed[at + CHUNK - 1 : at + CHUNK], (CHUNK, HDIM))
            for at in range(0, length, CHUNK)
        ],
        axis=0,
    )
    flags = flags_ref[0]
    start = jnp.exp(summed) * flags[:, 0:1]
    tail = jnp.exp(last - summed) * flags[:, 1:2]
    lane = iota2((length, HDIM), 1)
    packed = jnp.zeros((length, HDIM), F32)
    for limit, member, shift in (
        (56, log_decay, 32),
        (48, sigmoid(shifted), 24),
        (40, tail, 16),
        (32, start, 8),
        (24, summed, 0),
        (16, sigmoid(rates), 0),
    ):
        member = pltpu.roll(member, shift, 1) if shift else member
        packed = jnp.where(lane < limit, member, packed)
    col_ref[0] = packed
    row_ref[0] = packed.T


def front(hidden_in, gain, w_rates, a_log, dt_bias, flags):
    rows, length = hidden_in.shape[:2]
    w_padded = jnp.pad(w_rates, ((0, 0), (0, HDIM - w_rates.shape[1])))
    first = NH * HEADS
    lanes = jnp.pad(
        jnp.stack([-jnp.exp(a_log), dt_bias]), ((0, 0), (first, HDIM - first - HEADS))
    )
    return pl.pallas_call(
        front_kernel,
        grid=(rows,),
        in_specs=[
            pl.BlockSpec((1, length, D), lambda r: (r, 0, 0)),
            pl.BlockSpec((1, D), lambda r: (0, 0)),
            pl.BlockSpec((D, HDIM), lambda r: (0, 0)),
            pl.BlockSpec((2, HDIM), lambda r: (0, 0)),
            pl.BlockSpec((1, length, 2), lambda r: (r, 0, 0)),
        ],
        out_specs=[
            pl.BlockSpec((1, length, D), lambda r: (r, 0, 0)),
            pl.BlockSpec((1, length, HDIM), lambda r: (r, 0, 0)),
            pl.BlockSpec((1, HDIM, length), lambda r: (r, 0, 0)),
        ],
        out_shape=[
            jax.ShapeDtypeStruct((rows, length, D), BF16),
            jax.ShapeDtypeStruct((rows, length, HDIM), F32),
            jax.ShapeDtypeStruct((rows, HDIM, length), F32),
        ],
        compiler_params=params("arbitrary"),
        name="front",
    )(hidden_in, gain.astype(F32)[None], w_padded, lanes, flags)


def convolved(x_ref, halo_ref, taps_ref, keep_ref, ext_ref, lanes):
    length = x_ref.shape[1]
    ext_ref[0:8] = halo_ref[0, :, lanes].astype(F32)
    x = x_ref[0, :, lanes].astype(F32)
    ext_ref[8 : 8 + length] = x
    summed = x * taps_ref[3:4, lanes]
    for tap in range(3):
        summed = summed + ext_ref[5 + tap : 5 + tap + length] * keep_ref[0, tap] * taps_ref[
            tap : tap + 1, lanes
        ]
    return summed


def head_columns(col_ref, head):
    return pltpu.roll(col_ref[0], (HDIM - head) % HDIM, 1)


def lane_sums(tensor):
    return mm(tensor, jnp.ones((HDIM, HDIM), BF16))


def split(tensor):
    high = tensor.astype(BF16)
    return jnp.concatenate([high, (tensor - high.astype(F32)).astype(BF16)], axis=1)


def row_sums(tensor):
    return mm(jnp.ones((8, 2 * HDIM), BF16), split(tensor), (1, 1))[0:1]


def column_sums(tensor):
    total = mm(jnp.ones((8, tensor.shape[0]), BF16), split(tensor))
    return total[0:1, :HDIM] + total[0:1, HDIM:]


def wide(column):
    return jnp.broadcast_to(column, (column.shape[0], HDIM))


def pick(row_ref, place, head, at):
    own = iota2((HEADS, CHUNK), 0) == head
    rows = row_ref[0, place * HEADS : place * HEADS + HEADS, at : at + CHUNK]
    return jnp.sum(jnp.where(own, rows, 0.0), axis=0, keepdims=True)


def lanes_of(sub):
    return slice(sub * HDIM, sub * HDIM + HDIM)


def in_turns(makers):
    running = list(makers)
    while running:
        running = [member for member in running if next(member, "end") != "end"]


def both(tensor):
    return jnp.concatenate([tensor, tensor], axis=0)


def decay_matrix(cols, row_ref, mask_ref, head, chunk):
    at = chunk * CHUNK
    across = pick(row_ref, 2, head, at)
    down = cols[at : at + CHUNK, 16:17]
    return jnp.exp(down - across + mask_ref[0, chunk])


def maps_kernel(core_ref, *refs):
    xs, halos, taps = refs[0:5], refs[5:10], refs[10:15]
    keep_ref, col_ref, row_ref, mask_ref, level_ref = refs[15:20]
    q_ref, k_ref, v_ref, t_ref, wu_ref, p_ref, m_ref, dev_ref, ext_ref = refs[20:]
    length = xs[0].shape[1]
    chunks = length // CHUNK
    eye = (iota2((HDIM, HDIM), 0) == iota2((HDIM, HDIM), 1)).astype(F32)
    eye_wide = (iota2((VIRT, VIRT), 0) == iota2((VIRT, VIRT), 1)).astype(BF16)
    heads = q_ref.shape[1]
    data = []
    for sub in range(heads):
        head = heads * pl.program_id(1) + sub
        cols = head_columns(col_ref, head)
        parts = []
        for group in range(GROUPS):
            summed = convolved(
                xs[group], halos[group], taps[group], keep_ref, ext_ref.at[group], lanes_of(sub)
            )
            active = summed * sigmoid(summed)
            if group < 1 + NH:
                active = active * lax.rsqrt(lane_sums(active * active) + EPSILON)
            parts.append(active.astype(BF16))
        q_ref[0, sub] = parts[0]
        for chunk in range(chunks):
            at = chunk * CHUNK
            rows = slice(at, at + CHUNK)
            query = parts[0][rows]
            keys = jnp.concatenate([parts[1][rows], parts[2][rows]], axis=0)
            values = jnp.concatenate([parts[3][rows], parts[4][rows]], axis=0)
            k_ref[0, sub, chunk] = keys
            v_ref[0, sub, chunk] = values
            decay = decay_matrix(cols, row_ref, mask_ref, head, chunk)
            wide_decay = jnp.concatenate([decay, decay], axis=1)
            beta = jnp.concatenate([wide(cols[rows, 0:1]), wide(cols[rows, 8:9])], axis=0)
            beta_wide = jnp.concatenate([beta, beta], axis=1)
            mixing = (mm(keys, keys, (1, 1)) * both(wide_decay) * beta_wide).astype(BF16)
            p_ref[0, sub, chunk] = (mm(query, keys, (1, 1)) * wide_decay).astype(BF16)
            inverse = eye_wide - mixing * level_ref[0]
            data.append((keys, values, beta, mixing, inverse, cols[rows]))
    for step in range(1, 8):
        mids = [mm(member[3] * level_ref[step], member[4]) for member in data]
        data = [
            member[:4] + (member[4] - mm(member[4], mid).astype(BF16),) + member[5:]
            for member, mid in zip(data, mids)
        ]
    device = [None] * heads
    for chunk in range(chunks):
        for sub in range(heads):
            keys, values, beta, mixing, inverse, cols = data[sub * chunks + chunk]
            t_ref[0, sub, chunk] = inverse
            keys_float = keys.astype(F32)
            right = jnp.concatenate(
                [keys_float * (both(wide(cols[:, 24:25])) * beta), values.astype(F32) * beta], axis=1
            )
            solved = mm(inverse, right).astype(BF16)
            wu_ref[0, sub, chunk] = solved
            tail_keys = keys_float * both(wide(cols[:, 32:33]))
            pair = mm(solved, tail_keys, (0, 0))
            block_m = cols[CHUNK - 1 : CHUNK, 24:25] * eye - pair[:HDIM]
            block_b = pair[HDIM:]
            m_ref[0, sub, chunk] = block_m.astype(BF16)
            if chunk == 0:
                device[sub] = (block_m, block_b)
            else:
                chained = mm(jnp.concatenate(device[sub], axis=0), block_m)
                device[sub] = (chained[:HDIM], chained[HDIM:] + block_b)
    for sub in range(heads):
        dev_ref[0, 0, 0, sub] = device[sub][0].astype(BF16)
        dev_ref[0, 1, 0, sub] = device[sub][1].astype(BF16)


def group_specs(block, index, first):
    return [
        pl.BlockSpec(
            block + (PAIR * HDIM,),
            partial(lambda g, r, h, *_: index(r, (g * HEADS + first) // PAIR + h), g),
        )
        for g in range(GROUPS)
    ]


def head_spec(*block, first=0):
    return pl.BlockSpec(
        (1, PAIR) + block, lambda r, h, *_: (r, first // PAIR + h) + (0,) * len(block)
    )


def conv_specs(length, first=0):
    return (
        group_specs((1, length), lambda r, c: (r, 0, c), first)
        + group_specs((1, 8), lambda r, c: (r, 0, c), first)
        + group_specs((4,), lambda r, c: (0, c), first)
        + [pl.BlockSpec((1, 3, length, HDIM), lambda r, h, *_: (r, 0, 0, 0))]
    )


def rate_specs(length):
    return [
        pl.BlockSpec((1, length, HDIM), lambda r, h, *_: (r, 0, 0)),
        pl.BlockSpec((1, HDIM, length), lambda r, h, *_: (r, 0, 0)),
        pl.BlockSpec((1, length // CHUNK, CHUNK, CHUNK), lambda r, h, *_: (r, 0, 0, 0)),
    ]


def levels():
    place = jnp.arange(VIRT)
    place = NH * (place % CHUNK) + place // CHUNK
    differ = place[:, None] ^ place[None, :]
    level = sum((differ >= (1 << bit)).astype(jnp.int32) for bit in range(1, 8))
    level = jnp.where(place[:, None] > place[None, :], level, -1)
    return (level[None] == jnp.arange(8)[:, None, None]).astype(BF16)


def slot_spec(rows, *lead):
    half = rows // 2
    return pl.BlockSpec(
        (1,) + lead + (1, PAIR, HDIM, HDIM),
        lambda r, h, core: ((r // half) ^ core[0],) + (0,) * len(lead) + (r % half, h, 0, 0),
    )


def maps(projected, halo, taps, keep, col, row, mask, level, order):
    rows, length = projected.shape[:2]
    chunks = length // CHUNK
    shape = lambda *tail: jax.ShapeDtypeStruct((rows, HEADS) + tail, BF16)
    masks = pl.BlockSpec((8, VIRT, VIRT), lambda r, h, *_: (0, 0, 0))
    return call_with_core(
        maps_kernel,
        (rows, HEADS // PAIR),
        conv_specs(length) + rate_specs(length) + [masks],
        [
            head_spec(length, HDIM),
            head_spec(chunks, VIRT, HDIM),
            head_spec(chunks, VIRT, HDIM),
            head_spec(chunks, VIRT, VIRT),
            head_spec(chunks, VIRT, VIRT),
            head_spec(chunks, CHUNK, VIRT),
            head_spec(chunks, HDIM, HDIM),
            slot_spec(rows, 2),
        ],
        [
            shape(length, HDIM),
            shape(chunks, VIRT, HDIM),
            shape(chunks, VIRT, HDIM),
            shape(chunks, VIRT, VIRT),
            shape(chunks, VIRT, VIRT),
            shape(chunks, CHUNK, VIRT),
            shape(chunks, HDIM, HDIM),
            jax.ShapeDtypeStruct((2, 2, rows // 2, HEADS, HDIM, HDIM), BF16),
        ],
        [projected] * 5 + [halo] * 5 + [taps] * 5 + [keep, col, row, mask, level],
        [pltpu.VMEM((GROUPS, length + 8, HDIM), F32)],
        order,
        name="maps",
        cost=40.0,
    )


def entering_spec(rows, first=0):
    half = rows // 2
    return pl.BlockSpec(
        (1, PAIR, HDIM, HDIM), lambda r, h, *_: (r % half, first // PAIR + h, 0, 0)
    )


def entering_state(core_ref, own_ref, other_ref, sub, rows):
    mine = pl.program_id(0) // (rows // 2) == core_ref[0]
    return jnp.where(mine, own_ref[0, sub].astype(F32), other_ref[0, sub].astype(F32))


def mixed_kernel(
    row_count, core_ref, q_ref, k_ref, wu_ref, p_ref, col_ref, own_ref, other_ref, gate_ref, gain_ref,
    branch_ref, mixed_ref, states_ref, delta_ref,
):
    heads, chunks = k_ref.shape[1:3]

    def one(sub):
        cols = head_columns(col_ref, heads * pl.program_id(1) + sub)
        state = entering_state(core_ref, own_ref, other_ref, sub, row_count)
        outputs = []
        for chunk in range(chunks):
            at = chunk * CHUNK
            rows = slice(at, at + CHUNK)
            solved = wu_ref[0, sub, chunk]
            states_ref[0, sub, chunk] = state.astype(BF16)
            seen = mm(
                jnp.concatenate([solved[:, :HDIM], q_ref[0, sub, rows]], axis=0), state, (1, 1)
            )
            yield
            delta = (solved[:, HDIM:].astype(F32) - seen[:VIRT]).astype(BF16)
            delta_ref[0, sub, chunk] = delta
            if chunk + 1 < chunks:
                tail_keys = k_ref[0, sub, chunk].astype(F32) * both(cols[rows, 32:33])
                state = cols[at + CHUNK - 1 : at + CHUNK, 24:25] * state + mm(
                    delta, tail_keys, (0, 0)
                )
            outputs.append(cols[rows, 24:25] * seen[VIRT:] + mm(p_ref[0, sub, chunk], delta))
            yield
        mixed = jnp.concatenate(outputs, axis=0)
        mixed_ref[0, :, lanes_of(sub)] = mixed
        scale = lax.rsqrt(lane_sums(mixed * mixed) * (1.0 / HDIM) + EPSILON)
        gate = gate_ref[0, :, lanes_of(sub)]
        branch_ref[0, :, lanes_of(sub)] = (
            mixed * scale * gain_ref[...] * (gate * sigmoid(gate))
        ).astype(BF16)

    in_turns([one(sub) for sub in range(heads)])


def column_spec(length, first=0):
    return pl.BlockSpec((1, length, PAIR * HDIM), lambda r, h, *_: (r, 0, first // PAIR + h))


def mix(q, k, wu, p, col, states_in, gate, gain, order):
    rows, _, length = q.shape[:3]
    chunks = length // CHUNK
    return call_with_core(
        partial(mixed_kernel, rows),
        (rows, HEADS // PAIR),
        [
            head_spec(length, HDIM),
            head_spec(chunks, VIRT, HDIM),
            head_spec(chunks, VIRT, VIRT),
            head_spec(chunks, CHUNK, VIRT),
            rate_specs(length)[0],
            entering_spec(rows),
            entering_spec(rows),
            column_spec(length),
            pl.BlockSpec((1, HDIM), lambda r, h, *_: (0, 0)),
        ],
        [
            column_spec(length),
            column_spec(length),
            head_spec(chunks, HDIM, HDIM),
            head_spec(chunks, VIRT, HDIM),
        ],
        [
            jax.ShapeDtypeStruct((rows, length, D), BF16),
            jax.ShapeDtypeStruct((rows, length, D), F32),
            jax.ShapeDtypeStruct((rows, HEADS, chunks, HDIM, HDIM), BF16),
            jax.ShapeDtypeStruct((rows, HEADS, chunks, VIRT, HDIM), BF16),
        ],
        [q, k, wu, p, col, *states_in, gate, gain.astype(F32)[None]],
        order=order,
        name="mix",
        cost=11.0,
    )


def adjoint_kernel(
    core_ref, up_ref, mixed_ref, gate_ref, gain_ref, q_ref, wu_ref, p_ref, m_ref, col_ref,
    grad_mixed_ref, grad_gate_ref, grad_gain_ref, own_ref,
):
    heads, chunks = p_ref.shape[1:3]

    def one(sub):
        lanes = lanes_of(sub)
        cols = head_columns(col_ref, heads * pl.program_id(1) + sub)
        upstream, mixed, gate = up_ref[0, :, lanes], mixed_ref[0, :, lanes], gate_ref[0, :, lanes]
        gain = gain_ref[...]
        sig = sigmoid(gate)
        scale = lax.rsqrt(lane_sums(mixed * mixed) * (1.0 / HDIM) + EPSILON)
        unit = mixed * scale
        grad_gate_ref[0, :, lanes] = (
            upstream * unit * gain * (sig * (1.0 + gate * (1.0 - sig)))
        ).astype(BF16)
        upstream = upstream * (gate * sig)
        partial_gain = upstream * unit
        grad_gain_ref[0, sub] = jnp.sum(
            partial_gain.reshape(partial_gain.shape[0] // 8, 8, HDIM), axis=0
        )
        weighted = gain * upstream
        grad_mixed = scale * (weighted - unit * (lane_sums(unit * weighted) * (1.0 / HDIM)))
        low = grad_mixed.astype(BF16)
        grad_mixed_ref[0, :, lanes] = low
        yield
        grad_state = None
        for chunk in reversed(range(chunks)):
            at = chunk * CHUNK
            rows = slice(at, at + CHUNK)
            own_delta = mm(p_ref[0, sub, chunk], low[rows], (0, 0))
            yield
            left = jnp.concatenate(
                [(grad_mixed[rows] * cols[rows, 24:25]).astype(BF16), (-own_delta).astype(BF16)],
                axis=0,
            )
            right = jnp.concatenate([q_ref[0, sub, rows], wu_ref[0, sub, chunk, :, :HDIM]], axis=0)
            own = mm(left, right, (0, 0))
            if grad_state is not None:
                own = own + mm(grad_state, m_ref[0, sub, chunk], (1, 1))
            grad_state = own
            yield
        own_ref[0, 0, sub] = grad_state.astype(BF16)

    in_turns([one(sub) for sub in range(heads)])


def adjoint(upstream, mixed, gate, gain, q, wu, p, m, col, order):
    rows, _, length = q.shape[:3]
    chunks = length // CHUNK
    return call_with_core(
        adjoint_kernel,
        (rows, HEADS // PAIR),
        [
            column_spec(length),
            column_spec(length),
            column_spec(length),
            pl.BlockSpec((1, HDIM), lambda r, h, *_: (0, 0)),
            head_spec(length, HDIM),
            head_spec(chunks, VIRT, VIRT),
            head_spec(chunks, CHUNK, VIRT),
            head_spec(chunks, HDIM, HDIM),
            rate_specs(length)[0],
        ],
        [
            column_spec(length),
            column_spec(length),
            head_spec(8, HDIM),
            slot_spec(rows),
        ],
        [
            jax.ShapeDtypeStruct((rows, length, D), BF16),
            jax.ShapeDtypeStruct((rows, length, D), BF16),
            jax.ShapeDtypeStruct((rows, HEADS, 8, HDIM), F32),
            jax.ShapeDtypeStruct((2, rows // 2, HEADS, HDIM, HDIM), BF16),
        ],
        [upstream, mixed, gate, gain.astype(F32)[None], q, wu, p, m, col],
        order=order,
        name="adjoint",
        cost=11.0,
    )


def before(count, dim):
    place = iota2((count, count), dim)
    return NH * (place % CHUNK) + place // CHUNK


def back_kernel(first, rows, core_ref, *refs):
    xs, halos, taps = refs[0:5], refs[5:10], refs[10:15]
    keep_ref, col_ref, row_ref, mask_ref = refs[15:19]
    q_ref, shift_ref = refs[19], refs[-1]
    length = xs[0].shape[1]
    chunks = length // CHUNK
    heads = q_ref.shape[1]
    stats_ref = refs[-3]

    @pl.when(pl.program_id(1) == 0)
    def _():
        stats_ref[...] = jnp.zeros_like(stats_ref)

    strict = (before(VIRT, 0) > before(VIRT, 1)).astype(F32)
    for tap in range(3):
        shift_ref[tap, 0:8] = jnp.zeros((8, HDIM), F32)
        shift_ref[tap, 8 + length : 16 + length] = jnp.zeros((8, HDIM), F32)
    in_turns(
        [
            back_head(
                first, rows, core_ref, sub, heads, xs, halos, taps, keep_ref, col_ref, row_ref, mask_ref, strict, refs[19:],
            )
            for sub in range(heads)
        ]
    )


def back_head(
    first, row_count, core_ref, sub, heads, xs, halos, taps, keep_ref, col_ref, row_ref, mask_ref,
    strict, refs,
):
    q_ref, k_ref, v_ref, t_ref, wu_ref, p_ref, states_ref, delta_ref = refs[:8]
    grad_mixed_ref, own_ref, other_ref = refs[8:11]
    gp_ref, gh_ref, gw_ref, stats_ref, ext_ref, shift_ref = refs[11:]
    length = xs[0].shape[1]
    chunks = length // CHUNK
    head = first + heads * pl.program_id(1) + sub
    lanes = lanes_of(sub)
    cols = head_columns(col_ref, head)
    own_row = iota2((HEADS, CHUNK), 0) == head
    grad_next = entering_state(core_ref, own_ref, other_ref, sub, row_count)
    grads = [[None] * chunks for _ in range(GROUPS)]
    for chunk in reversed(range(chunks)):
        at = chunk * CHUNK
        rows = slice(at, at + CHUNK)
        query = q_ref[0, sub, rows]
        query_float = query.astype(F32)
        keys, values = k_ref[0, sub, chunk], v_ref[0, sub, chunk]
        keys_float, values_float = keys.astype(F32), values.astype(F32)
        solved, scores = wu_ref[0, sub, chunk], p_ref[0, sub, chunk]
        state, delta = states_ref[0, sub, chunk], delta_ref[0, sub, chunk]
        grad_out = grad_mixed_ref[0, rows, lanes]
        beta = jnp.concatenate([wide(cols[rows, 0:1]), wide(cols[rows, 8:9])], axis=0)
        beta_wide = jnp.concatenate([beta, beta], axis=1)
        start, tail = wide(cols[rows, 24:25]), wide(cols[rows, 32:33])
        start_wide, tail_wide = both(start), both(tail)
        end = cols[at + CHUNK - 1 : at + CHUNK, 24:25]
        decay = decay_matrix(cols, row_ref, mask_ref, head, chunk)
        wide_decay = jnp.concatenate([decay, decay], axis=1)
        full_decay = both(wide_decay) * strict
        next_low = grad_next.astype(BF16)
        tail_keys = (keys_float * tail_wide).astype(BF16)
        grad_delta = mm(scores, grad_out, (0, 0)) + mm(tail_keys, next_low, (1, 1))
        delta_low = grad_delta.astype(BF16)
        grad_scores = mm(grad_out, delta, (1, 1))
        weighted_scores = grad_scores * scores.astype(F32)
        grad_raw = (grad_scores * wide_decay).astype(BF16)
        yield
        seen = mm(jnp.concatenate([grad_out, delta_low], axis=0), state)
        grad_query = start * seen[:CHUNK] + mm(grad_raw, keys)
        by_start = seen[:CHUNK] * query_float
        grad_wide = jnp.concatenate([-seen[CHUNK:], grad_delta], axis=1).astype(BF16)
        grad_end = jnp.sum(
            jnp.sum(grad_next * state.astype(F32), axis=0, keepdims=True), axis=1, keepdims=True
        )
        grad_tail_keys = mm(delta, next_low)
        left = jnp.concatenate(
            [(grad_out.astype(F32) * start).astype(BF16), (-grad_delta).astype(BF16)], axis=0
        )
        grad_next = end * grad_next + mm(
            left, jnp.concatenate([query, solved[:, :HDIM]], axis=0), (0, 0)
        )
        yield
        grad_right = mm(t_ref[0, sub, chunk], grad_wide, (0, 0))
        yield
        right_keys, right_values = grad_right[:, :HDIM], grad_right[:, HDIM:]
        grad_mixing = -mm(grad_right, solved, (1, 1))
        gram = mm(keys, keys, (1, 1))
        decayed = grad_mixing * full_decay
        weighted = decayed * gram
        grad_gram = (decayed * beta_wide).astype(BF16)
        yield
        by_keys = keys_float * right_keys
        by_values = values_float * right_values
        by_mixing = weighted[:, :CHUNK] + weighted[:, CHUNK:]
        grad_keys = (
            (start_wide * beta) * right_keys
            + tail_wide * grad_tail_keys
            + mm(grad_raw, query, (0, 0))
            + mm(grad_gram, keys)
            + mm(grad_gram, keys, (0, 0))
        )
        grad_values = beta * right_values
        fold = lambda tensor: tensor[:CHUNK] + tensor[CHUNK:]
        pairs = fold(beta * by_mixing) + weighted_scores[:, :CHUNK] + weighted_scores[:, CHUNK:]
        by_tail = fold(keys_float * grad_tail_keys) * tail
        by_log = pairs + (by_start + fold(beta * by_keys)) * start
        by_beta = start_wide * by_keys + by_values + by_mixing
        sums = row_sums(jnp.concatenate([by_beta, by_log, by_tail], axis=0))
        tail_sums = sums[:, 3 * CHUNK :]
        at_end = jnp.sum(tail_sums, axis=1, keepdims=True) + grad_end * end
        last = iota2((1, CHUNK), 1) == CHUNK - 1
        log_sums = sums[:, 2 * CHUNK : 3 * CHUNK] - tail_sums - column_sums(pairs)
        log_sums = log_sums + jnp.where(last, at_end, 0.0)
        for place, member in enumerate((sums[:, :CHUNK], sums[:, CHUNK : 2 * CHUNK], log_sums)):
            spot = slice(place * HEADS, place * HEADS + HEADS)
            stats_ref[0, spot, rows] = jnp.where(own_row, member, stats_ref[0, spot, rows])
        for group, member in enumerate(
            (grad_query, grad_keys[:CHUNK], grad_keys[CHUNK:], grad_values[:CHUNK], grad_values[CHUNK:])
        ):
            grads[group][chunk] = member
        yield
    for group in range(GROUPS):
        ext = ext_ref.at[group]
        summed = convolved(xs[group], halos[group], taps[group], keep_ref, ext, lanes)
        sig = sigmoid(summed)
        active = summed * sig
        grad = jnp.concatenate(grads[group], axis=0).astype(BF16).astype(F32)
        if group < 1 + NH:
            scale = lax.rsqrt(lane_sums(active * active) + EPSILON)
            unit = active * scale
            grad = scale * (grad - unit * lane_sums(unit * grad))
        grad = grad * (sig * (1.0 + summed * (1.0 - sig)))
        total = grad * taps[group][3:4, lanes]
        before = None
        weight_rows = []
        for tap in range(3):
            kept = grad * keep_ref[0, tap]
            weight_rows.append(
                jnp.sum(kept * ext[5 + tap : 5 + tap + length], axis=0, keepdims=True)
            )
            shift_ref[tap, 8 : 8 + length] = kept * taps[group][tap : tap + 1, lanes]
            total = total + shift_ref[tap, 11 - tap : 11 - tap + length]
            early = shift_ref[tap, 3 - tap : 11 - tap]
            before = early if before is None else before + early
        weight_rows.append(
            jnp.sum(grad * ext[8 : 8 + length], axis=0, keepdims=True)
        )
        gp_ref[group, 0, :, lanes] = total.astype(BF16)
        gh_ref[group, 0, :, lanes] = before.astype(BF16)
        gw_ref[0, group, sub] = jnp.concatenate(
            weight_rows + [jnp.zeros((4, HDIM), F32)], axis=0
        )


def back(first, count, projected, halo, taps, keep, col, row, mask, saved, grad_mixed, adjoints, order):
    rows, length = projected.shape[:2]
    chunks = length // CHUNK
    spec = partial(head_spec, first=first)
    return call_with_core(
        partial(back_kernel, first, rows),
        (rows, count // PAIR),
        conv_specs(length, first)
        + rate_specs(length)
        + [
            spec(length, HDIM),
            spec(chunks, VIRT, HDIM),
            spec(chunks, VIRT, HDIM),
            spec(chunks, VIRT, VIRT),
            spec(chunks, VIRT, VIRT),
            spec(chunks, CHUNK, VIRT),
            spec(chunks, HDIM, HDIM),
            spec(chunks, VIRT, HDIM),
            column_spec(length, first),
            entering_spec(rows, first),
            entering_spec(rows, first),
        ],
        [
            pl.BlockSpec((GROUPS, 1, length, PAIR * HDIM), lambda r, h, *_: (0, r, 0, h)),
            pl.BlockSpec((GROUPS, 1, 8, PAIR * HDIM), lambda r, h, *_: (0, r, 0, h)),
            pl.BlockSpec((1, GROUPS, PAIR, 8, HDIM), lambda r, h, *_: (r, 0, h, 0, 0)),
            pl.BlockSpec((1, 24, length), lambda r, h, *_: (r, 0, 0)),
        ],
        [
            jax.ShapeDtypeStruct((GROUPS, rows, length, count * HDIM), BF16),
            jax.ShapeDtypeStruct((GROUPS, rows, 8, count * HDIM), BF16),
            jax.ShapeDtypeStruct((rows, GROUPS, count, 8, HDIM), F32),
            jax.ShapeDtypeStruct((rows, 24, length), F32),
        ],
        [projected] * 5 + [halo] * 5 + [taps] * 5
        + [keep, col, row, mask, *saved, grad_mixed, *adjoints],
        [
            pltpu.VMEM((GROUPS, length + 8, HDIM), F32),
            pltpu.VMEM((3, length + 16, HDIM), F32),
        ],
        order,
        name="back",
        cost=LONG,
    )


def rates_kernel(core_ref, *refs):
    row_ref, nega_ref, rates_ref, sums_ref = refs[-4:]
    rows, _, length = row_ref.shape
    shape = (length, length)
    here, there = iota2(shape, 0), iota2(shape, 1)
    lower = ((here >= there) & (here // CHUNK == there // CHUNK)).astype(F32)
    lane = iota2((HEADS, HDIM), 1)
    total = jnp.zeros((HEADS, HDIM), F32)
    for r in range(rows):
        beta = row_ref[r, 0:16]
        stats = sum(ref[r] for ref in refs[:-4])
        grad_log = exact_mm(stats[16:24], lower)
        grad_bias = grad_log * nega_ref[:, 0:1] * row_ref[r, 40:48]
        rates_ref[r, 0:16] = (stats[0:16] * beta * (1.0 - beta)).astype(BF16)
        rates_ref[r, 16:24] = grad_bias.astype(BF16)
        rates_ref[r, 24:32] = jnp.zeros((8, length), BF16)
        by_log = jnp.sum(grad_log * row_ref[r, 48:56], axis=1, keepdims=True)
        by_bias = jnp.sum(grad_bias, axis=1, keepdims=True)
        total = total + jnp.where(lane == 0, by_log, jnp.where(lane == 1, by_bias, 0.0))
    sums_ref[...] = total


def rates_back(stats, row, a_log, order):
    rows, _, length = stats[0].shape
    nega = jnp.broadcast_to(-jnp.exp(a_log)[:, None], (HEADS, HDIM))
    return whole_call(
        rates_kernel,
        [*stats, row, nega],
        [
            jax.ShapeDtypeStruct((rows, 32, length), BF16),
            jax.ShapeDtypeStruct((HEADS, HDIM), F32),
        ],
        order,
        "rates_back",
        LONG,
    )


def to_core(value):
    count = lax.axis_size("seq")
    return lax.ppermute(value, "seq", [(at, at ^ 1) for at in range(count)])


def to_chip(value, step):
    count = lax.axis_size("seq")
    pairs = [(at, at + 2 * step) for at in range(count) if 0 <= at + 2 * step < count]
    return lax.ppermute(value, "seq", pairs)


def along(value, step):
    count = lax.axis_size("seq")
    pairs = [(at, at + step) for at in range(count) if 0 <= at + step < count]
    return lax.ppermute(value, "seq", pairs)


def whole_call(kernel, args, out_shape, order, name, cost=1.0):
    return call_with_core(
        kernel,
        (1,),
        [pl.BlockSpec(arg.shape, lambda t, c, n=arg.ndim: (0,) * n) for arg in args],
        [pl.BlockSpec(out.shape, lambda t, c, n=len(out.shape): (0,) * n) for out in out_shape],
        out_shape,
        args,
        order=order,
        name=name,
        limit=VMEM_SMALL,
        cost=cost,
    )


def chip_maps_kernel(core_ref, own_ref, other_ref, m_ref, b_ref, leaving_ref):
    own_first = core_ref[0] == 0
    for at in range(own_ref.shape[1]):
        own_m, own_b = own_ref[0, at].astype(F32), own_ref[1, at].astype(F32)
        other_m, other_b = other_ref[0, at].astype(F32), other_ref[1, at].astype(F32)
        first = jnp.concatenate(
            [jnp.where(own_first, own_m, other_m), jnp.where(own_first, own_b, other_b)], axis=0
        )
        second_m = jnp.where(own_first, other_m, own_m)
        second_b = jnp.where(own_first, other_b, own_b)
        both_maps = mm(first, second_m)
        m_ref[at] = both_maps[:HDIM].astype(BF16)
        total = both_maps[HDIM:] + second_b
        b_ref[at] = total
        leaving_ref[at] = total.astype(BF16)


def chip_grads_kernel(core_ref, own_ref, other_ref, own_m_ref, other_m_ref, b_ref, leaving_ref):
    own_first = core_ref[0] == 1
    for at in range(own_ref.shape[0]):
        own, other = own_ref[at].astype(F32), other_ref[at].astype(F32)
        own_m, other_m = own_m_ref[at].astype(F32), other_m_ref[at].astype(F32)
        first = jnp.where(own_first, own, other)
        second = jnp.where(own_first, other, own)
        second_m = jnp.where(own_first, other_m, own_m)
        total = mm(first, second_m, (1, 1)) + second
        b_ref[at] = total
        leaving_ref[at] = total.astype(BF16)


def hop_kernel(over, core_ref, entering_ref, m_ref, b_ref, leaving_ref):
    for at in range(entering_ref.shape[0]):
        leaving_ref[at] = (mm(entering_ref[at], m_ref[at], over) + b_ref[at]).astype(BF16)


def last_kernel(over, first_core, core_ref, entering_ref, own_m, other_m, own_b, other_b, keep_ref, give_ref):
    own_first = core_ref[0] == first_core
    for at in range(entering_ref.shape[0]):
        entering = entering_ref[at].astype(F32)
        first_m = jnp.where(own_first, own_m[at].astype(F32), other_m[at].astype(F32))
        first_b = jnp.where(own_first, own_b[at].astype(F32), other_b[at].astype(F32))
        between = mm(entering, first_m, over) + first_b
        keep_ref[at] = jnp.where(own_first, entering, between).astype(BF16)
        give_ref[at] = jnp.where(own_first, between, entering).astype(BF16)


def carried(own_m, other_m, own_b, other_b, chip_m, chip_b, leaving, step, order, meanwhile=()):
    over, first_core = ((1, 0), 0) if step > 0 else ((1, 1), 1)
    low = jax.ShapeDtypeStruct(leaving.shape, BF16)
    hops = lax.axis_size("seq") // 2 - 1
    for at in range(hops):
        entering = to_chip(leaving, step)
        if at < len(meanwhile):
            meanwhile[at]()
        if at + 1 < hops:
            (leaving,) = whole_call(
                partial(hop_kernel, over), [entering, chip_m, chip_b], [low], order, "hop"
            )
    keep, give = whole_call(
        partial(last_kernel, over, first_core),
        [entering, own_m, other_m, own_b, other_b],
        [low, low],
        order,
        "entering",
    )
    return keep, to_core(give)


def project_kernel(core_ref, x_ref, w_ref, out_ref):
    out_ref[...] = jnp.dot(x_ref[...], w_ref[...], preferred_element_type=F32)


def project(x, w, order, tile=256):
    return call_with_core(
        project_kernel,
        (w.shape[1] // tile,),
        [
            pl.BlockSpec(x.shape, lambda t, c: (0, 0)),
            pl.BlockSpec((w.shape[0], tile), lambda t, c: (0, t)),
        ],
        pl.BlockSpec((x.shape[0], tile), lambda t, c: (0, t)),
        jax.ShapeDtypeStruct((x.shape[0], w.shape[1]), F32),
        [x, w],
        order=order,
        name="project",
        cost=LONG,
    )


def weight_kernel(sides, per, core_ref, *refs):
    keep_ref, send_ref, turned_ref, ordered_ref, y_scratch = refs[-5:]
    chips, rows = keep_ref.shape[:2]
    half = chips * rows
    pairs = 1 if sides else (len(refs) - 5) // 2
    width = keep_ref.shape[2]
    step = 512 if width % 512 == 0 else width // 2 if width > 512 else width

    def product(y):
        for at in range(0, width, step):
            spot = slice(at, at + step)
            total = jnp.dot(ordered_ref[...], y[:, spot], preferred_element_type=F32).astype(BF16)
            keep_ref[:, :, spot] = total[:half].reshape(chips, rows, step)
            send_ref[:, :, spot] = total[half:].reshape(chips, rows, step)

    def turn(x_ref):
        turned_ref[...] = x_ref[...].T
        for chip in range(chips):
            for which in range(2):
                core = core_ref[0] if which == 0 else 1 - core_ref[0]
                at = pl.multiple_of((2 * chip + core) * rows, rows)
                ordered_ref[which * half + chip * rows : which * half + (chip + 1) * rows] = (
                    turned_ref[pl.ds(at, rows)]
                )

    for pair in range(pairs):
        pl.when(pl.program_id(0) == pair * per)(partial(turn, refs[pair]))
    if sides:
        mend(refs[1 : 1 + sides], refs[1 + sides], y_scratch)
        product(y_scratch)
    elif pairs == 1:
        product(refs[1].at[0])
    else:
        for pair in range(pairs):
            pl.when(pl.program_id(0) // per == pair)(partial(product, refs[pairs + pair].at[0]))


def local_kernel(core_ref, x_ref, y_ref, out_ref):
    out_ref[...] = mm(x_ref[...], y_ref[...], (0, 0)).astype(BF16)


def local_grad(x, y, order, tile=256):
    positions, inputs = x.shape
    return call_with_core(
        local_kernel,
        (inputs // tile,),
        [
            pl.BlockSpec((positions, tile), lambda t, c: (0, t)),
            pl.BlockSpec(y.shape, lambda t, c: (0, 0)),
        ],
        pl.BlockSpec((tile, y.shape[1]), lambda t, c: (t, 0)),
        jax.ShapeDtypeStruct((inputs, y.shape[1]), BF16),
        [x, y],
        order=order,
        name="local_grad",
        cost=1.0,
    )


def copy_kernel(core_ref, x_ref, out_ref):
    out_ref[...] = x_ref[...]


def placed(array, order):
    shape = jax.ShapeDtypeStruct(array.shape, array.dtype)
    return whole_call(copy_kernel, [array], [shape], order, "placed")[0]


def mend(y_refs, fix_ref, y_scratch):
    at = 0
    for y_ref in y_refs:
        y_scratch[:, at : at + y_ref.shape[2]] = y_ref[0]
        at += y_ref.shape[2]
    parts = fix_ref.shape[1]
    length = y_scratch.shape[0] // parts
    for part in range(parts):
        end = (part + 1) * length
        y_scratch[end - 16 : end] = y_scratch[end - 16 : end] + fix_ref[0, part]


def weight_grads(xs, ys, order, fix=None, width=None, cost=LONG):
    positions, inputs = xs[0].shape
    tiles = ys[0].shape[0]
    columns = ys[0].shape[2] if fix is None else sum(member.shape[2] for member in ys)
    width = width or columns
    count = columns // width
    per = tiles * count
    chips = lax.axis_size("seq") // 2
    rows = inputs // (2 * chips)
    out = jax.ShapeDtypeStruct((chips, rows, len(xs) * tiles * columns), BF16)
    out_spec = pl.BlockSpec((chips, rows, width), lambda t, c: (0, 0, t))
    in_specs = [pl.BlockSpec((positions, inputs), lambda t, c: (0, 0)) for _ in xs]
    if fix is None:

        def place(pair, t, c):
            t = jnp.clip(t - pair * per, 0, per - 1)
            return (t // count, 0, t % count)

        in_specs += [
            pl.BlockSpec((1, positions, width), partial(place, pair)) for pair in range(len(xs))
        ]
    else:
        in_specs += [
            pl.BlockSpec((1, positions, member.shape[2]), lambda t, c: (t, 0, 0)) for member in ys
        ]
        in_specs.append(pl.BlockSpec((1,) + fix.shape[1:], lambda t, c: (t, 0, 0, 0)))
    return call_with_core(
        partial(weight_kernel, 0 if fix is None else len(ys), per),
        (len(xs) * per,),
        in_specs,
        [out_spec, out_spec],
        [out, out],
        [*xs, *ys] + ([] if fix is None else [fix]),
        [
            pltpu.VMEM((inputs, positions), BF16),
            pltpu.VMEM((inputs, positions), BF16),
            pltpu.VMEM((positions, width), BF16),
        ],
        order,
        name="weight_grads",
        cost=cost,
    )


def dense_kernel(
    core_ref, branch_ref, x_ref, w_out_ref, gain_ref, w_gate_ref, w_up_ref, w_down_ref, cot_ref,
    out_ref, normed_ref, act_ref, grad_up_ref, hidden_out_ref, attended_ref, branch_out_ref,
    hidden_ref, out_total_ref, back_total_ref,
):
    step = pl.program_id(0)

    @pl.when(step == 0)
    def _():
        hidden = x_ref[...].astype(F32) + jnp.dot(
            branch_ref[...], w_out_ref[...], preferred_element_type=F32
        )
        hidden_ref[...] = hidden
        scale = lax.rsqrt(jnp.mean(hidden * hidden, axis=-1, keepdims=True) + EPSILON)
        normed_ref[...] = (hidden * scale * gain_ref[...]).astype(BF16)
        out_total_ref[...] = hidden
        back_total_ref[...] = jnp.zeros_like(back_total_ref)

    normed = normed_ref[...]
    gate = mm(normed, w_gate_ref[...])
    up = mm(normed, w_up_ref[...])
    grad_act = mm(cot_ref[...], w_down_ref[...], (1, 1))
    sig = sigmoid(gate)
    active = gate * sig
    act = (active * up).astype(BF16)
    grad_gate = (grad_act * up * (sig * (1.0 + gate * (1.0 - sig)))).astype(BF16)
    grad_up = (grad_act * active).astype(BF16)
    act_ref[...] = act
    grad_up_ref[0] = grad_gate
    grad_up_ref[1] = grad_up
    out_total_ref[...] += mm(act, w_down_ref[...])
    back_total_ref[...] += mm(grad_gate, w_gate_ref[...], (1, 1)) + mm(
        grad_up, w_up_ref[...], (1, 1)
    )

    @pl.when(step == pl.num_programs(0) - 1)
    def _():
        out_ref[...] = out_total_ref[...].astype(BF16)
        hidden = hidden_ref[...]
        scale = lax.rsqrt(jnp.mean(hidden * hidden, axis=-1, keepdims=True) + EPSILON)
        unit = hidden * scale
        weighted = gain_ref[...] * back_total_ref[...]
        back = scale * (weighted - unit * jnp.mean(unit * weighted, axis=-1, keepdims=True))
        grad_hidden = cot_ref[...].astype(F32) + back
        hidden_out_ref[...] = grad_hidden
        attended = grad_hidden.astype(BF16)
        attended_ref[...] = attended
        branch_out_ref[...] = mm(attended, w_out_ref[...], (1, 1))


def dense(branch, x, w_out, gain, w_up, w_down, cotangent, order, tile=256):
    positions = x.shape[0]
    steps = FF // tile
    full = lambda *shape: pl.BlockSpec(shape, lambda t, c: (0,) * len(shape))
    wide = full(positions, D)
    low = jax.ShapeDtypeStruct((positions, D), BF16)
    high = jax.ShapeDtypeStruct((positions, D), F32)
    return call_with_core(
        dense_kernel,
        (steps,),
        [
            wide, wide, full(D, D), full(1, D),
            pl.BlockSpec((D, tile), lambda t, c: (0, t)),
            pl.BlockSpec((D, tile), lambda t, c: (0, steps + t)),
            pl.BlockSpec((tile, D), lambda t, c: (t, 0)),
            wide,
        ],
        [
            wide, wide,
            pl.BlockSpec((positions, tile), lambda t, c: (0, t)),
            pl.BlockSpec((2, positions, tile), lambda t, c: (0, 0, t)),
            wide, wide, wide,
        ],
        [
            low, low,
            jax.ShapeDtypeStruct((positions, FF), BF16),
            jax.ShapeDtypeStruct((2, positions, FF), BF16),
            high, low, high,
        ],
        [branch, x, w_out, gain.astype(F32)[None], w_up, w_up, w_down, cotangent],
        [pltpu.VMEM((positions, D), F32)] * 3,
        order,
        name="dense",
        cost=30.0,
    )


def input_kernel(count, core_ref, *refs):
    y_refs, fix_ref = refs[:count], refs[count]
    w_ref, gate_ref, w_gate_ref, rates_ref, w_rates_ref, x_ref, gain_ref, hidden_ref = refs[
        count + 1 : count + 9
    ]
    out_ref, total_ref, y_scratch = refs[count + 9 :]
    step = pl.program_id(0)
    parts = x_ref.shape[0]
    length = y_scratch.shape[0] // parts

    @pl.when(step == 0)
    def _():
        total_ref[...] = mm(gate_ref[...], w_gate_ref[...], (1, 1))
        for part in range(parts):
            spot = slice(part * length, (part + 1) * length)
            total_ref[spot] = total_ref[spot] + mm(rates_ref[part], w_rates_ref[...], (0, 1))

    mend(y_refs, fix_ref, y_scratch)
    total_ref[...] += mm(y_scratch[...], w_ref[...], (1, 1))

    @pl.when(step == pl.num_programs(0) - 1)
    def _():
        for part in range(parts):
            spot = slice(part * length, (part + 1) * length)
            x = x_ref[part].astype(F32)
            scale = lax.rsqrt(jnp.mean(x * x, axis=-1, keepdims=True) + EPSILON)
            unit = x * scale
            weighted = gain_ref[...] * total_ref[spot]
            back = scale * (weighted - unit * jnp.mean(unit * weighted, axis=-1, keepdims=True))
            out_ref[part] = (hidden_ref[spot] + back).astype(BF16)


def input_grad(ys, fix, w_qkv, grad_gate, w_gate, rates, w_rates, x, gain, hidden, order):
    groups, positions, width = ys[0].shape
    parts = x.shape[0]
    full = lambda array: pl.BlockSpec(array.shape, lambda t, c: (0,) * array.ndim)
    w_rates = jnp.pad(w_rates, ((0, 0), (0, rates.shape[1] - w_rates.shape[1])))
    gain = gain.astype(F32)[None]
    rest = [grad_gate, w_gate, rates, w_rates, x, gain, hidden]
    return call_with_core(
        partial(input_kernel, len(ys)),
        (groups,),
        [pl.BlockSpec((1, positions, width), lambda t, c: (t, 0, 0))] * len(ys)
        + [
            pl.BlockSpec((1, parts, 16, D), lambda t, c: (t, 0, 0, 0)),
            pl.BlockSpec((D, D), lambda t, c: (0, t)),
        ]
        + [full(member) for member in rest],
        full(x),
        jax.ShapeDtypeStruct(x.shape, BF16),
        [*ys, fix, w_qkv, *rest],
        [pltpu.VMEM((positions, D), F32), pltpu.VMEM((positions, D), BF16)],
        order,
        name="input_grad",
        cost=LONG,
    )


def bits(count):
    return range(count.bit_length() - 1)


def swap(value, axis, bit):
    count = lax.axis_size(axis)
    return lax.ppermute(value, axis, [(at, at ^ (1 << bit)) for at in range(count)])


def own_bit(axis, bit):
    return ((lax.axis_index(axis) >> bit) & 1).astype(jnp.int32).reshape(1)


def round_kernel(splits, count, bit_ref, *refs):
    step = 4 if splits else 2
    outs = refs[step * count :]
    at = 0
    for member in range(count):
        blocks = refs[step * member : step * member + step]
        width = blocks[0].shape[-1]
        for half in range(step // 2):
            own, got = blocks[2 * half], blocks[2 * half + 1]
            total = own[...].astype(F32) + got[...].astype(F32)
            out = outs[half]
            out[:, :, at : at + width] = total.reshape(out.shape[:2] + (width,)).astype(BF16)
        at += width


def added(members, split, order, name):
    columns = sum(member[3] for member in members)
    size = members[0][0].shape[0] * members[0][0].shape[1]
    args, in_specs = [], []
    if split is None:
        bit, ahead, behind = jnp.zeros((1,), jnp.int32), 1, size
    else:
        bit, ahead, behind = split
    for own, got, at, width in members:
        for half in range(1 if split is None else 2):
            for array in (own, got):
                if split is None:
                    args.append(array.reshape(1, size, array.shape[2]))
                    spec = pl.BlockSpec((1, behind, width), lambda a, b, n=at // width: (0, 0, n))
                else:
                    args.append(array.reshape(ahead, 2, behind, array.shape[2]))
                    spec = pl.BlockSpec(
                        (1, 1, behind, width),
                        lambda a, b, h=half, n=at // width: (a, b[0] ^ (1 - h), 0, n),
                    )
                in_specs.append(spec)
    out = jax.ShapeDtypeStruct((ahead, behind, columns), BF16)
    out_spec = pl.BlockSpec((1, behind, columns), lambda a, b: (a, 0, 0))
    outs = 1 if split is None else 2
    return call_with_core(
        partial(round_kernel, split is not None, len(members)),
        (ahead,),
        in_specs,
        [out_spec] * outs,
        [out] * outs,
        args,
        order=order,
        name=name,
        scalar=bit,
        limit=VMEM_SMALL,
        cost=3.0,
    )


def pair_kernel(bit_ref, value_ref, got_ref, out_ref):
    out_ref[:, pl.ds(bit_ref[0], 1)] = value_ref[...][:, None]
    out_ref[:, pl.ds(1 - bit_ref[0], 1)] = got_ref[...][:, None]


class Stream:
    def __init__(self, order, parts):
        self.order = order
        self.chips, self.rows = parts[0][0][0].shape[:2]
        self.count = lax.axis_size("row")
        self.share = self.rows // self.count
        self.parts = [list(part) for part in parts]
        row_bits = list(bits(self.count))
        self.row_plans = [row_bits, row_bits[::-1]]
        self.dims = [
            [("seq", bit + 1) for bit in bits(self.chips)][::-1]
            + [("row", bit) for bit in row_bits[::-1]]
            for _ in parts
        ]
        self.gathered = []

    def exchange(self, members, dims, name):
        place = dims.index(name)
        ahead, behind = 1 << place, (1 << (len(dims) - 1 - place)) * self.share
        sent, kept = added(members, (own_bit(*name), ahead, behind), self.order, "exchange")
        dims.remove(name)
        return (kept, swap(sent, *name), 0, kept.shape[2])

    def along_row_rest(self):
        for step in range(1, len(self.row_plans[0])):
            self.along_row(step)

    def along_seq_rest(self):
        for step in range(1, len(bits(self.chips))):
            self.along_seq(step)

    def gather_rest(self):
        for _ in range(1, len(self.row_plans[0])):
            self.gather()

    def along_row(self, step):
        for at, part in enumerate(self.parts):
            name = ("row", self.row_plans[at][step])
            self.parts[at] = [self.exchange(part, self.dims[at], name)]

    def along_seq(self, step):
        if len(self.parts) > 1:
            self.parts = [[member for part in self.parts for member in part]]
        self.parts[0] = [self.exchange(self.parts[0], self.dims[0], ("seq", step + 1))]

    def finish_offloaded(self):
        members = [member for part in self.parts for member in part]
        (value,) = added(members, None, self.order, "share")
        groups = [[2 * chip + core for chip in range(self.chips)] for core in range(2)]
        self.share_value = lax.psum_scatter(
            value[0], "seq", scatter_dimension=0, axis_index_groups=groups, tiled=True
        )
        self.value = lax.all_gather(self.share_value, "row", axis=0, tiled=True)[None]

    def share_found(self):
        members = [member for part in self.parts for member in part]
        (self.value,) = added(members, None, self.order, "share")
        self.value = self.value.reshape(1, self.share, -1)
        self.have = []
        self.send_gathered()

    def send_gathered(self):
        if len(self.have) < len(self.row_plans[0]):
            self.bit = self.row_plans[0][::-1][len(self.have)]
            self.got = swap(self.value, "row", self.bit)

    def gather(self):
        self.have = sorted(self.have + [self.bit], reverse=True)
        place = self.have.index(self.bit)
        ahead = 1 << place
        width = self.value.shape[-1]
        size = self.value.shape[0] * self.value.shape[1]
        value = self.value.reshape(ahead, size // ahead, width)
        got = self.got.reshape(ahead, size // ahead, width)
        spec = pl.BlockSpec(value.shape, lambda t, b: (0, 0, 0))
        out = jax.ShapeDtypeStruct((ahead, 2, size // ahead, width), BF16)
        self.value = call_with_core(
            pair_kernel,
            (1,),
            [spec, spec],
            pl.BlockSpec(out.shape, lambda t, b: (0, 0, 0, 0)),
            out,
            [value, got],
            order=self.order,
            name="gather",
            limit=VMEM_SMALL,
            scalar=own_bit("row", self.bit),
        ).reshape(1, 2 * size, width)
        self.send_gathered()

    def total(self):
        return self.value[0]


def final_kernel(pieces, seq_ref, *refs):
    count = len({piece[0] for piece in pieces})
    arrays, w_ref, out_ref, sums_ref = refs[:count], refs[count], refs[count + 1], refs[count + 2]
    partial_sums = jnp.zeros((out_ref.shape[0], HDIM), F32)
    for array, at, width, to in pieces:
        total = arrays[array][:, at : at + width].astype(F32)
        out_ref[:, to : to + width] = total
        weighted = total * w_ref[:, to : to + width].astype(F32)
        for lane in range(0, width, HDIM):
            partial_sums = partial_sums + weighted[:, lane : lane + HDIM]
    sums_ref[...] = partial_sums


def final(arrays, pieces, w, order):
    rows = arrays[0].shape[0]
    columns = w.shape[1]
    full = lambda *shape: pl.BlockSpec(shape, lambda t, c: (0, 0))
    return call_with_core(
        partial(final_kernel, pieces),
        (1,),
        [full(*array.shape) for array in arrays]
        + [pl.BlockSpec((rows, columns), lambda t, c: (c[0], 0))],
        [full(rows, columns), full(rows, HDIM)],
        [
            jax.ShapeDtypeStruct((rows, columns), F32),
            jax.ShapeDtypeStruct((rows, HDIM), F32),
        ],
        [*arrays, w],
        order=order,
        name="final",
        cost=3.0,
        scalar=lax.axis_index("seq").astype(jnp.int32).reshape(1),
    )


def sum_kernel(core_ref, own_ref, got_ref, out_ref):
    out_ref[...] = own_ref[...] + got_ref[...]


class Everywhere:
    def __init__(self, order, value):
        self.order, self.value = order, value
        self.plan = [
            (axis, bit) for axis in ("seq", "row") for bit in bits(lax.axis_size(axis))
        ]
        self.send()

    def send(self):
        if self.plan:
            self.got = swap(self.value, *self.plan.pop(0))
        else:
            self.got = None

    def step(self):
        if self.got is not None:
            shape = jax.ShapeDtypeStruct(self.value.shape, F32)
            (self.value,) = whole_call(
                sum_kernel, [self.value, self.got], [shape], self.order, "small"
            )
            self.send()


def half_product(formula, former, latter):
    return jnp.einsum(formula, former, latter, preferred_element_type=F32)


def shortened(value):
    return jax.tree.map(lambda part: part.astype(BF16), value)


def rms_norm(tensor, gain):
    return tensor * lax.rsqrt(jnp.mean(tensor * tensor, axis=-1, keepdims=True) + EPSILON) * gain


def swiglu(gate_up):
    return jax.nn.silu(gate_up[..., :FF]) * gate_up[..., FF:]


def find_docs(doc_ends, places):
    found = jnp.sum((places[None, :, None] >= doc_ends[:, None, :]).astype(jnp.int32), axis=2)
    return jnp.where(places[None, :] >= 0, found, -1)


def doc_masks(lengths, length):
    anchor = lax.axis_index("seq") * length
    doc_ends = jnp.cumsum(lengths, axis=1)
    extended = find_docs(doc_ends, anchor + jnp.arange(-3, length, dtype=jnp.int32))
    docs = extended[:, 3:]
    rows = docs.shape[0]
    keep = jnp.stack([extended[:, tap : tap + length] == docs for tap in range(3)], axis=1)
    keep = jnp.broadcast_to(keep.astype(F32)[..., None], keep.shape + (HDIM,))
    chunks = length // CHUNK
    blocks = docs.reshape(rows, chunks, CHUNK)
    before = find_docs(doc_ends, anchor + jnp.arange(0, length, CHUNK, dtype=jnp.int32) - 1)
    carry = blocks == before[..., None]
    same_last = blocks == blocks[..., -1:]
    flags = jnp.stack([carry, same_last], axis=-1).astype(F32).reshape(rows, length, 2)
    places = jnp.arange(CHUNK)
    allowed = (blocks[..., :, None] == blocks[..., None, :]) & (places[:, None] >= places)
    return keep, flags, jnp.where(allowed, 0.0, -1e30).astype(F32)


def local(
    hidden_in, lengths, norm1_gain, w_qkv, conv_w, w_rates, a_log, dt_bias,
    w_gate, out_gain, w_out, norm2_gain, w_up, w_down, cotangent,
):
    row_count, length = hidden_in.shape[:2]
    keep, flags, mask = doc_masks(lengths, length)
    level = levels()
    taps = conv_w.astype(F32).T
    normed, col, row = front(hidden_in, norm1_gain, w_rates, a_log, dt_bias, flags)
    projected = half_product("rld,de->rle", normed, w_qkv).astype(BF16)
    halo = along(projected[:, length - 8 :], 1)
    positions = row_count * length
    flat = lambda tensor: tensor.reshape(positions, tensor.shape[-1])
    unflat = lambda tensor: tensor.reshape(row_count, length, tensor.shape[-1])
    order = Order()
    q, k, v, t, wu, p, m, device = maps(
        projected, halo, taps, keep, col, row, mask, level, order
    )
    maps_shape = (row_count // 2 * HEADS, HDIM, HDIM)
    own = device[0].reshape((2,) + maps_shape)
    other = to_core(device[1]).reshape((2,) + maps_shape)
    low_maps = jax.ShapeDtypeStruct(maps_shape, BF16)
    high_maps = jax.ShapeDtypeStruct(maps_shape, F32)
    gate = unflat(project(flat(normed), w_gate, order))
    chip_m, chip_b, leaving = whole_call(
        chip_maps_kernel, [own, other], [low_maps, high_maps, low_maps], order, "chip_maps"
    )
    states_in = carried(own[0], other[0], own[1], other[1], chip_m, chip_b, leaving, 1, order)
    entering_shape = (row_count // 2, HEADS, HDIM, HDIM)
    states_in = [member.reshape(entering_shape) for member in states_in]
    branch, mixed, states, delta = mix(q, k, wu, p, col, states_in, gate, out_gain, order)
    layer_out, normed2, activated, grad_gate_up, grad_hidden, grad_attended, grad_branch = dense(
        flat(branch), flat(hidden_in), w_out, norm2_gain, w_up, w_down, flat(cotangent), order
    )
    grad_mixed, grad_gate, gain_parts, grads = adjoint(
        unflat(grad_branch), mixed, gate, out_gain, q, wu, p, m, col, order
    )
    grad_out_gain = jnp.sum(gain_parts, axis=(0, 1, 2))
    own_grad = grads[0].reshape(maps_shape)
    other_grad = to_core(grads[1]).reshape(maps_shape)
    with_other = lambda pair: (pair[0], to_core(pair[1]))
    chip_grad, leaving = whole_call(
        chip_grads_kernel,
        [own_grad, other_grad, own[0], other[0]],
        [high_maps, low_maps],
        order,
        "chip_grads",
    )
    done = {}

    def first_hop():
        done["up"] = with_other(weight_grads([normed2], [grad_gate_up], order, width=1408))

    def second_hop():
        done["others"] = with_other(
            weight_grads(
                [flat(branch), flat(normed)],
                [grad_attended[None], flat(grad_gate)[None]],
                order,
                width=512,
            )
        )

    def third_hop():
        up = done["up"]
        done["ups"] = Stream(order, [[up + (0, FF)], [up + (FF, FF)]])
        done["ups"].along_row(0)

    adjoints = carried(
        own[0], other[0], own_grad, other_grad, chip_m, chip_grad, leaving, -1, order,
        [first_hop, second_hop, third_hop],
    )
    adjoints = [member.reshape(entering_shape) for member in adjoints]
    seq = lax.axis_size("seq")
    rows = D // seq
    core = lax.axis_index("seq") % 2
    width = HEADS // 2 * HDIM
    cut = GROUPS * width // 2

    def back_part(first):
        return back(
            first, 2, projected, halo, taps, keep, col, row, mask,
            (q, k, v, t, wu, p, states, delta), grad_mixed, adjoints, order,
        )

    def fix_of(*members):
        gh = jnp.concatenate([member[1] for member in members], axis=3)
        return jnp.pad(along(gh, -1), ((0, 0), (0, 0), (8, 0), (0, 0)))

    tiles = lambda *members: [
        member[0].reshape(GROUPS, positions, member[0].shape[-1]) for member in members
    ]
    ups = done["ups"]
    first = back_part(0)
    down = local_grad(activated, flat(cotangent), order)
    down = lax.psum_scatter(down, "seq", scatter_dimension=0, tiled=True)
    ups.along_row_rest()
    second = back_part(2)
    fix_low = fix_of(first, second)
    low = with_other(weight_grads([flat(normed)], tiles(first, second), order, fix_low, cost=1.0))
    ups.finish_offloaded()
    third = back_part(4)
    low = Stream(order, [[low + (0, cut), done["others"] + (0, D)], [low + (cut, cut), done["others"] + (D, D)]])
    low.along_row(0)
    fourth = back_part(6)
    down_total = lax.psum(placed(down, order), "row").astype(F32)
    fix_high = fix_of(third, fourth)
    high = with_other(weight_grads([flat(normed)], tiles(third, fourth), order, fix_high, cost=1.0))
    low.along_row_rest()
    parts = (first, second, third, fourth)
    grad_rates, rate_sums = rates_back([member[3] for member in parts], row, a_log, order)
    small = jnp.concatenate(
        [rate_sums[:, :2].T.reshape(1, 2 * HEADS), grad_out_gain[None]], axis=1
    )
    small = Everywhere(order, jnp.pad(small, ((0, 7), (0, 256 - small.shape[1]))))
    grad_w_rates = half_product("rel,rld->ed", grad_rates[:, :24], normed)
    grad_conv = jnp.sum(jnp.concatenate([member[2] for member in parts], axis=2), axis=0)[:, :, :4]
    extra = jnp.concatenate(
        [
            jnp.moveaxis(grad_conv, 2, 0).reshape(4, seq, -1).swapaxes(0, 1).reshape(seq, -1, HDIM),
            grad_w_rates.reshape(24, seq, -1).swapaxes(0, 1).reshape(seq, -1, HDIM),
        ],
        axis=1,
    ).astype(BF16)
    extra_rows = extra.shape[1]
    extra = jnp.pad(extra, ((0, 0), (0, rows - extra_rows), (0, 0)))
    extra = extra.reshape(seq // 2, 2, rows, HDIM)
    take = lambda index: lax.dynamic_index_in_dim(extra, index, 1, keepdims=False)
    extra = with_other((take(core), take(1 - core)))
    high = Stream(order, [[high + (0, cut), extra + (0, HDIM)], [high + (cut, cut)]])
    high.along_row(0)
    grad_x = input_grad(
        tiles(*parts), jnp.concatenate([fix_low, fix_high], axis=3), w_qkv, flat(grad_gate), w_gate,
        grad_rates, w_rates, hidden_in, norm1_gain, grad_hidden, order,
    )
    small.step()
    high.along_row_rest()
    low.along_seq(0)
    small.step()
    high.along_seq(0)
    low.along_seq_rest()
    small.step()
    high.along_seq_rest()
    low.share_found()
    small.step()
    high.share_found()
    low.gather()
    small.step()
    high.gather()
    low.gather_rest()
    while small.got is not None:
        small.step()
    up_total, up_sums = final([ups.total()], [(0, 0, 2 * FF, 0)], w_up, order)
    high.gather_rest()
    low_total, high_total = low.total(), high.total()
    pieces = []
    for group in range(GROUPS):
        at = group * width
        for begin, end in ((at, min(at + width, cut)), (max(at, cut), at + width)):
            if begin < end:
                to = group * D + begin - at
                past = begin >= cut
                pieces.append((0, begin + D * past, end - begin, to))
                pieces.append((1, begin + HDIM * past, end - begin, to + width))
    qkv_total, qkv_sums = final([low_total, high_total], pieces, w_qkv, order)
    extra = high_total[:extra_rows, cut : cut + HDIM].astype(F32)
    conv_rows = GROUPS * D * 4 // (seq * HDIM)
    conv_total = extra[:conv_rows].reshape(4, -1).T
    rates_total = extra[conv_rows:].reshape(24, -1).T
    out_total = low_total[:, cut : cut + D].astype(F32)
    gate_total = low_total[:, 2 * cut + D :].astype(F32)
    small = small.value[0]
    layer_out = unflat(layer_out)
    at = lax.axis_index("seq") * rows
    mine = lambda tensor: lax.dynamic_slice_in_dim(tensor, at, rows, 0).astype(F32)
    norm1_total = (
        jnp.sum(qkv_sums, axis=1)
        + jnp.sum(gate_total * mine(w_gate), axis=1)
        + jnp.sum(rates_total * mine(w_rates), axis=1)
    ) / mine(norm1_gain)
    norm2_total = jnp.sum(up_sums, axis=1) / mine(norm2_gain)
    return (
        layer_out,
        grad_x,
        norm1_total,
        qkv_total,
        conv_total,
        rates_total,
        small[:HEADS],
        small[HEADS : 2 * HEADS],
        gate_total,
        small[2 * HEADS : 2 * HEADS + HDIM],
        out_total,
        norm2_total,
        up_total,
        down_total,
    )


def solution(mesh):
    return jax.shard_map(
        local,
        mesh=mesh,
        in_specs=(
            P("row", "seq", None),
            P("row", None),
            P(),
            P(),
            P(),
            P(),
            P(),
            P(),
            P(),
            P(),
            P(),
            P(),
            P(),
            P(),
            P("row", "seq", None),
        ),
        out_specs=(
            P("row", "seq", None),
            P("row", "seq", None),
            P("seq"),
            P("seq", None),
            P("seq", None),
            P("seq", None),
            P(),
            P(),
            P("seq", None),
            P(),
            P("seq", None),
            P("seq"),
            P("seq", None),
            P("seq", None),
        ),
        check_vma=False,
    )
```

```python
from functools import partial

import jax
import jax.numpy as jnp
from jax import lax
from jax.experimental import pallas as pl
from jax.experimental.pallas import tpu as pltpu
from jax.sharding import PartitionSpec as P

D = 1024
HEADS = 8
HDIM = 128
NH = 2
FF = 2816
CHUNK = 128
VIRT = NH * CHUNK
GROUPS = 1 + 2 * NH
PAIR = 2
QUAD = 4
HALO = 16
EPSILON = 1e-06
F32 = jnp.float32
BF16 = jnp.bfloat16
HIGHEST = lax.Precision.HIGHEST
VMEM_LIMIT = 60 * 1024 * 1024
VMEM_SMALL = 20 * 1024 * 1024
FLOPS_A_US = 1000000000
LONG = 200.0


def mm(former, latter, over=(1, 0)):
    return lax.dot_general(
        former.astype(BF16),
        latter.astype(BF16),
        (((over[0],), (over[1],)), ((), ())),
        preferred_element_type=F32,
    )


def exact_mm(former, latter):
    return jnp.dot(former, latter, precision=HIGHEST, preferred_element_type=F32)


def sigmoid(tensor):
    return 1.0 / (1.0 + jnp.exp(-tensor))


def iota2(shape, dim):
    return lax.broadcasted_iota(jnp.int32, shape, dim)


def params(*semantics, limit=VMEM_LIMIT):
    return pltpu.CompilerParams(dimension_semantics=semantics or None, vmem_limit_bytes=limit)


def pinned(kernel, inputs, pins):
    return lambda *refs: kernel(*refs[:inputs], *refs[inputs + len(pins) :])


def pin_specs(pins):
    return [pl.BlockSpec(memory_space=pl.ANY)] * len(pins)


def core_index():
    return (lax.axis_index("seq") % 2).astype(jnp.int32).reshape(1)


class Order:
    def __init__(self):
        self.last = ()

    def then(self, outputs):
        self.last = (jax.tree.leaves(outputs)[0],)
        return outputs


def call_with_core(
    kernel, grid, in_specs, out_specs, out_shape, args, scratch=(), order=None, name=None, scalar=None,
    limit=VMEM_LIMIT, cost=1.0,
):
    pins = order.last if order else ()
    outputs = pl.pallas_call(
        pinned(kernel, 1 + len(args), pins),
        grid_spec=pltpu.PrefetchScalarGridSpec(
            num_scalar_prefetch=1,
            grid=grid,
            in_specs=list(in_specs) + pin_specs(pins),
            out_specs=out_specs,
            scratch_shapes=list(scratch),
        ),
        out_shape=out_shape,
        compiler_params=params(*["arbitrary"] * len(grid), limit=limit),
        cost_estimate=pl.CostEstimate(
            flops=int(cost * FLOPS_A_US), bytes_accessed=1, transcendentals=0
        ),
        name=name,
    )(core_index() if scalar is None else scalar, *args, *pins)
    return order.then(outputs) if order else outputs


def doc_of(place, ends):
    found = sum((place >= end).astype(jnp.int32) for end in ends)
    return jnp.where(place >= 0, found, -1)


def doc_terms(anchor, ends, keep_ref, mask_ref):
    length = keep_ref.shape[1]
    place = anchor + iota2((length, HDIM), 0)
    docs = doc_of(place, ends)
    for tap in range(3):
        keep_ref[tap] = (doc_of(place - 3 + tap, ends) == docs).astype(F32)
    carry, same_last = [], []
    for chunk in range(length // CHUNK):
        at = chunk * CHUNK
        own = docs[at : at + CHUNK]
        across = doc_of(anchor + at + iota2((CHUNK, CHUNK), 1), ends)
        lower = iota2((CHUNK, CHUNK), 0) >= iota2((CHUNK, CHUNK), 1)
        mask_ref[chunk] = jnp.where((own == across) & lower, 0.0, -1e30)
        carry.append((own == doc_of(anchor + at - 1, ends)).astype(F32))
        same_last.append((own == doc_of(anchor + at + CHUNK - 1, ends)).astype(F32))
    return jnp.concatenate(carry, axis=0), jnp.concatenate(same_last, axis=0)


def front_kernel(
    scalar_ref, x_ref, halo_ref, gain_ref, w_ref, lanes_ref, w_qkv_ref,
    normed_ref, col_ref, row_ref, keep_ref, mask_ref, projected_ref, all_ref,
):
    rows, length = x_ref.shape[:2]
    count = (scalar_ref.shape[0] - 1) // rows

    def norm(x):
        x = x.astype(F32)
        scale = lax.rsqrt(jnp.mean(x * x, axis=-1, keepdims=True) + EPSILON)
        return (x * scale * gain_ref[...].astype(F32)).astype(BF16)

    @pl.when(pl.program_id(0) == 0)
    def _():
        for row in range(rows):
            normed = norm(x_ref[row])
            normed_ref[row] = normed
            all_ref[row * length : (row + 1) * length] = normed
            at = rows * length + row * HALO
            all_ref[at : at + HALO] = norm(halo_ref[row])
            ends, end = [], 0
            for place in range(count):
                end = end + scalar_ref[1 + row * count + place]
                ends.append(end)
            flags = doc_terms(scalar_ref[0], ends, keep_ref.at[row], mask_ref.at[row])
            packed = rate_terms(normed, w_ref, lanes_ref, flags)
            col_ref[row] = packed
            row_ref[row] = packed.T

    projected_ref[...] = jnp.dot(
        all_ref[...], w_qkv_ref[...], preferred_element_type=F32
    ).astype(BF16)


def rate_terms(normed, w_ref, lanes_ref, flags):
    length = normed.shape[0]
    rates = jnp.dot(normed, w_ref[...], preferred_element_type=F32)
    shifted = rates + lanes_ref[1:2]
    soft = jnp.maximum(shifted, 0.0) + jnp.log(1.0 + jnp.exp(-jnp.abs(shifted)))
    log_decay = lanes_ref[0:1] * soft
    shape = (length, length)
    here, there = iota2(shape, 0), iota2(shape, 1)
    lower = ((here >= there) & (here // CHUNK == there // CHUNK)).astype(F32)
    summed = exact_mm(lower, log_decay)
    last = jnp.concatenate(
        [
            jnp.broadcast_to(summed[at + CHUNK - 1 : at + CHUNK], (CHUNK, HDIM))
            for at in range(0, length, CHUNK)
        ],
        axis=0,
    )
    start = jnp.exp(summed) * flags[0]
    tail = jnp.exp(last - summed) * flags[1]
    lane = iota2((length, HDIM), 1)
    packed = jnp.zeros((length, HDIM), F32)
    for limit, member, shift in (
        (56, log_decay, 32),
        (48, sigmoid(shifted), 24),
        (40, tail, 16),
        (32, start, 8),
        (24, summed, 0),
        (16, sigmoid(rates), 0),
    ):
        member = pltpu.roll(member, shift, 1) if shift else member
        packed = jnp.where(lane < limit, member, packed)
    return packed


def front(hidden_in, halo, lengths, gain, w_rates, a_log, dt_bias, w_qkv, order, tile=512):
    rows, length = hidden_in.shape[:2]
    w_padded = jnp.pad(w_rates, ((0, 0), (0, HDIM - w_rates.shape[1])))
    first = NH * HEADS
    lanes = jnp.pad(
        jnp.stack([-jnp.exp(a_log), dt_bias]), ((0, 0), (first, HDIM - first - HEADS))
    )
    anchor = (lax.axis_index("seq") * length).astype(jnp.int32).reshape(1)
    count = rows * (length + HALO)
    chunks = length // CHUNK
    full = lambda *shape: pl.BlockSpec(shape, lambda t, c: (0,) * len(shape))
    return call_with_core(
        front_kernel,
        (w_qkv.shape[1] // tile,),
        [
            full(rows, length, D),
            full(rows, HALO, D),
            full(1, D),
            full(D, HDIM),
            full(2, HDIM),
            pl.BlockSpec((D, tile), lambda t, c: (0, t)),
        ],
        [
            full(rows, length, D),
            full(rows, length, HDIM),
            full(rows, HDIM, length),
            full(rows, 3, length, HDIM),
            full(rows, chunks, CHUNK, CHUNK),
            pl.BlockSpec((count, tile), lambda t, c: (0, t)),
        ],
        [
            jax.ShapeDtypeStruct((rows, length, D), BF16),
            jax.ShapeDtypeStruct((rows, length, HDIM), F32),
            jax.ShapeDtypeStruct((rows, HDIM, length), F32),
            jax.ShapeDtypeStruct((rows, 3, length, HDIM), F32),
            jax.ShapeDtypeStruct((rows, chunks, CHUNK, CHUNK), F32),
            jax.ShapeDtypeStruct((count, w_qkv.shape[1]), BF16),
        ],
        [hidden_in, halo, gain[None], w_padded, lanes, w_qkv],
        [pltpu.VMEM((count, D), BF16)],
        order,
        name="front",
        cost=10.0,
        scalar=jnp.concatenate([anchor, lengths.reshape(-1)]),
    )


def convolved(x_ref, halo_ref, taps_ref, keep_ref, ext_ref, lanes):
    length = x_ref.shape[0]
    ext_ref[0:8] = halo_ref[:, lanes].astype(F32)[HALO - 8 :]
    x = x_ref[:, lanes].astype(F32)
    ext_ref[8 : 8 + length] = x
    summed = x * taps_ref[3:4, lanes]
    for tap in range(3):
        summed = summed + ext_ref[5 + tap : 5 + tap + length] * keep_ref[0, tap] * taps_ref[
            tap : tap + 1, lanes
        ]
    return summed


def head_columns(col_ref, head):
    return pltpu.roll(col_ref[0], (HDIM - head) % HDIM, 1)


def lane_sums(tensor):
    return mm(tensor, jnp.ones((HDIM, HDIM), BF16))


def split(tensor):
    high = tensor.astype(BF16)
    return jnp.concatenate([high, (tensor - high.astype(F32)).astype(BF16)], axis=1)


def row_sums(tensor):
    return mm(jnp.ones((8, 2 * HDIM), BF16), split(tensor), (1, 1))[0:1]


def column_sums(tensor):
    total = mm(jnp.ones((8, tensor.shape[0]), BF16), split(tensor))
    return total[0:1, :HDIM] + total[0:1, HDIM:]


def wide(column):
    return jnp.broadcast_to(column, (column.shape[0], HDIM))


def pick(row_ref, place, head, at):
    own = iota2((HEADS, CHUNK), 0) == head
    rows = row_ref[0, place * HEADS : place * HEADS + HEADS, at : at + CHUNK]
    return jnp.sum(jnp.where(own, rows, 0.0), axis=0, keepdims=True)


def lanes_of(sub):
    return slice(sub * HDIM, sub * HDIM + HDIM)


def in_turns(makers):
    running = list(makers)
    while running:
        running = [member for member in running if next(member, "end") != "end"]


def both(tensor):
    return jnp.concatenate([tensor, tensor], axis=0)


def decay_matrix(cols, row_ref, mask_ref, head, chunk):
    at = chunk * CHUNK
    across = pick(row_ref, 2, head, at)
    down = cols[at : at + CHUNK, 16:17]
    return jnp.exp(down - across + mask_ref[0, chunk])


def maps_kernel(core_ref, *refs):
    xs, halos, taps = refs[0:5], refs[5:10], refs[10:15]
    keep_ref, col_ref, row_ref, mask_ref, level_ref = refs[15:20]
    q_ref, k_ref, v_ref, t_ref, wu_ref, p_ref, m_ref, dev_ref, ext_ref = refs[20:]
    length = xs[0].shape[0]
    chunks = length // CHUNK
    eye = (iota2((HDIM, HDIM), 0) == iota2((HDIM, HDIM), 1)).astype(F32)
    eye_wide = (iota2((VIRT, VIRT), 0) == iota2((VIRT, VIRT), 1)).astype(BF16)
    heads = q_ref.shape[1]
    data = []
    for sub in range(heads):
        head = heads * pl.program_id(1) + sub
        cols = head_columns(col_ref, head)
        parts = []
        for group in range(GROUPS):
            summed = convolved(
                xs[group], halos[group], taps[group], keep_ref, ext_ref.at[group], lanes_of(sub)
            )
            active = summed * sigmoid(summed)
            if group < 1 + NH:
                active = active * lax.rsqrt(lane_sums(active * active) + EPSILON)
            parts.append(active.astype(BF16))
        q_ref[0, sub] = parts[0]
        for chunk in range(chunks):
            at = chunk * CHUNK
            rows = slice(at, at + CHUNK)
            query = parts[0][rows]
            keys = jnp.concatenate([parts[1][rows], parts[2][rows]], axis=0)
            values = jnp.concatenate([parts[3][rows], parts[4][rows]], axis=0)
            k_ref[0, sub, chunk] = keys
            v_ref[0, sub, chunk] = values
            decay = decay_matrix(cols, row_ref, mask_ref, head, chunk)
            wide_decay = jnp.concatenate([decay, decay], axis=1)
            beta = jnp.concatenate([wide(cols[rows, 0:1]), wide(cols[rows, 8:9])], axis=0)
            beta_wide = jnp.concatenate([beta, beta], axis=1)
            mixing = (mm(keys, keys, (1, 1)) * both(wide_decay) * beta_wide).astype(BF16)
            p_ref[0, sub, chunk] = (mm(query, keys, (1, 1)) * wide_decay).astype(BF16)
            inverse = eye_wide - mixing * level_ref[0]
            data.append((keys, values, beta, mixing, inverse, cols[rows]))
    for step in range(1, 8):
        mids = [mm(member[3] * level_ref[step], member[4]) for member in data]
        data = [
            member[:4] + (member[4] - mm(member[4], mid).astype(BF16),) + member[5:]
            for member, mid in zip(data, mids)
        ]
    device = [None] * heads
    for chunk in range(chunks):
        for sub in range(heads):
            keys, values, beta, mixing, inverse, cols = data[sub * chunks + chunk]
            t_ref[0, sub, chunk] = inverse
            keys_float = keys.astype(F32)
            right = jnp.concatenate(
                [keys_float * (both(wide(cols[:, 24:25])) * beta), values.astype(F32) * beta], axis=1
            )
            solved = mm(inverse, right).astype(BF16)
            wu_ref[0, sub, chunk] = solved
            tail_keys = keys_float * both(wide(cols[:, 32:33]))
            pair = mm(solved, tail_keys, (0, 0))
            block_m = cols[CHUNK - 1 : CHUNK, 24:25] * eye - pair[:HDIM]
            block_b = pair[HDIM:]
            m_ref[0, sub, chunk] = block_m.astype(BF16)
            if chunk == 0:
                device[sub] = (block_m, block_b)
            else:
                chained = mm(jnp.concatenate(device[sub], axis=0), block_m)
                device[sub] = (chained[:HDIM], chained[HDIM:] + block_b)
    for sub in range(heads):
        dev_ref[0, 0, 0, sub] = device[sub][0].astype(BF16)
        dev_ref[0, 1, 0, sub] = device[sub][1].astype(BF16)


def group_specs(block, index, first, pair):
    return [
        pl.BlockSpec(
            block + (pair * HDIM,),
            partial(lambda g, r, h, *_: index(r, (g * HEADS + first) // pair + h), g),
        )
        for g in range(GROUPS)
    ]


def head_spec(*block, first=0, pair=PAIR):
    return pl.BlockSpec(
        (1, pair) + block, lambda r, h, *_: (r, first // pair + h) + (0,) * len(block)
    )


def conv_specs(rows, length, first=0, pair=PAIR):
    return (
        group_specs((length,), lambda r, c: (r, c), first, pair)
        + group_specs((HALO,), lambda r, c: (rows * length // HALO + r, c), first, pair)
        + group_specs((4,), lambda r, c: (0, c), first, pair)
        + [pl.BlockSpec((1, 3, length, HDIM), lambda r, h, *_: (r, 0, 0, 0))]
    )


def rate_specs(length):
    return [
        pl.BlockSpec((1, length, HDIM), lambda r, h, *_: (r, 0, 0)),
        pl.BlockSpec((1, HDIM, length), lambda r, h, *_: (r, 0, 0)),
        pl.BlockSpec((1, length // CHUNK, CHUNK, CHUNK), lambda r, h, *_: (r, 0, 0, 0)),
    ]


def levels():
    place = jnp.arange(VIRT)
    place = NH * (place % CHUNK) + place // CHUNK
    differ = place[:, None] ^ place[None, :]
    level = sum((differ >= (1 << bit)).astype(jnp.int32) for bit in range(1, 8))
    level = jnp.where(place[:, None] > place[None, :], level, -1)
    return (level[None] == jnp.arange(8)[:, None, None]).astype(BF16)


def slot_spec(rows, *lead, pair=PAIR):
    half = rows // 2
    return pl.BlockSpec(
        (1,) + lead + (1, pair, HDIM, HDIM),
        lambda r, h, core: ((r // half) ^ core[0],) + (0,) * len(lead) + (r % half, h, 0, 0),
    )


def maps(projected, taps, keep, col, row, mask, level, order):
    rows, length = col.shape[:2]
    spec = partial(head_spec, pair=QUAD)
    chunks = length // CHUNK
    shape = lambda *tail: jax.ShapeDtypeStruct((rows, HEADS) + tail, BF16)
    masks = pl.BlockSpec((8, VIRT, VIRT), lambda r, h, *_: (0, 0, 0))
    return call_with_core(
        maps_kernel,
        (rows, HEADS // QUAD),
        conv_specs(rows, length, pair=QUAD) + rate_specs(length) + [masks],
        [
            spec(length, HDIM),
            spec(chunks, VIRT, HDIM),
            spec(chunks, VIRT, HDIM),
            spec(chunks, VIRT, VIRT),
            spec(chunks, VIRT, VIRT),
            spec(chunks, CHUNK, VIRT),
            spec(chunks, HDIM, HDIM),
            slot_spec(rows, 2, pair=QUAD),
        ],
        [
            shape(length, HDIM),
            shape(chunks, VIRT, HDIM),
            shape(chunks, VIRT, HDIM),
            shape(chunks, VIRT, VIRT),
            shape(chunks, VIRT, VIRT),
            shape(chunks, CHUNK, VIRT),
            shape(chunks, HDIM, HDIM),
            jax.ShapeDtypeStruct((2, 2, rows // 2, HEADS, HDIM, HDIM), BF16),
        ],
        [projected] * 10 + [taps] * 5 + [keep, col, row, mask, level],
        [pltpu.VMEM((GROUPS, length + 8, HDIM), F32)],
        order,
        name="maps",
        cost=40.0,
    )


def entering_spec(rows, first=0, pair=PAIR):
    half = rows // 2
    return pl.BlockSpec(
        (1, pair, HDIM, HDIM), lambda r, h, *_: (r % half, first // pair + h, 0, 0)
    )


def entering_state(core_ref, own_ref, other_ref, sub, rows):
    mine = pl.program_id(0) // (rows // 2) == core_ref[0]
    return jnp.where(mine, own_ref[0, sub].astype(F32), other_ref[0, sub].astype(F32))


def mixed_kernel(
    row_count, core_ref, q_ref, k_ref, wu_ref, p_ref, col_ref, own_ref, other_ref, gate_ref, gain_ref,
    branch_ref, mixed_ref, states_ref, delta_ref,
):
    heads, chunks = k_ref.shape[1:3]

    def one(sub):
        cols = head_columns(col_ref, heads * pl.program_id(1) + sub)
        state = entering_state(core_ref, own_ref, other_ref, sub, row_count)
        outputs = []
        for chunk in range(chunks):
            at = chunk * CHUNK
            rows = slice(at, at + CHUNK)
            solved = wu_ref[0, sub, chunk]
            states_ref[0, sub, chunk] = state.astype(BF16)
            seen = mm(
                jnp.concatenate([solved[:, :HDIM], q_ref[0, sub, rows]], axis=0), state, (1, 1)
            )
            yield
            delta = (solved[:, HDIM:].astype(F32) - seen[:VIRT]).astype(BF16)
            delta_ref[0, sub, chunk] = delta
            if chunk + 1 < chunks:
                tail_keys = k_ref[0, sub, chunk].astype(F32) * both(cols[rows, 32:33])
                state = cols[at + CHUNK - 1 : at + CHUNK, 24:25] * state + mm(
                    delta, tail_keys, (0, 0)
                )
            outputs.append(cols[rows, 24:25] * seen[VIRT:] + mm(p_ref[0, sub, chunk], delta))
            yield
        mixed = jnp.concatenate(outputs, axis=0)
        mixed_ref[0, :, lanes_of(sub)] = mixed
        scale = lax.rsqrt(lane_sums(mixed * mixed) * (1.0 / HDIM) + EPSILON)
        gate = gate_ref[0, :, lanes_of(sub)].astype(F32)
        branch_ref[0, :, lanes_of(sub)] = (
            mixed * scale * gain_ref[...].astype(F32) * (gate * sigmoid(gate))
        ).astype(BF16)

    in_turns([one(sub) for sub in range(heads)])


def column_spec(length, first=0, pair=PAIR):
    return pl.BlockSpec((1, length, pair * HDIM), lambda r, h, *_: (r, 0, first // pair + h))


def mix(q, k, wu, p, col, states_in, gate, gain, order):
    rows, _, length = q.shape[:3]
    spec = partial(head_spec, pair=QUAD)
    chunks = length // CHUNK
    return call_with_core(
        partial(mixed_kernel, rows),
        (rows, HEADS // QUAD),
        [
            spec(length, HDIM),
            spec(chunks, VIRT, HDIM),
            spec(chunks, VIRT, VIRT),
            spec(chunks, CHUNK, VIRT),
            rate_specs(length)[0],
            entering_spec(rows, pair=QUAD),
            entering_spec(rows, pair=QUAD),
            column_spec(length, pair=QUAD),
            pl.BlockSpec((1, HDIM), lambda r, h, *_: (0, 0)),
        ],
        [
            column_spec(length, pair=QUAD),
            column_spec(length, pair=QUAD),
            spec(chunks, HDIM, HDIM),
            spec(chunks, VIRT, HDIM),
        ],
        [
            jax.ShapeDtypeStruct((rows, length, D), BF16),
            jax.ShapeDtypeStruct((rows, length, D), F32),
            jax.ShapeDtypeStruct((rows, HEADS, chunks, HDIM, HDIM), BF16),
            jax.ShapeDtypeStruct((rows, HEADS, chunks, VIRT, HDIM), BF16),
        ],
        [q, k, wu, p, col, *states_in, gate, gain[None]],
        order=order,
        name="mix",
        cost=11.0,
    )


def adjoint_kernel(
    core_ref, up_ref, mixed_ref, gate_ref, gain_ref, q_ref, wu_ref, p_ref, m_ref, col_ref,
    grad_mixed_ref, grad_gate_ref, grad_gain_ref, own_ref,
):
    heads, chunks = p_ref.shape[1:3]

    def one(sub):
        lanes = lanes_of(sub)
        cols = head_columns(col_ref, heads * pl.program_id(1) + sub)
        upstream, mixed, gate = (
            ref[0, :, lanes].astype(F32) for ref in (up_ref, mixed_ref, gate_ref)
        )
        gain = gain_ref[...].astype(F32)
        sig = sigmoid(gate)
        scale = lax.rsqrt(lane_sums(mixed * mixed) * (1.0 / HDIM) + EPSILON)
        unit = mixed * scale
        grad_gate_ref[0, :, lanes] = (
            upstream * unit * gain * (sig * (1.0 + gate * (1.0 - sig)))
        ).astype(BF16)
        upstream = upstream * (gate * sig)
        partial_gain = upstream * unit
        grad_gain_ref[0, sub] = jnp.sum(
            partial_gain.reshape(partial_gain.shape[0] // 8, 8, HDIM), axis=0
        )
        weighted = gain * upstream
        grad_mixed = scale * (weighted - unit * (lane_sums(unit * weighted) * (1.0 / HDIM)))
        low = grad_mixed.astype(BF16)
        grad_mixed_ref[0, :, lanes] = low
        yield
        grad_state = None
        for chunk in reversed(range(chunks)):
            at = chunk * CHUNK
            rows = slice(at, at + CHUNK)
            own_delta = mm(p_ref[0, sub, chunk], low[rows], (0, 0))
            yield
            left = jnp.concatenate(
                [(grad_mixed[rows] * cols[rows, 24:25]).astype(BF16), (-own_delta).astype(BF16)],
                axis=0,
            )
            right = jnp.concatenate([q_ref[0, sub, rows], wu_ref[0, sub, chunk, :, :HDIM]], axis=0)
            own = mm(left, right, (0, 0))
            if grad_state is not None:
                own = own + mm(grad_state, m_ref[0, sub, chunk], (1, 1))
            grad_state = own
            yield
        own_ref[0, 0, sub] = grad_state.astype(BF16)

    in_turns([one(sub) for sub in range(heads)])


def adjoint(upstream, mixed, gate, gain, q, wu, p, m, col, order):
    rows, _, length = q.shape[:3]
    spec = partial(head_spec, pair=QUAD)
    chunks = length // CHUNK
    return call_with_core(
        adjoint_kernel,
        (rows, HEADS // QUAD),
        [
            column_spec(length, pair=QUAD),
            column_spec(length, pair=QUAD),
            column_spec(length, pair=QUAD),
            pl.BlockSpec((1, HDIM), lambda r, h, *_: (0, 0)),
            spec(length, HDIM),
            spec(chunks, VIRT, VIRT),
            spec(chunks, CHUNK, VIRT),
            spec(chunks, HDIM, HDIM),
            rate_specs(length)[0],
        ],
        [
            column_spec(length, pair=QUAD),
            column_spec(length, pair=QUAD),
            spec(8, HDIM),
            slot_spec(rows, pair=QUAD),
        ],
        [
            jax.ShapeDtypeStruct((rows, length, D), BF16),
            jax.ShapeDtypeStruct((rows, length, D), BF16),
            jax.ShapeDtypeStruct((rows, HEADS, 8, HDIM), F32),
            jax.ShapeDtypeStruct((2, rows // 2, HEADS, HDIM, HDIM), BF16),
        ],
        [upstream, mixed, gate, gain[None], q, wu, p, m, col],
        order=order,
        name="adjoint",
        cost=11.0,
    )


def before(count, dim):
    place = iota2((count, count), dim)
    return NH * (place % CHUNK) + place // CHUNK


def back_kernel(first, rows, core_ref, *refs):
    xs, halos, taps = refs[0:5], refs[5:10], refs[10:15]
    keep_ref, col_ref, row_ref, mask_ref = refs[15:19]
    q_ref, shift_ref = refs[19], refs[-1]
    length = xs[0].shape[0]
    chunks = length // CHUNK
    heads = q_ref.shape[1]
    stats_ref = refs[-3]

    @pl.when(pl.program_id(1) == 0)
    def _():
        stats_ref[...] = jnp.zeros_like(stats_ref)

    strict = (before(VIRT, 0) > before(VIRT, 1)).astype(F32)
    for tap in range(3):
        shift_ref[tap, 0:8] = jnp.zeros((8, HDIM), F32)
        shift_ref[tap, 8 + length : 16 + length] = jnp.zeros((8, HDIM), F32)
    in_turns(
        [
            back_head(
                first, rows, core_ref, sub, heads, xs, halos, taps, keep_ref, col_ref, row_ref, mask_ref, strict, refs[19:],
            )
            for sub in range(heads)
        ]
    )


def back_head(
    first, row_count, core_ref, sub, heads, xs, halos, taps, keep_ref, col_ref, row_ref, mask_ref,
    strict, refs,
):
    q_ref, k_ref, v_ref, t_ref, wu_ref, p_ref, states_ref, delta_ref = refs[:8]
    grad_mixed_ref, own_ref, other_ref = refs[8:11]
    gp_ref, gh_ref, gw_ref, stats_ref, ext_ref, shift_ref = refs[11:]
    length = xs[0].shape[0]
    chunks = length // CHUNK
    head = first + heads * pl.program_id(1) + sub
    lanes = lanes_of(sub)
    cols = head_columns(col_ref, head)
    own_row = iota2((HEADS, CHUNK), 0) == head
    grad_next = entering_state(core_ref, own_ref, other_ref, sub, row_count)
    grads = [[None] * chunks for _ in range(GROUPS)]
    for chunk in reversed(range(chunks)):
        at = chunk * CHUNK
        rows = slice(at, at + CHUNK)
        query = q_ref[0, sub, rows]
        query_float = query.astype(F32)
        keys, values = k_ref[0, sub, chunk], v_ref[0, sub, chunk]
        keys_float, values_float = keys.astype(F32), values.astype(F32)
        solved, scores = wu_ref[0, sub, chunk], p_ref[0, sub, chunk]
        state, delta = states_ref[0, sub, chunk], delta_ref[0, sub, chunk]
        grad_out = grad_mixed_ref[0, rows, lanes]
        beta = jnp.concatenate([wide(cols[rows, 0:1]), wide(cols[rows, 8:9])], axis=0)
        beta_wide = jnp.concatenate([beta, beta], axis=1)
        start, tail = wide(cols[rows, 24:25]), wide(cols[rows, 32:33])
        start_wide, tail_wide = both(start), both(tail)
        end = cols[at + CHUNK - 1 : at + CHUNK, 24:25]
        decay = decay_matrix(cols, row_ref, mask_ref, head, chunk)
        wide_decay = jnp.concatenate([decay, decay], axis=1)
        full_decay = both(wide_decay) * strict
        next_low = grad_next.astype(BF16)
        tail_keys = (keys_float * tail_wide).astype(BF16)
        grad_delta = mm(scores, grad_out, (0, 0)) + mm(tail_keys, next_low, (1, 1))
        delta_low = grad_delta.astype(BF16)
        grad_scores = mm(grad_out, delta, (1, 1))
        weighted_scores = grad_scores * scores.astype(F32)
        grad_raw = (grad_scores * wide_decay).astype(BF16)
        yield
        seen = mm(jnp.concatenate([grad_out, delta_low], axis=0), state)
        grad_query = start * seen[:CHUNK] + mm(grad_raw, keys)
        by_start = seen[:CHUNK] * query_float
        grad_wide = jnp.concatenate([-seen[CHUNK:], grad_delta], axis=1).astype(BF16)
        grad_end = jnp.sum(
            jnp.sum(grad_next * state.astype(F32), axis=0, keepdims=True), axis=1, keepdims=True
        )
        grad_tail_keys = mm(delta, next_low)
        left = jnp.concatenate(
            [(grad_out.astype(F32) * start).astype(BF16), (-grad_delta).astype(BF16)], axis=0
        )
        grad_next = end * grad_next + mm(
            left, jnp.concatenate([query, solved[:, :HDIM]], axis=0), (0, 0)
        )
        yield
        grad_right = mm(t_ref[0, sub, chunk], grad_wide, (0, 0))
        yield
        right_keys, right_values = grad_right[:, :HDIM], grad_right[:, HDIM:]
        grad_mixing = -mm(grad_right, solved, (1, 1))
        gram = mm(keys, keys, (1, 1))
        decayed = grad_mixing * full_decay
        weighted = decayed * gram
        grad_gram = (decayed * beta_wide).astype(BF16)
        yield
        by_keys = keys_float * right_keys
        by_values = values_float * right_values
        by_mixing = weighted[:, :CHUNK] + weighted[:, CHUNK:]
        grad_keys = (
            (start_wide * beta) * right_keys
            + tail_wide * grad_tail_keys
            + mm(grad_raw, query, (0, 0))
            + mm(grad_gram, keys)
            + mm(grad_gram, keys, (0, 0))
        )
        grad_values = beta * right_values
        fold = lambda tensor: tensor[:CHUNK] + tensor[CHUNK:]
        pairs = fold(beta * by_mixing) + weighted_scores[:, :CHUNK] + weighted_scores[:, CHUNK:]
        by_tail = fold(keys_float * grad_tail_keys) * tail
        by_log = pairs + (by_start + fold(beta * by_keys)) * start
        by_beta = start_wide * by_keys + by_values + by_mixing
        sums = row_sums(jnp.concatenate([by_beta, by_log, by_tail], axis=0))
        tail_sums = sums[:, 3 * CHUNK :]
        at_end = jnp.sum(tail_sums, axis=1, keepdims=True) + grad_end * end
        last = iota2((1, CHUNK), 1) == CHUNK - 1
        log_sums = sums[:, 2 * CHUNK : 3 * CHUNK] - tail_sums - column_sums(pairs)
        log_sums = log_sums + jnp.where(last, at_end, 0.0)
        for place, member in enumerate((sums[:, :CHUNK], sums[:, CHUNK : 2 * CHUNK], log_sums)):
            spot = slice(place * HEADS, place * HEADS + HEADS)
            stats_ref[0, spot, rows] = jnp.where(own_row, member, stats_ref[0, spot, rows])
        for group, member in enumerate(
            (grad_query, grad_keys[:CHUNK], grad_keys[CHUNK:], grad_values[:CHUNK], grad_values[CHUNK:])
        ):
            grads[group][chunk] = member
        yield
    for group in range(GROUPS):
        ext = ext_ref.at[group]
        summed = convolved(xs[group], halos[group], taps[group], keep_ref, ext, lanes)
        sig = sigmoid(summed)
        active = summed * sig
        grad = jnp.concatenate(grads[group], axis=0).astype(BF16).astype(F32)
        if group < 1 + NH:
            scale = lax.rsqrt(lane_sums(active * active) + EPSILON)
            unit = active * scale
            grad = scale * (grad - unit * lane_sums(unit * grad))
        grad = grad * (sig * (1.0 + summed * (1.0 - sig)))
        total = grad * taps[group][3:4, lanes]
        before = None
        weight_rows = []
        for tap in range(3):
            kept = grad * keep_ref[0, tap]
            weight_rows.append(
                jnp.sum(kept * ext[5 + tap : 5 + tap + length], axis=0, keepdims=True)
            )
            shift_ref[tap, 8 : 8 + length] = kept * taps[group][tap : tap + 1, lanes]
            total = total + shift_ref[tap, 11 - tap : 11 - tap + length]
            early = shift_ref[tap, 3 - tap : 11 - tap]
            before = early if before is None else before + early
        weight_rows.append(
            jnp.sum(grad * ext[8 : 8 + length], axis=0, keepdims=True)
        )
        gp_ref[group, 0, :, lanes] = total.astype(BF16)
        gh_ref[group, 0, :, lanes] = before.astype(BF16)
        gw_ref[0, group, sub] = jnp.concatenate(
            weight_rows + [jnp.zeros((4, HDIM), F32)], axis=0
        )


def back(first, count, projected, taps, keep, col, row, mask, saved, grad_mixed, adjoints, order):
    rows, length = col.shape[:2]
    chunks = length // CHUNK
    spec = partial(head_spec, first=first)
    return call_with_core(
        partial(back_kernel, first, rows),
        (rows, count // PAIR),
        conv_specs(rows, length, first)
        + rate_specs(length)
        + [
            spec(length, HDIM),
            spec(chunks, VIRT, HDIM),
            spec(chunks, VIRT, HDIM),
            spec(chunks, VIRT, VIRT),
            spec(chunks, VIRT, VIRT),
            spec(chunks, CHUNK, VIRT),
            spec(chunks, HDIM, HDIM),
            spec(chunks, VIRT, HDIM),
            column_spec(length, first),
            entering_spec(rows, first),
            entering_spec(rows, first),
        ],
        [
            pl.BlockSpec((GROUPS, 1, length, PAIR * HDIM), lambda r, h, *_: (0, r, 0, h)),
            pl.BlockSpec((GROUPS, 1, 8, PAIR * HDIM), lambda r, h, *_: (0, r, 0, h)),
            pl.BlockSpec((1, GROUPS, PAIR, 8, HDIM), lambda r, h, *_: (r, 0, h, 0, 0)),
            pl.BlockSpec((1, 24, length), lambda r, h, *_: (r, 0, 0)),
        ],
        [
            jax.ShapeDtypeStruct((GROUPS, rows, length, count * HDIM), BF16),
            jax.ShapeDtypeStruct((GROUPS, rows, 8, count * HDIM), BF16),
            jax.ShapeDtypeStruct((rows, GROUPS, count, 8, HDIM), F32),
            jax.ShapeDtypeStruct((rows, 24, length), F32),
        ],
        [projected] * 10 + [taps] * 5
        + [keep, col, row, mask, *saved, grad_mixed, *adjoints],
        [
            pltpu.VMEM((GROUPS, length + 8, HDIM), F32),
            pltpu.VMEM((3, length + 16, HDIM), F32),
        ],
        order,
        name="back",
        cost=LONG,
    )


def rates_kernel(core_ref, *refs):
    row_ref, nega_ref, rates_ref, sums_ref = refs[-4:]
    rows, _, length = row_ref.shape
    shape = (length, length)
    here, there = iota2(shape, 0), iota2(shape, 1)
    lower = ((here >= there) & (here // CHUNK == there // CHUNK)).astype(F32)
    lane = iota2((HEADS, HDIM), 1)
    total = jnp.zeros((HEADS, HDIM), F32)
    for r in range(rows):
        beta = row_ref[r, 0:16]
        stats = sum(ref[r] for ref in refs[:-4])
        grad_log = exact_mm(stats[16:24], lower)
        grad_bias = grad_log * nega_ref[:, 0:1] * row_ref[r, 40:48]
        rates_ref[r, 0:16] = (stats[0:16] * beta * (1.0 - beta)).astype(BF16)
        rates_ref[r, 16:24] = grad_bias.astype(BF16)
        rates_ref[r, 24:32] = jnp.zeros((8, length), BF16)
        by_log = jnp.sum(grad_log * row_ref[r, 48:56], axis=1, keepdims=True)
        by_bias = jnp.sum(grad_bias, axis=1, keepdims=True)
        total = total + jnp.where(lane == 0, by_log, jnp.where(lane == 1, by_bias, 0.0))
    sums_ref[...] = total


def rates_back(stats, row, a_log, order):
    rows, _, length = stats[0].shape
    nega = jnp.broadcast_to(-jnp.exp(a_log)[:, None], (HEADS, HDIM))
    return whole_call(
        rates_kernel,
        [*stats, row, nega],
        [
            jax.ShapeDtypeStruct((rows, 32, length), BF16),
            jax.ShapeDtypeStruct((HEADS, HDIM), F32),
        ],
        order,
        "rates_back",
        LONG,
    )


def to_core(value):
    count = lax.axis_size("seq")
    return lax.ppermute(value, "seq", [(at, at ^ 1) for at in range(count)])


def to_chip(value, step):
    count = lax.axis_size("seq")
    pairs = [(at, at + 2 * step) for at in range(count) if 0 <= at + 2 * step < count]
    return lax.ppermute(value, "seq", pairs)


def along(value, step):
    count = lax.axis_size("seq")
    pairs = [(at, at + step) for at in range(count) if 0 <= at + step < count]
    return lax.ppermute(value, "seq", pairs)


def whole_call(kernel, args, out_shape, order, name, cost=1.0):
    return call_with_core(
        kernel,
        (1,),
        [pl.BlockSpec(arg.shape, lambda t, c, n=arg.ndim: (0,) * n) for arg in args],
        [pl.BlockSpec(out.shape, lambda t, c, n=len(out.shape): (0,) * n) for out in out_shape],
        out_shape,
        args,
        order=order,
        name=name,
        limit=VMEM_SMALL,
        cost=cost,
    )


def chip_maps_kernel(core_ref, device_ref, other_ref, m_ref, b_ref, leaving_ref):
    own_first = core_ref[0] == 0
    for at in range(m_ref.shape[0]):
        own_m, own_b = (device_ref[0, place, at].astype(F32) for place in range(2))
        other_m, other_b = (other_ref[1, place, at].astype(F32) for place in range(2))
        first = jnp.concatenate(
            [jnp.where(own_first, own_m, other_m), jnp.where(own_first, own_b, other_b)], axis=0
        )
        second_m = jnp.where(own_first, other_m, own_m)
        second_b = jnp.where(own_first, other_b, own_b)
        both_maps = mm(first, second_m)
        m_ref[at] = both_maps[:HDIM].astype(BF16)
        total = both_maps[HDIM:] + second_b
        b_ref[at] = total
        leaving_ref[at] = total.astype(BF16)


def chip_grads_kernel(core_ref, own_ref, other_ref, device_ref, other_map_ref, b_ref, leaving_ref):
    own_first = core_ref[0] == 1
    for at in range(b_ref.shape[0]):
        own, other = own_ref[0, at].astype(F32), other_ref[1, at].astype(F32)
        own_m, other_m = device_ref[0, 0, at].astype(F32), other_map_ref[1, 0, at].astype(F32)
        first = jnp.where(own_first, own, other)
        second = jnp.where(own_first, other, own)
        second_m = jnp.where(own_first, other_m, own_m)
        total = mm(first, second_m, (1, 1)) + second
        b_ref[at] = total
        leaving_ref[at] = total.astype(BF16)


def hop_kernel(over, core_ref, entering_ref, m_ref, b_ref, leaving_ref):
    for at in range(entering_ref.shape[0]):
        leaving_ref[at] = (mm(entering_ref[at], m_ref[at], over) + b_ref[at]).astype(BF16)


def last_kernel(over, first_core, core_ref, entering_ref, device_ref, other_ref, *refs):
    own_b, other_b = (refs[0], refs[1]) if len(refs) == 4 else (None, None)
    keep_ref, give_ref = refs[-2:]
    own_first = core_ref[0] == first_core
    for at in range(entering_ref.shape[0]):
        entering = entering_ref[at].astype(F32)
        first_m = jnp.where(
            own_first, device_ref[0, 0, at].astype(F32), other_ref[1, 0, at].astype(F32)
        )
        own = device_ref[0, 1, at] if own_b is None else own_b[0, at]
        other = other_ref[1, 1, at] if other_b is None else other_b[1, at]
        first_b = jnp.where(own_first, own.astype(F32), other.astype(F32))
        between = mm(entering, first_m, over) + first_b
        keep_ref[at] = jnp.where(own_first, entering, between).astype(BF16)
        give_ref[at] = jnp.where(own_first, between, entering).astype(BF16)


def carried(device, other, grads, chip_m, chip_b, leaving, step, order, meanwhile=()):
    over, first_core = ((1, 0), 0) if step > 0 else ((1, 1), 1)
    low = jax.ShapeDtypeStruct(leaving.shape, BF16)
    hops = lax.axis_size("seq") // 2 - 1
    for at in range(hops):
        entering = to_chip(leaving, step)
        if at < len(meanwhile):
            meanwhile[at]()
        if at + 1 < hops:
            (leaving,) = whole_call(
                partial(hop_kernel, over), [entering, chip_m, chip_b], [low], order, "hop"
            )
    keep, give = whole_call(
        partial(last_kernel, over, first_core),
        [entering, device, other, *grads],
        [low, low],
        order,
        "entering",
    )
    return keep, to_core(give)


def project_kernel(core_ref, x_ref, w_ref, out_ref):
    out_ref[...] = jnp.dot(x_ref[...], w_ref[...], preferred_element_type=F32).astype(BF16)


def project(x, w, order, tile=256):
    return call_with_core(
        project_kernel,
        (w.shape[1] // tile,),
        [
            pl.BlockSpec(x.shape, lambda t, c: (0, 0)),
            pl.BlockSpec((w.shape[0], tile), lambda t, c: (0, t)),
        ],
        pl.BlockSpec((x.shape[0], tile), lambda t, c: (0, t)),
        jax.ShapeDtypeStruct((x.shape[0], w.shape[1]), BF16),
        [x, w],
        order=order,
        name="project",
        cost=LONG,
    )


def weight_kernel(sides, per, core_ref, *refs):
    keep_ref, send_ref, turned_ref, ordered_ref, y_scratch = refs[-5:]
    chips, rows = keep_ref.shape[:2]
    half = chips * rows
    pairs = 1 if sides else (len(refs) - 5) // 2
    width = keep_ref.shape[2]
    step = 512 if width % 512 == 0 else width // 2 if width > 512 else width

    def product(y):
        for at in range(0, width, step):
            spot = slice(at, at + step)
            total = jnp.dot(ordered_ref[...], y[:, spot], preferred_element_type=F32).astype(BF16)
            keep_ref[:, :, spot] = total[:half].reshape(chips, rows, step)
            send_ref[:, :, spot] = total[half:].reshape(chips, rows, step)

    def turn(x_ref):
        turned_ref[...] = x_ref[...].T
        for chip in range(chips):
            for which in range(2):
                core = core_ref[0] if which == 0 else 1 - core_ref[0]
                at = pl.multiple_of((2 * chip + core) * rows, rows)
                ordered_ref[which * half + chip * rows : which * half + (chip + 1) * rows] = (
                    turned_ref[pl.ds(at, rows)]
                )

    for pair in range(pairs):
        pl.when(pl.program_id(0) == pair * per)(partial(turn, refs[pair]))
    if sides:
        mend(refs[1 : 1 + sides], refs[1 + sides], y_scratch)
        product(y_scratch)
    elif pairs == 1:
        product(refs[1].at[0])
    else:
        for pair in range(pairs):
            pl.when(pl.program_id(0) // per == pair)(partial(product, refs[pairs + pair].at[0]))


def down_blocks(rows):
    height, width = rows // 4, D // 4
    blocks = [
        ((down * height, across * width), (across * height, down * width))
        for down in range(FF // width)
        for across in range(4)
    ]
    return blocks, height, width


def down_kernel(core_ref, x_ref, y_ref, keep_ref, send_ref, turned_ref):
    chip = pl.program_id(0)
    rows = keep_ref.shape[1]
    share = turned_ref.shape[0] // (2 * pl.num_programs(0))
    blocks, height, width = down_blocks(rows)

    @pl.when(chip == 0)
    def _():
        turned_ref[...] = x_ref[...].T

    for core, out_ref in ((core_ref[0], keep_ref), (1 - core_ref[0], send_ref)):
        at = pl.multiple_of((2 * chip + core) * share, 16)
        total = jnp.dot(turned_ref[pl.ds(at, share)], y_ref[...], preferred_element_type=F32)
        total = total.astype(BF16)
        for (row, column), (to_row, to_column) in blocks:
            out_ref[0, to_row : to_row + height, to_column : to_column + width] = total[
                row : row + height, column : column + width
            ]


def down_grads(x, y, order):
    positions, inputs = x.shape
    chips = lax.axis_size("seq") // 2
    rows = y.shape[1] // (2 * chips)
    out = jax.ShapeDtypeStruct((chips, rows, inputs), BF16)
    out_spec = pl.BlockSpec((1, rows, inputs), lambda t, c: (t, 0, 0))
    return call_with_core(
        down_kernel,
        (chips,),
        [pl.BlockSpec(x.shape, lambda t, c: (0, 0)), pl.BlockSpec(y.shape, lambda t, c: (0, 0))],
        [out_spec, out_spec],
        [out, out],
        [x, y],
        [pltpu.VMEM((inputs, positions), BF16)],
        order,
        name="down_grads",
        cost=LONG,
    )


def copy_kernel(core_ref, x_ref, out_ref):
    out_ref[...] = x_ref[...]


def placed(array, order):
    shape = jax.ShapeDtypeStruct(array.shape, array.dtype)
    return whole_call(copy_kernel, [array], [shape], order, "placed")[0]


def mend(y_refs, fix_ref, y_scratch):
    at = 0
    for y_ref in y_refs:
        y_scratch[:, at : at + y_ref.shape[2]] = y_ref[0]
        at += y_ref.shape[2]
    parts = fix_ref.shape[1]
    length = y_scratch.shape[0] // parts
    for part in range(parts):
        end = (part + 1) * length
        y_scratch[end - 16 : end] = y_scratch[end - 16 : end] + fix_ref[0, part]


def weight_grads(xs, ys, order, fix=None, width=None, cost=LONG):
    positions, inputs = xs[0].shape
    tiles = ys[0].shape[0]
    columns = ys[0].shape[2] if fix is None else sum(member.shape[2] for member in ys)
    width = width or columns
    count = columns // width
    per = tiles * count
    chips = lax.axis_size("seq") // 2
    rows = inputs // (2 * chips)
    out = jax.ShapeDtypeStruct((chips, rows, len(xs) * tiles * columns), BF16)
    out_spec = pl.BlockSpec((chips, rows, width), lambda t, c: (0, 0, t))
    in_specs = [pl.BlockSpec((positions, inputs), lambda t, c: (0, 0)) for _ in xs]
    if fix is None:

        def place(pair, t, c):
            t = jnp.clip(t - pair * per, 0, per - 1)
            return (t // count, 0, t % count)

        in_specs += [
            pl.BlockSpec((1, positions, width), partial(place, pair)) for pair in range(len(xs))
        ]
    else:
        in_specs += [
            pl.BlockSpec((1, positions, member.shape[2]), lambda t, c: (t, 0, 0)) for member in ys
        ]
        in_specs.append(pl.BlockSpec((1,) + fix.shape[1:], lambda t, c: (t, 0, 0, 0)))
    return call_with_core(
        partial(weight_kernel, 0 if fix is None else len(ys), per),
        (len(xs) * per,),
        in_specs,
        [out_spec, out_spec],
        [out, out],
        [*xs, *ys] + ([] if fix is None else [fix]),
        [
            pltpu.VMEM((inputs, positions), BF16),
            pltpu.VMEM((inputs, positions), BF16),
            pltpu.VMEM((positions, width), BF16),
        ],
        order,
        name="weight_grads",
        cost=cost,
    )


def dense_kernel(
    core_ref, branch_ref, x_ref, w_out_ref, gain_ref, w_gate_ref, w_up_ref, w_down_ref, cot_ref,
    out_ref, normed_ref, act_ref, grad_up_ref, attended_ref, branch_out_ref,
    hidden_ref, out_total_ref, back_total_ref,
):
    step = pl.program_id(0)

    @pl.when(step == 0)
    def _():
        hidden = x_ref[...].astype(F32) + jnp.dot(
            branch_ref[...], w_out_ref[...], preferred_element_type=F32
        )
        hidden_ref[...] = hidden
        scale = lax.rsqrt(jnp.mean(hidden * hidden, axis=-1, keepdims=True) + EPSILON)
        normed_ref[...] = (hidden * scale * gain_ref[...].astype(F32)).astype(BF16)
        out_total_ref[...] = hidden
        back_total_ref[...] = jnp.zeros_like(back_total_ref)

    normed = normed_ref[...]
    gate = mm(normed, w_gate_ref[...])
    up = mm(normed, w_up_ref[...])
    grad_act = mm(cot_ref[...], w_down_ref[...], (1, 1))
    sig = sigmoid(gate)
    active = gate * sig
    act = (active * up).astype(BF16)
    grad_gate = (grad_act * up * (sig * (1.0 + gate * (1.0 - sig)))).astype(BF16)
    grad_up = (grad_act * active).astype(BF16)
    act_ref[...] = act
    grad_up_ref[0] = grad_gate
    grad_up_ref[1] = grad_up
    out_total_ref[...] += mm(act, w_down_ref[...])
    back_total_ref[...] += mm(
        jnp.concatenate([grad_gate, grad_up], axis=1),
        jnp.concatenate([w_gate_ref[...], w_up_ref[...]], axis=1),
        (1, 1),
    )

    @pl.when(step == pl.num_programs(0) - 1)
    def _():
        out_ref[...] = out_total_ref[...].astype(BF16)
        hidden = hidden_ref[...]
        scale = lax.rsqrt(jnp.mean(hidden * hidden, axis=-1, keepdims=True) + EPSILON)
        unit = hidden * scale
        weighted = gain_ref[...].astype(F32) * back_total_ref[...]
        back = scale * (weighted - unit * jnp.mean(unit * weighted, axis=-1, keepdims=True))
        attended = (cot_ref[...].astype(F32) + back).astype(BF16)
        attended_ref[...] = attended
        branch_out_ref[...] = mm(attended, w_out_ref[...], (1, 1)).astype(BF16)


def dense(branch, x, w_out, gain, w_up, w_down, cotangent, order, tile=256):
    positions = x.shape[0]
    steps = FF // tile
    full = lambda *shape: pl.BlockSpec(shape, lambda t, c: (0,) * len(shape))
    wide = full(positions, D)
    low = jax.ShapeDtypeStruct((positions, D), BF16)
    return call_with_core(
        dense_kernel,
        (steps,),
        [
            wide, wide, full(D, D), full(1, D),
            pl.BlockSpec((D, tile), lambda t, c: (0, t)),
            pl.BlockSpec((D, tile), lambda t, c: (0, steps + t)),
            pl.BlockSpec((tile, D), lambda t, c: (t, 0)),
            wide,
        ],
        [
            wide, wide,
            pl.BlockSpec((positions, tile), lambda t, c: (0, t)),
            pl.BlockSpec((2, positions, tile), lambda t, c: (0, 0, t)),
            wide, wide,
        ],
        [
            low, low,
            jax.ShapeDtypeStruct((positions, FF), BF16),
            jax.ShapeDtypeStruct((2, positions, FF), BF16),
            low, low,
        ],
        [branch, x, w_out, gain[None], w_up, w_up, w_down, cotangent],
        [pltpu.VMEM((positions, D), F32)] * 3,
        order,
        name="dense",
        cost=30.0,
    )


def input_kernel(count, first, last, core_ref, *refs):
    y_refs, fix_ref, w_ref = refs[:count], refs[count], refs[count + 1]
    rest, (out_ref, total_ref, y_scratch) = refs[count + 2 : -3], refs[-3:]
    step = pl.program_id(0)

    @pl.when(step == 0)
    def _():
        if not first:
            total_ref[...] = rest[0][...]
            return
        gate_ref, w_gate_ref, rates_ref, w_rates_ref = rest
        total_ref[...] = mm(gate_ref[...], w_gate_ref[...], (1, 1))
        length = rates_ref.shape[2]
        for part in range(rates_ref.shape[0]):
            spot = slice(part * length, (part + 1) * length)
            total_ref[spot] = total_ref[spot] + mm(rates_ref[part], w_rates_ref[...], (0, 1))

    mend(y_refs, fix_ref, y_scratch)
    total_ref[...] += mm(y_scratch[...], w_ref[...], (1, 1))

    @pl.when(step == pl.num_programs(0) - 1)
    def _():
        if not last:
            out_ref[...] = total_ref[...]
            return
        x_ref, gain_ref, hidden_ref = rest[1:]
        length = x_ref.shape[1]
        for part in range(x_ref.shape[0]):
            spot = slice(part * length, (part + 1) * length)
            x = x_ref[part].astype(F32)
            scale = lax.rsqrt(jnp.mean(x * x, axis=-1, keepdims=True) + EPSILON)
            unit = x * scale
            weighted = gain_ref[...].astype(F32) * total_ref[spot]
            back = scale * (weighted - unit * jnp.mean(unit * weighted, axis=-1, keepdims=True))
            out_ref[part] = (hidden_ref[spot].astype(F32) + back).astype(BF16)


def input_grad(ys, fix, w_qkv, begin, end, rest, x, order):
    groups, positions, width = ys[0].shape
    parts = x.shape[0]
    first, last = begin == 0, end == groups
    full = lambda array: pl.BlockSpec(array.shape, lambda t, c: (0,) * array.ndim)
    out = jax.ShapeDtypeStruct(x.shape, BF16) if last else jax.ShapeDtypeStruct((positions, D), F32)
    return call_with_core(
        partial(input_kernel, len(ys), first, last),
        (end - begin,),
        [pl.BlockSpec((1, positions, width), lambda t, c: (begin + t, 0, 0))] * len(ys)
        + [
            pl.BlockSpec((1, parts, 16, D), lambda t, c: (begin + t, 0, 0, 0)),
            pl.BlockSpec((D, D), lambda t, c: (0, begin + t)),
        ]
        + [full(member) for member in rest],
        full(out),
        out,
        [*ys, fix, w_qkv, *rest],
        [pltpu.VMEM((positions, D), F32), pltpu.VMEM((positions, D), BF16)],
        order,
        name="input_grad",
        cost=LONG,
    )


def bits(count):
    return range(count.bit_length() - 1)


def swap(value, axis, bit):
    count = lax.axis_size(axis)
    return lax.ppermute(value, axis, [(at, at ^ (1 << bit)) for at in range(count)])


def own_bit(axis, bit):
    return ((lax.axis_index(axis) >> bit) & 1).astype(jnp.int32).reshape(1)


def round_kernel(splits, count, bit_ref, *refs):
    step = 4 if splits else 2
    outs = refs[step * count :]
    at = 0
    for member in range(count):
        blocks = refs[step * member : step * member + step]
        width = blocks[0].shape[-1]
        for half in range(step // 2):
            own, got = blocks[2 * half], blocks[2 * half + 1]
            total = own[...].astype(F32) + got[...].astype(F32)
            out = outs[half]
            out[:, :, at : at + width] = total.reshape(out.shape[:2] + (width,)).astype(BF16)
        at += width


def added(members, split, order, name):
    columns = sum(member[3] for member in members)
    lead = 1
    if split is not None:
        while split[1] % (4 * lead) == 0 and lead * split[2] * columns * 2 < 400000:
            lead *= 2
    size = members[0][0].shape[0] * members[0][0].shape[1]
    args, in_specs = [], []
    if split is None:
        bit, ahead, behind = jnp.zeros((1,), jnp.int32), 1, size
    else:
        bit, ahead, behind = split
    for own, got, at, width in members:
        for half in range(1 if split is None else 2):
            for array in (own, got):
                if split is None:
                    args.append(array.reshape(1, size, array.shape[2]))
                    spec = pl.BlockSpec((1, behind, width), lambda a, b, n=at // width: (0, 0, n))
                else:
                    args.append(array.reshape(ahead, 2, behind, array.shape[2]))
                    spec = pl.BlockSpec(
                        (lead, 1, behind, width),
                        lambda a, b, h=half, n=at // width: (a, b[0] ^ (1 - h), 0, n),
                    )
                in_specs.append(spec)
    out = jax.ShapeDtypeStruct((ahead, behind, columns), BF16)
    out_spec = pl.BlockSpec((lead, behind, columns), lambda a, b: (a, 0, 0))
    outs = 1 if split is None else 2
    return call_with_core(
        partial(round_kernel, split is not None, len(members)),
        (ahead // lead,),
        in_specs,
        [out_spec] * outs,
        [out] * outs,
        args,
        order=order,
        name=name,
        scalar=bit,
        limit=VMEM_SMALL if split is None else VMEM_LIMIT,
        cost=3.0,
    )


def sum_kernel(core_ref, own_ref, got_ref, out_ref):
    out_ref[...] = (own_ref[...].astype(F32) + got_ref[...].astype(F32)).astype(out_ref.dtype)


def summed_with(value, got, order, dtype):
    rows, columns = value.shape
    spec = pl.BlockSpec((rows // 2, columns), lambda t, c: (t, 0))
    return call_with_core(
        sum_kernel,
        (2,),
        [spec, spec],
        spec,
        jax.ShapeDtypeStruct(value.shape, dtype),
        [value, got],
        order=order,
        name="summed",
        cost=2.0,
    )


def pair_kernel(bit_ref, value_ref, got_ref, out_ref):
    out_ref[:, pl.ds(bit_ref[0], 1)] = value_ref[...][:, None]
    out_ref[:, pl.ds(1 - bit_ref[0], 1)] = got_ref[...][:, None]


class Stream:
    def __init__(self, order, parts):
        self.order = order
        self.chips, self.rows = parts[0][0][0].shape[:2]
        self.count = lax.axis_size("row")
        self.share = self.rows // self.count
        self.parts = [list(part) for part in parts]
        row_bits = list(bits(self.count))
        self.row_plans = [row_bits, row_bits[::-1]]
        self.dims = [
            [("seq", bit + 1) for bit in bits(self.chips)][::-1]
            + [("row", bit) for bit in row_bits[::-1]]
            for _ in parts
        ]
        self.gathered = []

    def exchange(self, members, dims, name):
        place = dims.index(name)
        ahead, behind = 1 << place, (1 << (len(dims) - 1 - place)) * self.share
        sent, kept = added(members, (own_bit(*name), ahead, behind), self.order, "exchange")
        dims.remove(name)
        return (kept, swap(sent, *name), 0, kept.shape[2])

    def along_row_rest(self):
        for step in range(1, len(self.row_plans[0])):
            self.along_row(step)

    def along_seq_rest(self):
        for step in range(1, len(bits(self.chips))):
            self.along_seq(step)

    def gather_rest(self):
        for _ in range(1, len(self.row_plans[0])):
            self.gather()

    def along_row(self, step):
        for at, part in enumerate(self.parts):
            name = ("row", self.row_plans[at][step])
            self.parts[at] = [self.exchange(part, self.dims[at], name)]

    def along_seq(self, step):
        if len(self.parts) > 1:
            self.parts = [[member for part in self.parts for member in part]]
        self.parts[0] = [self.exchange(self.parts[0], self.dims[0], ("seq", step + 1))]

    def finish_offloaded(self):
        members = [member for part in self.parts for member in part]
        (value,) = added(members, None, self.order, "share")
        groups = [[2 * chip + core for chip in range(self.chips)] for core in range(2)]
        self.share_value = lax.psum_scatter(
            value[0], "seq", scatter_dimension=0, axis_index_groups=groups, tiled=True
        )

    def share_found(self):
        members = [member for part in self.parts for member in part]
        (self.value,) = added(members, None, self.order, "share")
        self.value = self.value.reshape(1, self.share, -1)
        self.have = []
        self.send_gathered()

    def send_gathered(self):
        if len(self.have) < len(self.row_plans[0]):
            self.bit = self.row_plans[0][::-1][len(self.have)]
            self.got = swap(self.value, "row", self.bit)

    def gather(self):
        self.have = sorted(self.have + [self.bit], reverse=True)
        place = self.have.index(self.bit)
        ahead = 1 << place
        width = self.value.shape[-1]
        size = self.value.shape[0] * self.value.shape[1]
        value = self.value.reshape(ahead, size // ahead, width)
        got = self.got.reshape(ahead, size // ahead, width)
        spec = pl.BlockSpec(value.shape, lambda t, b: (0, 0, 0))
        out = jax.ShapeDtypeStruct((ahead, 2, size // ahead, width), BF16)
        self.value = call_with_core(
            pair_kernel,
            (1,),
            [spec, spec],
            pl.BlockSpec(out.shape, lambda t, b: (0, 0, 0, 0)),
            out,
            [value, got],
            order=self.order,
            name="gather",
            limit=VMEM_SMALL,
            scalar=own_bit("row", self.bit),
        ).reshape(1, 2 * size, width)
        self.send_gathered()

    def total(self):
        return self.value[0]


def placed_gather(stream, order):
    return lax.all_gather(placed(stream.share_value, order), "row", axis=0, tiled=True)


def final_kernel(plan, seq_ref, *refs):
    results = len(plan)
    arrays = refs[: len(refs) - 2 * results - 1]
    weights, outs, sums_ref = refs[len(arrays) :][:results], refs[-results - 1 : -1], refs[-1]
    sums = jnp.zeros((sums_ref.shape[1], HDIM), F32)
    for pieces, w_ref, out_ref in zip(plan, weights, outs):
        for piece in pieces:
            if len(piece) > 4:
                array, row, height, at, width, to_row, to = piece
                out_ref[to_row : to_row + height, to : to + width] = arrays[array][
                    row : row + height, at : at + width
                ].astype(F32)
                continue
            array, at, width, to = piece
            total = arrays[array][:, at : at + width].astype(F32)
            out_ref[:, to : to + width] = total
            if w_ref.shape[1] < out_ref.shape[1]:
                continue
            weighted = total * w_ref[:, to : to + width].astype(F32)
            for lane in range(0, width, HDIM):
                sums = sums + weighted[:, lane : lane + HDIM]
    sums_ref[...] = mm(jnp.ones((8, 2 * HDIM), BF16), split(sums), (1, 1))


def final(arrays, plan, weights, order):
    rows = arrays[0].shape[0]
    full = lambda *shape: pl.BlockSpec(shape, lambda t, c: (0, 0))
    return call_with_core(
        partial(final_kernel, plan),
        (1,),
        [full(*array.shape) for array in arrays]
        + [pl.BlockSpec((rows, w.shape[1]), lambda t, c: (c[0], 0)) for w, _ in weights],
        [full(*shape) for _, shape in weights] + [full(8, rows)],
        [jax.ShapeDtypeStruct(shape, F32) for _, shape in weights]
        + [jax.ShapeDtypeStruct((8, rows), F32)],
        [*arrays, *[w for w, _ in weights]],
        order=order,
        name="final",
        cost=3.0,
        scalar=lax.axis_index("seq").astype(jnp.int32).reshape(1),
    )


def half_product(formula, former, latter):
    return jnp.einsum(formula, former, latter, preferred_element_type=F32)


def shortened(value):
    return jax.tree.map(lambda part: part.astype(BF16), value)


def rms_norm(tensor, gain):
    return tensor * lax.rsqrt(jnp.mean(tensor * tensor, axis=-1, keepdims=True) + EPSILON) * gain


def swiglu(gate_up):
    return jax.nn.silu(gate_up[..., :FF]) * gate_up[..., FF:]


def local(
    hidden_in, lengths, norm1_gain, w_qkv, conv_w, w_rates, a_log, dt_bias,
    w_gate, out_gain, w_out, norm2_gain, w_up, w_down, cotangent,
):
    row_count, length = hidden_in.shape[:2]
    level = levels()
    taps = conv_w.astype(F32).T
    norm_column = norm1_gain[:, None]
    positions = row_count * length
    flat = lambda tensor: tensor.reshape(positions, tensor.shape[-1])
    unflat = lambda tensor: tensor.reshape(row_count, length, tensor.shape[-1])
    order = Order()
    normed, col, row, keep, mask, projected = front(
        hidden_in, along(hidden_in[:, length - HALO :], 1), lengths, norm1_gain, w_rates, a_log,
        dt_bias, w_qkv, order,
    )
    q, k, v, t, wu, p, m, device = maps(projected, taps, keep, col, row, mask, level, order)
    maps_shape = (row_count // 2 * HEADS, HDIM, HDIM)
    device = device.reshape((2, 2) + maps_shape)
    other = to_core(device)
    low_maps = jax.ShapeDtypeStruct(maps_shape, BF16)
    high_maps = jax.ShapeDtypeStruct(maps_shape, F32)
    gate = unflat(project(flat(normed), w_gate, order))
    chip_m, chip_b, leaving = whole_call(
        chip_maps_kernel, [device, other], [low_maps, high_maps, low_maps], order, "chip_maps"
    )
    states_in = carried(device, other, (), chip_m, chip_b, leaving, 1, order)
    entering_shape = (row_count // 2, HEADS, HDIM, HDIM)
    states_in = [member.reshape(entering_shape) for member in states_in]
    branch, mixed, states, delta = mix(q, k, wu, p, col, states_in, gate, out_gain, order)
    layer_out, normed2, activated, grad_gate_up, grad_attended, grad_branch = dense(
        flat(branch), flat(hidden_in), w_out, norm2_gain, w_up, w_down, flat(cotangent), order
    )
    grad_mixed, grad_gate, gain_parts, grads = adjoint(
        unflat(grad_branch), mixed, gate, out_gain, q, wu, p, m, col, order
    )
    grad_out_gain = jnp.sum(gain_parts, axis=(0, 1, 2))
    grads = grads.reshape((2,) + maps_shape)
    other_grads = to_core(grads)
    with_other = lambda pair: (pair[0], to_core(pair[1]))
    chip_grad, leaving = whole_call(
        chip_grads_kernel,
        [grads, other_grads, device, other],
        [high_maps, low_maps],
        order,
        "chip_grads",
    )
    done = {}

    def first_hop():
        done["down"] = with_other(down_grads(activated, flat(cotangent), order))

    def second_hop():
        done["up"] = with_other(weight_grads([normed2], [grad_gate_up], order, width=1408))

    def third_hop():
        done["others"] = with_other(
            weight_grads(
                [flat(branch), flat(normed)],
                [grad_attended[None], flat(grad_gate)[None]],
                order,
                width=512,
            )
        )

    adjoints = carried(
        device, other, (grads, other_grads), chip_m, chip_grad, leaving, -1, order,
        [first_hop, second_hop, third_hop],
    )
    adjoints = [member.reshape(entering_shape) for member in adjoints]
    seq = lax.axis_size("seq")
    rows = D // seq
    core = lax.axis_index("seq") % 2
    width = HEADS // 2 * HDIM
    cut = GROUPS * width // 2

    def back_part(first):
        return back(
            first, 2, projected, taps, keep, col, row, mask,
            (q, k, v, t, wu, p, states, delta), grad_mixed, adjoints, order,
        )

    def fix_of(*members):
        gh = jnp.concatenate([member[1] for member in members], axis=3)
        return jnp.pad(along(gh, -1), ((0, 0), (0, 0), (8, 0), (0, 0)))

    tiles = lambda *members: [
        member[0].reshape(GROUPS, positions, member[0].shape[-1]) for member in members
    ]
    up, down, others = done["up"], done["down"], done["others"]
    ups = Stream(order, [[up + (0, 3 * FF // 2)], [up + (3 * FF // 2, FF // 2), down + (0, FF)]])
    ups.along_row(0)
    first = back_part(0)
    second = back_part(2)
    fix_low = fix_of(first, second)
    low = with_other(weight_grads([flat(normed)], tiles(first, second), order, fix_low, cost=1.0))
    ups.along_row_rest()
    third = back_part(4)
    low = Stream(order, [[low + (0, cut), others + (0, D)], [low + (cut, cut), others + (D, D)]])
    low.along_row(0)
    ups.finish_offloaded()
    fourth = back_part(6)
    fix_high = fix_of(third, fourth)
    high = with_other(weight_grads([flat(normed)], tiles(third, fourth), order, fix_high, cost=1.0))
    low.along_row_rest()
    parts = (first, second, third, fourth)
    grad_rates, rate_sums = rates_back([member[3] for member in parts], row, a_log, order)
    grad_w_rates = half_product("rel,rld->ed", grad_rates[:, :24], normed)
    small = jnp.pad(rate_sums[:, :2].T.reshape(1, 2 * HEADS), ((0, 0), (0, HDIM - 2 * HEADS)))
    small = jnp.concatenate([small, grad_out_gain[None]], axis=0)
    grad_conv = jnp.sum(jnp.concatenate([member[2] for member in parts], axis=2), axis=0)[:, :, :4]
    extra = jnp.concatenate(
        [
            jnp.moveaxis(grad_conv, 2, 0).reshape(4, seq, -1).swapaxes(0, 1).reshape(seq, -1, HDIM),
            grad_w_rates.reshape(24, seq, -1).swapaxes(0, 1).reshape(seq, -1, HDIM),
            jnp.broadcast_to(small, (seq, 2, HDIM)),
        ],
        axis=1,
    ).astype(BF16)
    extra_rows = extra.shape[1]
    extra = jnp.pad(extra, ((0, 0), (0, rows - extra_rows), (0, 0)))
    extra = extra.reshape(seq // 2, 2, rows, HDIM)
    take = lambda index: lax.dynamic_index_in_dim(extra, index, 1, keepdims=False)
    extra = with_other((take(core), take(1 - core)))
    high = Stream(order, [[high + (0, cut), extra + (0, HDIM)], [high + (cut, cut)]])
    high.along_row(0)
    low.along_seq(0)
    up_total = placed_gather(ups, order)
    fix = jnp.concatenate([fix_low, fix_high], axis=3)
    w_rates_wide = jnp.pad(w_rates, ((0, 0), (0, grad_rates.shape[1] - w_rates.shape[1])))
    part = input_grad(
        tiles(*parts), fix, w_qkv, 0, 3, [flat(grad_gate), w_gate, grad_rates, w_rates_wide],
        hidden_in, order,
    )
    high.along_row_rest()
    grad_x = input_grad(
        tiles(*parts), fix, w_qkv, 3, GROUPS, [part, hidden_in, norm1_gain[None], grad_attended],
        hidden_in, order,
    )
    low.along_seq_rest()
    high.along_seq(0)
    low.share_found()
    high.along_seq_rest()
    low.gather()
    high.share_found()
    low.gather_rest()
    blocks, height, block = down_blocks(rows)
    up_total, down_total, up_sums = final(
        [up_total],
        [
            [(0, 0, 2 * FF, 0)],
            [
                (0, there[0], height, 2 * FF + there[1], block, here[0], here[1])
                for here, there in blocks
            ],
        ],
        [(w_up, (rows, 2 * FF)), (norm_column, (FF // seq, D))],
        order,
    )
    high.gather()
    high.gather_rest()
    low_total, high_total = low.total(), high.total()
    pieces = []
    for group in range(GROUPS):
        at = group * width
        for begin, end in ((at, min(at + width, cut)), (max(at, cut), at + width)):
            if begin < end:
                to = group * D + begin - at
                past = begin >= cut
                pieces.append((0, begin + D * past, end - begin, to))
                pieces.append((1, begin + HDIM * past, end - begin, to + width))
    qkv_total, out_total, gate_total, qkv_sums = final(
        [low_total, high_total],
        [pieces, [(0, cut, D, 0)], [(0, 2 * cut + D, D, 0)]],
        [(w_qkv, (rows, GROUPS * D)), (norm_column, (rows, D)), (w_gate, (rows, D))],
        order,
    )
    extra = high_total[:extra_rows, cut : cut + HDIM].astype(F32)
    conv_rows = GROUPS * D * 4 // (seq * HDIM)
    conv_total = extra[:conv_rows].reshape(4, -1).T
    rates_total = extra[conv_rows:-2].reshape(24, -1)
    small = extra[-2:]
    layer_out = unflat(layer_out)
    at = lax.axis_index("seq") * rows
    mine = lambda tensor: lax.dynamic_slice_in_dim(tensor, at, rows, 0).astype(F32)
    norm1_total = (
        qkv_sums[0] + jnp.sum(rates_total * mine(w_rates).T, axis=0)
    ) / mine(norm1_gain)
    norm2_total = up_sums[0] / mine(norm2_gain)
    return (
        layer_out,
        grad_x,
        norm1_total,
        qkv_total,
        conv_total,
        rates_total.T,
        small[0, :HEADS],
        small[0, HEADS : 2 * HEADS],
        gate_total,
        small[1],
        out_total,
        norm2_total,
        up_total,
        down_total,
    )


def solution(mesh):
    return jax.shard_map(
        local,
        mesh=mesh,
        in_specs=(
            P("row", "seq", None),
            P("row", None),
            P(),
            P(),
            P(),
            P(),
            P(),
            P(),
            P(),
            P(),
            P(),
            P(),
            P(),
            P(),
            P("row", "seq", None),
        ),
        out_specs=(
            P("row", "seq", None),
            P("row", "seq", None),
            P("seq"),
            P("seq", None),
            P("seq", None),
            P("seq", None),
            P(),
            P(),
            P("seq", None),
            P(),
            P("seq", None),
            P("seq"),
            P("seq", None),
            P("seq", None),
        ),
        check_vma=False,
    )
```

```python
from functools import partial

import jax
import jax.numpy as jnp
from jax import lax
from jax.experimental import pallas as pl
from jax.experimental.pallas import tpu as pltpu
from jax.sharding import PartitionSpec as P

D = 1024
HEADS = 8
HDIM = 128
NH = 2
FF = 2816
CHUNK = 128
VIRT = NH * CHUNK
GROUPS = 1 + 2 * NH
PAIR = 2
QUAD = 4
HALO = 16
EPSILON = 1e-06
F32 = jnp.float32
BF16 = jnp.bfloat16
HIGHEST = lax.Precision.HIGHEST
VMEM_LIMIT = 60 * 1024 * 1024
VMEM_SMALL = 20 * 1024 * 1024
FLOPS_A_US = 1000000000
LONG = 200.0


def mm(former, latter, over=(1, 0)):
    return lax.dot_general(
        former.astype(BF16),
        latter.astype(BF16),
        (((over[0],), (over[1],)), ((), ())),
        preferred_element_type=F32,
    )


def exact_mm(former, latter):
    return jnp.dot(former, latter, precision=HIGHEST, preferred_element_type=F32)


def sigmoid(tensor):
    return 1.0 / (1.0 + jnp.exp(-tensor))


def iota2(shape, dim):
    return lax.broadcasted_iota(jnp.int32, shape, dim)


def params(*semantics, limit=VMEM_LIMIT):
    return pltpu.CompilerParams(dimension_semantics=semantics or None, vmem_limit_bytes=limit)


def pinned(kernel, inputs, pins):
    return lambda *refs: kernel(*refs[:inputs], *refs[inputs + len(pins) :])


def pin_specs(pins):
    return [pl.BlockSpec(memory_space=pl.ANY)] * len(pins)


def core_index():
    return (lax.axis_index("seq") % 2).astype(jnp.int32).reshape(1)


class Order:
    def __init__(self):
        self.last = ()

    def then(self, outputs):
        self.last = (jax.tree.leaves(outputs)[0],)
        return outputs


def call_with_core(
    kernel, grid, in_specs, out_specs, out_shape, args, scratch=(), order=None, name=None, scalar=None,
    limit=VMEM_LIMIT, cost=1.0,
):
    pins = order.last if order else ()
    outputs = pl.pallas_call(
        pinned(kernel, 1 + len(args), pins),
        grid_spec=pltpu.PrefetchScalarGridSpec(
            num_scalar_prefetch=1,
            grid=grid,
            in_specs=list(in_specs) + pin_specs(pins),
            out_specs=out_specs,
            scratch_shapes=list(scratch),
        ),
        out_shape=out_shape,
        compiler_params=params(*["arbitrary"] * len(grid), limit=limit),
        cost_estimate=pl.CostEstimate(
            flops=int(cost * FLOPS_A_US), bytes_accessed=1, transcendentals=0
        ),
        name=name,
    )(core_index() if scalar is None else scalar, *args, *pins)
    return order.then(outputs) if order else outputs


def doc_of(place, ends):
    found = sum((place >= end).astype(jnp.int32) for end in ends)
    return jnp.where(place >= 0, found, -1)


def doc_terms(anchor, ends, keep_ref, mask_ref):
    length = keep_ref.shape[1]
    place = anchor + iota2((length, HDIM), 0)
    docs = doc_of(place, ends)
    for tap in range(3):
        keep_ref[tap] = (doc_of(place - 3 + tap, ends) == docs).astype(F32)
    carry, same_last = [], []
    for chunk in range(length // CHUNK):
        at = chunk * CHUNK
        own = docs[at : at + CHUNK]
        across = doc_of(anchor + at + iota2((CHUNK, CHUNK), 1), ends)
        lower = iota2((CHUNK, CHUNK), 0) >= iota2((CHUNK, CHUNK), 1)
        mask_ref[chunk] = jnp.where((own == across) & lower, 0.0, -1e30)
        carry.append((own == doc_of(anchor + at - 1, ends)).astype(F32))
        same_last.append((own == doc_of(anchor + at + CHUNK - 1, ends)).astype(F32))
    return jnp.concatenate(carry, axis=0), jnp.concatenate(same_last, axis=0)


def front_kernel(
    scalar_ref, x_ref, halo_ref, gain_ref, w_ref, lanes_ref, w_qkv_ref,
    normed_ref, col_ref, row_ref, keep_ref, mask_ref, projected_ref, all_ref,
):
    rows, length = x_ref.shape[:2]
    count = (scalar_ref.shape[0] - 1) // rows

    def norm(x):
        x = x.astype(F32)
        scale = lax.rsqrt(jnp.mean(x * x, axis=-1, keepdims=True) + EPSILON)
        return (x * scale * gain_ref[...].astype(F32)).astype(BF16)

    @pl.when(pl.program_id(0) == 0)
    def _():
        for row in range(rows):
            normed = norm(x_ref[row])
            normed_ref[row] = normed
            all_ref[row * length : (row + 1) * length] = normed
            at = rows * length + row * HALO
            all_ref[at : at + HALO] = norm(halo_ref[row])
            ends, end = [], 0
            for place in range(count):
                end = end + scalar_ref[1 + row * count + place]
                ends.append(end)
            flags = doc_terms(scalar_ref[0], ends, keep_ref.at[row], mask_ref.at[row])
            packed = rate_terms(normed, w_ref, lanes_ref, flags)
            col_ref[row] = packed
            row_ref[row] = packed.T

    projected_ref[...] = jnp.dot(
        all_ref[...], w_qkv_ref[...], preferred_element_type=F32
    ).astype(BF16)


def rate_terms(normed, w_ref, lanes_ref, flags):
    length = normed.shape[0]
    rates = jnp.dot(normed, w_ref[...], preferred_element_type=F32)
    shifted = rates + lanes_ref[1:2]
    soft = jnp.maximum(shifted, 0.0) + jnp.log(1.0 + jnp.exp(-jnp.abs(shifted)))
    log_decay = lanes_ref[0:1] * soft
    shape = (length, length)
    here, there = iota2(shape, 0), iota2(shape, 1)
    lower = ((here >= there) & (here // CHUNK == there // CHUNK)).astype(F32)
    summed = exact_mm(lower, log_decay)
    last = jnp.concatenate(
        [
            jnp.broadcast_to(summed[at + CHUNK - 1 : at + CHUNK], (CHUNK, HDIM))
            for at in range(0, length, CHUNK)
        ],
        axis=0,
    )
    start = jnp.exp(summed) * flags[0]
    tail = jnp.exp(last - summed) * flags[1]
    lane = iota2((length, HDIM), 1)
    packed = jnp.zeros((length, HDIM), F32)
    for limit, member, shift in (
        (56, log_decay, 32),
        (48, sigmoid(shifted), 24),
        (40, tail, 16),
        (32, start, 8),
        (24, summed, 0),
        (16, sigmoid(rates), 0),
    ):
        member = pltpu.roll(member, shift, 1) if shift else member
        packed = jnp.where(lane < limit, member, packed)
    return packed


def front(hidden_in, halo, lengths, gain, w_rates, a_log, dt_bias, w_qkv, order, tile=512):
    rows, length = hidden_in.shape[:2]
    w_padded = jnp.pad(w_rates, ((0, 0), (0, HDIM - w_rates.shape[1])))
    first = NH * HEADS
    lanes = jnp.pad(
        jnp.stack([-jnp.exp(a_log), dt_bias]), ((0, 0), (first, HDIM - first - HEADS))
    )
    anchor = (lax.axis_index("seq") * length).astype(jnp.int32).reshape(1)
    count = rows * (length + HALO)
    chunks = length // CHUNK
    full = lambda *shape: pl.BlockSpec(shape, lambda t, c: (0,) * len(shape))
    return call_with_core(
        front_kernel,
        (w_qkv.shape[1] // tile,),
        [
            full(rows, length, D),
            full(rows, HALO, D),
            full(1, D),
            full(D, HDIM),
            full(2, HDIM),
            pl.BlockSpec((D, tile), lambda t, c: (0, t)),
        ],
        [
            full(rows, length, D),
            full(rows, length, HDIM),
            full(rows, HDIM, length),
            full(rows, 3, length, HDIM),
            full(rows, chunks, CHUNK, CHUNK),
            pl.BlockSpec((count, tile), lambda t, c: (0, t)),
        ],
        [
            jax.ShapeDtypeStruct((rows, length, D), BF16),
            jax.ShapeDtypeStruct((rows, length, HDIM), F32),
            jax.ShapeDtypeStruct((rows, HDIM, length), F32),
            jax.ShapeDtypeStruct((rows, 3, length, HDIM), F32),
            jax.ShapeDtypeStruct((rows, chunks, CHUNK, CHUNK), F32),
            jax.ShapeDtypeStruct((count, w_qkv.shape[1]), BF16),
        ],
        [hidden_in, halo, gain[None], w_padded, lanes, w_qkv],
        [pltpu.VMEM((count, D), BF16)],
        order,
        name="front",
        cost=10.0,
        scalar=jnp.concatenate([anchor, lengths.reshape(-1)]),
    )


def convolved(x_ref, halo_ref, taps_ref, keep_ref, ext_ref, lanes):
    length = x_ref.shape[0]
    ext_ref[0:8] = halo_ref[:, lanes].astype(F32)[HALO - 8 :]
    x = x_ref[:, lanes].astype(F32)
    ext_ref[8 : 8 + length] = x
    summed = x * taps_ref[3:4, lanes]
    for tap in range(3):
        summed = summed + ext_ref[5 + tap : 5 + tap + length] * keep_ref[0, tap] * taps_ref[
            tap : tap + 1, lanes
        ]
    return summed


def head_columns(col_ref, head):
    return pltpu.roll(col_ref[0], (HDIM - head) % HDIM, 1)


def lane_sums(tensor):
    return mm(tensor, jnp.ones((HDIM, HDIM), BF16))


def split(tensor):
    high = tensor.astype(BF16)
    return jnp.concatenate([high, (tensor - high.astype(F32)).astype(BF16)], axis=1)


def row_sums(tensor):
    return mm(jnp.ones((8, 2 * HDIM), BF16), split(tensor), (1, 1))[0:1]


def column_sums(tensor):
    total = mm(jnp.ones((8, tensor.shape[0]), BF16), split(tensor))
    return total[0:1, :HDIM] + total[0:1, HDIM:]


def wide(column):
    return jnp.broadcast_to(column, (column.shape[0], HDIM))


def pick(row_ref, place, head, at):
    own = iota2((HEADS, CHUNK), 0) == head
    rows = row_ref[0, place * HEADS : place * HEADS + HEADS, at : at + CHUNK]
    return jnp.sum(jnp.where(own, rows, 0.0), axis=0, keepdims=True)


def lanes_of(sub):
    return slice(sub * HDIM, sub * HDIM + HDIM)


def in_turns(makers):
    running = list(makers)
    while running:
        running = [member for member in running if next(member, "end") != "end"]


def stacked(first, second):
    half = CHUNK // 2
    return jnp.concatenate([first[:half], second[:half], first[half:], second[half:]], axis=0)


def both(tensor):
    return stacked(tensor, tensor)


def unstacked(tensor):
    half = CHUNK // 2
    return (
        jnp.concatenate([tensor[:half], tensor[2 * half : 3 * half]], axis=0),
        jnp.concatenate([tensor[half : 2 * half], tensor[3 * half :]], axis=0),
    )


def merged(left, right):
    low = iota2(left.shape, 1) < CHUNK // 2
    return (
        jnp.where(low, left, pltpu.roll(right, CHUNK // 2, 1)),
        jnp.where(low, pltpu.roll(left, CHUNK // 2, 1), right),
    )


def folded(tensor):
    first, second = merged(tensor[:, :CHUNK], tensor[:, CHUNK:])
    return first + second


def place_of(index):
    half = CHUNK // 2
    return NH * ((index // CHUNK) * half + index % half) + (index // half) % NH


def decay_matrix(cols, row_ref, mask_ref, head, chunk):
    at = chunk * CHUNK
    across = pick(row_ref, 2, head, at)
    down = cols[at : at + CHUNK, 16:17]
    return jnp.exp(down - across + mask_ref[0, chunk])


def doubled(decay):
    low = iota2(decay.shape, 1) < CHUNK // 2
    turned = pltpu.roll(decay, CHUNK // 2, 1)
    return jnp.concatenate(
        [jnp.where(low, decay, turned), jnp.where(low, turned, decay)], axis=1
    )


def diagonal(pair):
    zero = jnp.zeros((CHUNK, CHUNK), pair.dtype)
    return jnp.concatenate(
        [
            jnp.concatenate([pair[:, :CHUNK], zero], axis=1),
            jnp.concatenate([zero, pair[:, CHUNK:]], axis=1),
        ],
        axis=0,
    )


def maps_kernel(core_ref, *refs):
    xs, halos, taps = refs[0:5], refs[5:10], refs[10:15]
    keep_ref, col_ref, row_ref, mask_ref, level_ref = refs[15:20]
    q_ref, k_ref, v_ref, t_ref, wu_ref, p_ref, m_ref, dev_ref, ext_ref = refs[20:]
    length = xs[0].shape[0]
    chunks = length // CHUNK
    eye = (iota2((HDIM, HDIM), 0) == iota2((HDIM, HDIM), 1)).astype(F32)
    eye_pair = jnp.concatenate([eye, eye], axis=1).astype(BF16)
    heads = q_ref.shape[1]
    data = []
    for sub in range(heads):
        head = heads * pl.program_id(1) + sub
        cols = head_columns(col_ref, head)
        parts = []
        for group in range(GROUPS):
            summed = convolved(
                xs[group], halos[group], taps[group], keep_ref, ext_ref.at[group], lanes_of(sub)
            )
            active = summed * sigmoid(summed)
            if group < 1 + NH:
                active = active * lax.rsqrt(lane_sums(active * active) + EPSILON)
            parts.append(active.astype(BF16))
        q_ref[0, sub] = parts[0]
        for chunk in range(chunks):
            at = chunk * CHUNK
            rows = slice(at, at + CHUNK)
            query = parts[0][rows]
            keys = stacked(parts[1][rows], parts[2][rows])
            values = stacked(parts[3][rows], parts[4][rows])
            k_ref[0, sub, chunk] = keys
            v_ref[0, sub, chunk] = values
            decay = decay_matrix(cols, row_ref, mask_ref, head, chunk)
            wide_decay = doubled(decay)
            beta = stacked(wide(cols[rows, 0:1]), wide(cols[rows, 8:9]))
            beta_wide = jnp.concatenate([beta, beta], axis=1)
            mixing = (mm(keys, keys, (1, 1)) * both(wide_decay) * beta_wide).astype(BF16)
            p_ref[0, sub, chunk] = (mm(query, keys, (1, 1)) * wide_decay).astype(BF16)
            blocks = jnp.concatenate([mixing[:CHUNK, :CHUNK], mixing[CHUNK:, CHUNK:]], axis=1)
            inverse = eye_pair - blocks * level_ref[0]
            data.append([keys, values, beta, blocks, inverse, cols[rows], mixing[CHUNK:, :CHUNK]])
    for step in range(1, 7):
        mids = [
            mm(member[3] * level_ref[step], diagonal(member[4])).astype(BF16) for member in data
        ]
        for member, mid in zip(data, mids):
            member[4] = member[4] - mm(member[4], diagonal(mid)).astype(BF16)
    mids = [mm(member[6], member[4][:, :CHUNK]).astype(BF16) for member in data]
    for member, mid in zip(data, mids):
        corner = -mm(member[4][:, CHUNK:], mid).astype(BF16)
        member[4] = jnp.concatenate(
            [
                jnp.concatenate([member[4][:, :CHUNK], jnp.zeros_like(corner)], axis=1),
                jnp.concatenate([corner, member[4][:, CHUNK:]], axis=1),
            ],
            axis=0,
        )
    device = [None] * heads
    for chunk in range(chunks):
        for sub in range(heads):
            keys, values, beta, _, inverse, cols, _ = data[sub * chunks + chunk]
            t_ref[0, sub, chunk] = inverse
            keys_float = keys.astype(F32)
            right = jnp.concatenate(
                [keys_float * (both(wide(cols[:, 24:25])) * beta), values.astype(F32) * beta], axis=1
            )
            solved = mm(inverse, right).astype(BF16)
            wu_ref[0, sub, chunk] = solved
            tail_keys = keys_float * both(wide(cols[:, 32:33]))
            pair = mm(solved, tail_keys, (0, 0))
            block_m = cols[CHUNK - 1 : CHUNK, 24:25] * eye - pair[:HDIM]
            block_b = pair[HDIM:]
            m_ref[0, sub, chunk] = block_m.astype(BF16)
            if chunk == 0:
                device[sub] = (block_m, block_b)
            else:
                chained = mm(jnp.concatenate(device[sub], axis=0), block_m)
                device[sub] = (chained[:HDIM], chained[HDIM:] + block_b)
    for sub in range(heads):
        dev_ref[0, 0, 0, sub] = device[sub][0].astype(BF16)
        dev_ref[0, 1, 0, sub] = device[sub][1].astype(BF16)


def group_specs(block, index, first, pair):
    return [
        pl.BlockSpec(
            block + (pair * HDIM,),
            partial(lambda g, r, h, *_: index(r, (g * HEADS + first) // pair + h), g),
        )
        for g in range(GROUPS)
    ]


def head_spec(*block, first=0, pair=PAIR):
    return pl.BlockSpec(
        (1, pair) + block, lambda r, h, *_: (r, first // pair + h) + (0,) * len(block)
    )


def conv_specs(rows, length, first=0, pair=PAIR):
    return (
        group_specs((length,), lambda r, c: (r, c), first, pair)
        + group_specs((HALO,), lambda r, c: (rows * length // HALO + r, c), first, pair)
        + group_specs((4,), lambda r, c: (0, c), first, pair)
        + [pl.BlockSpec((1, 3, length, HDIM), lambda r, h, *_: (r, 0, 0, 0))]
    )


def rate_specs(length):
    return [
        pl.BlockSpec((1, length, HDIM), lambda r, h, *_: (r, 0, 0)),
        pl.BlockSpec((1, HDIM, length), lambda r, h, *_: (r, 0, 0)),
        pl.BlockSpec((1, length // CHUNK, CHUNK, CHUNK), lambda r, h, *_: (r, 0, 0, 0)),
    ]


def levels():
    place = place_of(jnp.arange(CHUNK))
    differ = place[:, None] ^ place[None, :]
    level = sum((differ >= (1 << bit)).astype(jnp.int32) for bit in range(1, 7))
    level = jnp.where(place[:, None] > place[None, :], level, -1)
    masks = (level[None] == jnp.arange(7)[:, None, None]).astype(BF16)
    return jnp.concatenate([masks, masks], axis=2)


def slot_spec(rows, *lead, pair=PAIR):
    half = rows // 2
    return pl.BlockSpec(
        (1,) + lead + (1, pair, HDIM, HDIM),
        lambda r, h, core: ((r // half) ^ core[0],) + (0,) * len(lead) + (r % half, h, 0, 0),
    )


def maps(projected, taps, keep, col, row, mask, level, order):
    rows, length = col.shape[:2]
    spec = partial(head_spec, pair=QUAD)
    chunks = length // CHUNK
    shape = lambda *tail: jax.ShapeDtypeStruct((rows, HEADS) + tail, BF16)
    masks = pl.BlockSpec((7, CHUNK, VIRT), lambda r, h, *_: (0, 0, 0))
    return call_with_core(
        maps_kernel,
        (rows, HEADS // QUAD),
        conv_specs(rows, length, pair=QUAD) + rate_specs(length) + [masks],
        [
            spec(length, HDIM),
            spec(chunks, VIRT, HDIM),
            spec(chunks, VIRT, HDIM),
            spec(chunks, VIRT, VIRT),
            spec(chunks, VIRT, VIRT),
            spec(chunks, CHUNK, VIRT),
            spec(chunks, HDIM, HDIM),
            slot_spec(rows, 2, pair=QUAD),
        ],
        [
            shape(length, HDIM),
            shape(chunks, VIRT, HDIM),
            shape(chunks, VIRT, HDIM),
            shape(chunks, VIRT, VIRT),
            shape(chunks, VIRT, VIRT),
            shape(chunks, CHUNK, VIRT),
            shape(chunks, HDIM, HDIM),
            jax.ShapeDtypeStruct((2, 2, rows // 2, HEADS, HDIM, HDIM), BF16),
        ],
        [projected] * 10 + [taps] * 5 + [keep, col, row, mask, level],
        [pltpu.VMEM((GROUPS, length + 8, HDIM), F32)],
        order,
        name="maps",
        cost=40.0,
    )


def entering_spec(rows, first=0, pair=PAIR):
    half = rows // 2
    return pl.BlockSpec(
        (1, pair, HDIM, HDIM), lambda r, h, *_: (r % half, first // pair + h, 0, 0)
    )


def entering_state(core_ref, own_ref, other_ref, sub, rows):
    mine = pl.program_id(0) // (rows // 2) == core_ref[0]
    return jnp.where(mine, own_ref[0, sub].astype(F32), other_ref[0, sub].astype(F32))


def mixed_kernel(
    row_count, core_ref, q_ref, k_ref, wu_ref, p_ref, col_ref, own_ref, other_ref, gate_ref, gain_ref,
    branch_ref, mixed_ref, states_ref, delta_ref,
):
    heads, chunks = k_ref.shape[1:3]

    def one(sub):
        cols = head_columns(col_ref, heads * pl.program_id(1) + sub)
        state = entering_state(core_ref, own_ref, other_ref, sub, row_count)
        outputs = []
        for chunk in range(chunks):
            at = chunk * CHUNK
            rows = slice(at, at + CHUNK)
            solved = wu_ref[0, sub, chunk]
            states_ref[0, sub, chunk] = state.astype(BF16)
            seen = mm(
                jnp.concatenate([solved[:, :HDIM], q_ref[0, sub, rows]], axis=0), state, (1, 1)
            )
            yield
            delta = (solved[:, HDIM:].astype(F32) - seen[:VIRT]).astype(BF16)
            delta_ref[0, sub, chunk] = delta
            if chunk + 1 < chunks:
                tail_keys = k_ref[0, sub, chunk].astype(F32) * both(cols[rows, 32:33])
                state = cols[at + CHUNK - 1 : at + CHUNK, 24:25] * state + mm(
                    delta, tail_keys, (0, 0)
                )
            outputs.append(cols[rows, 24:25] * seen[VIRT:] + mm(p_ref[0, sub, chunk], delta))
            yield
        mixed = jnp.concatenate(outputs, axis=0)
        mixed_ref[0, :, lanes_of(sub)] = mixed
        scale = lax.rsqrt(lane_sums(mixed * mixed) * (1.0 / HDIM) + EPSILON)
        gate = gate_ref[0, :, lanes_of(sub)].astype(F32)
        branch_ref[0, :, lanes_of(sub)] = (
            mixed * scale * gain_ref[...].astype(F32) * (gate * sigmoid(gate))
        ).astype(BF16)

    in_turns([one(sub) for sub in range(heads)])


def column_spec(length, first=0, pair=PAIR):
    return pl.BlockSpec((1, length, pair * HDIM), lambda r, h, *_: (r, 0, first // pair + h))


def mix(q, k, wu, p, col, states_in, gate, gain, order):
    rows, _, length = q.shape[:3]
    spec = partial(head_spec, pair=QUAD)
    chunks = length // CHUNK
    return call_with_core(
        partial(mixed_kernel, rows),
        (rows, HEADS // QUAD),
        [
            spec(length, HDIM),
            spec(chunks, VIRT, HDIM),
            spec(chunks, VIRT, VIRT),
            spec(chunks, CHUNK, VIRT),
            rate_specs(length)[0],
            entering_spec(rows, pair=QUAD),
            entering_spec(rows, pair=QUAD),
            column_spec(length, pair=QUAD),
            pl.BlockSpec((1, HDIM), lambda r, h, *_: (0, 0)),
        ],
        [
            column_spec(length, pair=QUAD),
            column_spec(length, pair=QUAD),
            spec(chunks, HDIM, HDIM),
            spec(chunks, VIRT, HDIM),
        ],
        [
            jax.ShapeDtypeStruct((rows, length, D), BF16),
            jax.ShapeDtypeStruct((rows, length, D), F32),
            jax.ShapeDtypeStruct((rows, HEADS, chunks, HDIM, HDIM), BF16),
            jax.ShapeDtypeStruct((rows, HEADS, chunks, VIRT, HDIM), BF16),
        ],
        [q, k, wu, p, col, *states_in, gate, gain[None]],
        order=order,
        name="mix",
        cost=11.0,
    )


def adjoint_kernel(
    core_ref, up_ref, mixed_ref, gate_ref, gain_ref, q_ref, wu_ref, p_ref, m_ref, col_ref,
    grad_mixed_ref, grad_gate_ref, grad_gain_ref, own_ref,
):
    heads, chunks = p_ref.shape[1:3]

    def one(sub):
        lanes = lanes_of(sub)
        cols = head_columns(col_ref, heads * pl.program_id(1) + sub)
        upstream, mixed, gate = (
            ref[0, :, lanes].astype(F32) for ref in (up_ref, mixed_ref, gate_ref)
        )
        gain = gain_ref[...].astype(F32)
        sig = sigmoid(gate)
        scale = lax.rsqrt(lane_sums(mixed * mixed) * (1.0 / HDIM) + EPSILON)
        unit = mixed * scale
        grad_gate_ref[0, :, lanes] = (
            upstream * unit * gain * (sig * (1.0 + gate * (1.0 - sig)))
        ).astype(BF16)
        upstream = upstream * (gate * sig)
        partial_gain = upstream * unit
        grad_gain_ref[0, sub] = jnp.sum(
            partial_gain.reshape(partial_gain.shape[0] // 8, 8, HDIM), axis=0
        )
        weighted = gain * upstream
        grad_mixed = scale * (weighted - unit * (lane_sums(unit * weighted) * (1.0 / HDIM)))
        low = grad_mixed.astype(BF16)
        grad_mixed_ref[0, :, lanes] = low
        yield
        grad_state = None
        for chunk in reversed(range(chunks)):
            at = chunk * CHUNK
            rows = slice(at, at + CHUNK)
            own_delta = mm(p_ref[0, sub, chunk], low[rows], (0, 0))
            yield
            left = jnp.concatenate(
                [(grad_mixed[rows] * cols[rows, 24:25]).astype(BF16), (-own_delta).astype(BF16)],
                axis=0,
            )
            right = jnp.concatenate([q_ref[0, sub, rows], wu_ref[0, sub, chunk, :, :HDIM]], axis=0)
            own = mm(left, right, (0, 0))
            if grad_state is not None:
                own = own + mm(grad_state, m_ref[0, sub, chunk], (1, 1))
            grad_state = own
            yield
        own_ref[0, 0, sub] = grad_state.astype(BF16)

    in_turns([one(sub) for sub in range(heads)])


def adjoint(upstream, mixed, gate, gain, q, wu, p, m, col, order):
    rows, _, length = q.shape[:3]
    spec = partial(head_spec, pair=QUAD)
    chunks = length // CHUNK
    return call_with_core(
        adjoint_kernel,
        (rows, HEADS // QUAD),
        [
            column_spec(length, pair=QUAD),
            column_spec(length, pair=QUAD),
            column_spec(length, pair=QUAD),
            pl.BlockSpec((1, HDIM), lambda r, h, *_: (0, 0)),
            spec(length, HDIM),
            spec(chunks, VIRT, VIRT),
            spec(chunks, CHUNK, VIRT),
            spec(chunks, HDIM, HDIM),
            rate_specs(length)[0],
        ],
        [
            column_spec(length, pair=QUAD),
            column_spec(length, pair=QUAD),
            spec(8, HDIM),
            slot_spec(rows, pair=QUAD),
        ],
        [
            jax.ShapeDtypeStruct((rows, length, D), BF16),
            jax.ShapeDtypeStruct((rows, length, D), BF16),
            jax.ShapeDtypeStruct((rows, HEADS, 8, HDIM), F32),
            jax.ShapeDtypeStruct((2, rows // 2, HEADS, HDIM, HDIM), BF16),
        ],
        [upstream, mixed, gate, gain[None], q, wu, p, m, col],
        order=order,
        name="adjoint",
        cost=11.0,
    )


def before(count, dim):
    return place_of(iota2((count, count), dim))


def back_kernel(first, rows, core_ref, *refs):
    xs, halos, taps = refs[0:5], refs[5:10], refs[10:15]
    keep_ref, col_ref, row_ref, mask_ref = refs[15:19]
    q_ref, shift_ref = refs[19], refs[-1]
    length = xs[0].shape[0]
    chunks = length // CHUNK
    heads = q_ref.shape[1]
    stats_ref = refs[-3]

    @pl.when(pl.program_id(1) == 0)
    def _():
        stats_ref[...] = jnp.zeros_like(stats_ref)

    strict = (before(VIRT, 0) > before(VIRT, 1)).astype(F32)
    for tap in range(3):
        shift_ref[tap, 0:8] = jnp.zeros((8, HDIM), F32)
        shift_ref[tap, 8 + length : 16 + length] = jnp.zeros((8, HDIM), F32)
    in_turns(
        [
            back_head(
                first, rows, core_ref, sub, heads, xs, halos, taps, keep_ref, col_ref, row_ref, mask_ref, strict, refs[19:],
            )
            for sub in range(heads)
        ]
    )


def back_head(
    first, row_count, core_ref, sub, heads, xs, halos, taps, keep_ref, col_ref, row_ref, mask_ref,
    strict, refs,
):
    q_ref, k_ref, v_ref, t_ref, wu_ref, p_ref, states_ref, delta_ref = refs[:8]
    grad_mixed_ref, own_ref, other_ref = refs[8:11]
    gp_ref, gh_ref, gw_ref, stats_ref, ext_ref, shift_ref = refs[11:]
    length = xs[0].shape[0]
    chunks = length // CHUNK
    head = first + heads * pl.program_id(1) + sub
    lanes = lanes_of(sub)
    cols = head_columns(col_ref, head)
    own_row = iota2((HEADS, CHUNK), 0) == head
    grad_next = entering_state(core_ref, own_ref, other_ref, sub, row_count)
    grads = [[None] * chunks for _ in range(GROUPS)]
    for chunk in reversed(range(chunks)):
        at = chunk * CHUNK
        rows = slice(at, at + CHUNK)
        query = q_ref[0, sub, rows]
        query_float = query.astype(F32)
        keys, values = k_ref[0, sub, chunk], v_ref[0, sub, chunk]
        keys_float, values_float = keys.astype(F32), values.astype(F32)
        solved, scores = wu_ref[0, sub, chunk], p_ref[0, sub, chunk]
        state, delta = states_ref[0, sub, chunk], delta_ref[0, sub, chunk]
        grad_out = grad_mixed_ref[0, rows, lanes]
        beta = stacked(wide(cols[rows, 0:1]), wide(cols[rows, 8:9]))
        beta_wide = jnp.concatenate([beta, beta], axis=1)
        start, tail = wide(cols[rows, 24:25]), wide(cols[rows, 32:33])
        start_wide, tail_wide = both(start), both(tail)
        end = cols[at + CHUNK - 1 : at + CHUNK, 24:25]
        decay = decay_matrix(cols, row_ref, mask_ref, head, chunk)
        wide_decay = doubled(decay)
        full_decay = both(wide_decay) * strict
        next_low = grad_next.astype(BF16)
        tail_keys = (keys_float * tail_wide).astype(BF16)
        grad_delta = mm(scores, grad_out, (0, 0)) + mm(tail_keys, next_low, (1, 1))
        delta_low = grad_delta.astype(BF16)
        grad_scores = mm(grad_out, delta, (1, 1))
        weighted_scores = grad_scores * scores.astype(F32)
        grad_raw = (grad_scores * wide_decay).astype(BF16)
        yield
        seen = mm(jnp.concatenate([grad_out, delta_low], axis=0), state)
        grad_query = start * seen[:CHUNK] + mm(grad_raw, keys)
        by_start = seen[:CHUNK] * query_float
        grad_wide = jnp.concatenate([-seen[CHUNK:], grad_delta], axis=1).astype(BF16)
        grad_end = jnp.sum(
            jnp.sum(grad_next * state.astype(F32), axis=0, keepdims=True), axis=1, keepdims=True
        )
        grad_tail_keys = mm(delta, next_low)
        left = jnp.concatenate(
            [(grad_out.astype(F32) * start).astype(BF16), (-grad_delta).astype(BF16)], axis=0
        )
        grad_next = end * grad_next + mm(
            left, jnp.concatenate([query, solved[:, :HDIM]], axis=0), (0, 0)
        )
        yield
        grad_right = mm(t_ref[0, sub, chunk], grad_wide, (0, 0))
        yield
        right_keys, right_values = grad_right[:, :HDIM], grad_right[:, HDIM:]
        grad_mixing = -mm(grad_right, solved, (1, 1))
        gram = mm(keys, keys, (1, 1))
        decayed = grad_mixing * full_decay
        weighted = decayed * gram
        grad_gram = (decayed * beta_wide).astype(BF16)
        yield
        by_keys = keys_float * right_keys
        by_values = values_float * right_values
        by_mixing = folded(weighted)
        grad_keys = (
            (start_wide * beta) * right_keys
            + tail_wide * grad_tail_keys
            + mm(grad_raw, query, (0, 0))
            + mm(grad_gram, keys)
            + mm(grad_gram, keys, (0, 0))
        )
        grad_values = beta * right_values
        fold = lambda tensor: sum(unstacked(tensor))
        pairs = fold(beta * by_mixing) + folded(weighted_scores)
        by_tail = fold(keys_float * grad_tail_keys) * tail
        by_log = pairs + (by_start + fold(beta * by_keys)) * start
        by_beta = start_wide * by_keys + by_values + by_mixing
        sums = row_sums(jnp.concatenate([by_beta, by_log, by_tail], axis=0))
        tail_sums = sums[:, 3 * CHUNK :]
        at_end = jnp.sum(tail_sums, axis=1, keepdims=True) + grad_end * end
        last = iota2((1, CHUNK), 1) == CHUNK - 1
        log_sums = sums[:, 2 * CHUNK : 3 * CHUNK] - tail_sums - column_sums(pairs)
        log_sums = log_sums + jnp.where(last, at_end, 0.0)
        beta_sums = merged(sums[:, :CHUNK], sums[:, CHUNK : 2 * CHUNK])
        for place, member in enumerate((*beta_sums, log_sums)):
            spot = slice(place * HEADS, place * HEADS + HEADS)
            stats_ref[0, spot, rows] = jnp.where(own_row, member, stats_ref[0, spot, rows])
        for group, member in enumerate(
            (grad_query, *unstacked(grad_keys), *unstacked(grad_values))
        ):
            grads[group][chunk] = member
        yield
    for group in range(GROUPS):
        ext = ext_ref.at[group]
        summed = convolved(xs[group], halos[group], taps[group], keep_ref, ext, lanes)
        sig = sigmoid(summed)
        active = summed * sig
        grad = jnp.concatenate(grads[group], axis=0).astype(BF16).astype(F32)
        if group < 1 + NH:
            scale = lax.rsqrt(lane_sums(active * active) + EPSILON)
            unit = active * scale
            grad = scale * (grad - unit * lane_sums(unit * grad))
        grad = grad * (sig * (1.0 + summed * (1.0 - sig)))
        total = grad * taps[group][3:4, lanes]
        before = None
        weight_rows = []
        for tap in range(3):
            kept = grad * keep_ref[0, tap]
            weight_rows.append(
                jnp.sum(kept * ext[5 + tap : 5 + tap + length], axis=0, keepdims=True)
            )
            shift_ref[tap, 8 : 8 + length] = kept * taps[group][tap : tap + 1, lanes]
            total = total + shift_ref[tap, 11 - tap : 11 - tap + length]
            early = shift_ref[tap, 3 - tap : 11 - tap]
            before = early if before is None else before + early
        weight_rows.append(
            jnp.sum(grad * ext[8 : 8 + length], axis=0, keepdims=True)
        )
        gp_ref[group, 0, :, lanes] = total.astype(BF16)
        gh_ref[group, 0, :, lanes] = before.astype(BF16)
        gw_ref[0, group, sub] = jnp.concatenate(
            weight_rows + [jnp.zeros((4, HDIM), F32)], axis=0
        )


def back(first, count, projected, taps, keep, col, row, mask, saved, grad_mixed, adjoints, order):
    rows, length = col.shape[:2]
    chunks = length // CHUNK
    spec = partial(head_spec, first=first)
    return call_with_core(
        partial(back_kernel, first, rows),
        (rows, count // PAIR),
        conv_specs(rows, length, first)
        + rate_specs(length)
        + [
            spec(length, HDIM),
            spec(chunks, VIRT, HDIM),
            spec(chunks, VIRT, HDIM),
            spec(chunks, VIRT, VIRT),
            spec(chunks, VIRT, VIRT),
            spec(chunks, CHUNK, VIRT),
            spec(chunks, HDIM, HDIM),
            spec(chunks, VIRT, HDIM),
            column_spec(length, first),
            entering_spec(rows, first),
            entering_spec(rows, first),
        ],
        [
            pl.BlockSpec((GROUPS, 1, length, PAIR * HDIM), lambda r, h, *_: (0, r, 0, h)),
            pl.BlockSpec((GROUPS, 1, 8, PAIR * HDIM), lambda r, h, *_: (0, r, 0, h)),
            pl.BlockSpec((1, GROUPS, PAIR, 8, HDIM), lambda r, h, *_: (r, 0, h, 0, 0)),
            pl.BlockSpec((1, 24, length), lambda r, h, *_: (r, 0, 0)),
        ],
        [
            jax.ShapeDtypeStruct((GROUPS, rows, length, count * HDIM), BF16),
            jax.ShapeDtypeStruct((GROUPS, rows, 8, count * HDIM), BF16),
            jax.ShapeDtypeStruct((rows, GROUPS, count, 8, HDIM), F32),
            jax.ShapeDtypeStruct((rows, 24, length), F32),
        ],
        [projected] * 10 + [taps] * 5
        + [keep, col, row, mask, *saved, grad_mixed, *adjoints],
        [
            pltpu.VMEM((GROUPS, length + 8, HDIM), F32),
            pltpu.VMEM((3, length + 16, HDIM), F32),
        ],
        order,
        name="back",
        cost=LONG,
    )


def rates_kernel(core_ref, *refs):
    row_ref, nega_ref, rates_ref, sums_ref = refs[-4:]
    rows, _, length = row_ref.shape
    shape = (length, length)
    here, there = iota2(shape, 0), iota2(shape, 1)
    lower = ((here >= there) & (here // CHUNK == there // CHUNK)).astype(F32)
    lane = iota2((HEADS, HDIM), 1)
    total = jnp.zeros((HEADS, HDIM), F32)
    for r in range(rows):
        beta = row_ref[r, 0:16]
        stats = sum(ref[r] for ref in refs[:-4])
        grad_log = exact_mm(stats[16:24], lower)
        grad_bias = grad_log * nega_ref[:, 0:1] * row_ref[r, 40:48]
        rates_ref[r, 0:16] = (stats[0:16] * beta * (1.0 - beta)).astype(BF16)
        rates_ref[r, 16:24] = grad_bias.astype(BF16)
        rates_ref[r, 24:32] = jnp.zeros((8, length), BF16)
        by_log = jnp.sum(grad_log * row_ref[r, 48:56], axis=1, keepdims=True)
        by_bias = jnp.sum(grad_bias, axis=1, keepdims=True)
        total = total + jnp.where(lane == 0, by_log, jnp.where(lane == 1, by_bias, 0.0))
    sums_ref[...] = total


def rates_back(stats, row, a_log, order):
    rows, _, length = stats[0].shape
    nega = jnp.broadcast_to(-jnp.exp(a_log)[:, None], (HEADS, HDIM))
    return whole_call(
        rates_kernel,
        [*stats, row, nega],
        [
            jax.ShapeDtypeStruct((rows, 32, length), BF16),
            jax.ShapeDtypeStruct((HEADS, HDIM), F32),
        ],
        order,
        "rates_back",
        LONG,
    )


def to_core(value):
    count = lax.axis_size("seq")
    return lax.ppermute(value, "seq", [(at, at ^ 1) for at in range(count)])


def to_chip(value, step):
    count = lax.axis_size("seq")
    pairs = [(at, at + 2 * step) for at in range(count) if 0 <= at + 2 * step < count]
    return lax.ppermute(value, "seq", pairs)


def along(value, step):
    count = lax.axis_size("seq")
    pairs = [(at, at + step) for at in range(count) if 0 <= at + step < count]
    return lax.ppermute(value, "seq", pairs)


def whole_call(kernel, args, out_shape, order, name, cost=1.0):
    return call_with_core(
        kernel,
        (1,),
        [pl.BlockSpec(arg.shape, lambda t, c, n=arg.ndim: (0,) * n) for arg in args],
        [pl.BlockSpec(out.shape, lambda t, c, n=len(out.shape): (0,) * n) for out in out_shape],
        out_shape,
        args,
        order=order,
        name=name,
        limit=VMEM_SMALL,
        cost=cost,
    )


def chip_maps_kernel(core_ref, device_ref, other_ref, m_ref, b_ref, leaving_ref):
    own_first = core_ref[0] == 0
    for at in range(m_ref.shape[0]):
        own_m, own_b = (device_ref[0, place, at].astype(F32) for place in range(2))
        other_m, other_b = (other_ref[1, place, at].astype(F32) for place in range(2))
        first = jnp.concatenate(
            [jnp.where(own_first, own_m, other_m), jnp.where(own_first, own_b, other_b)], axis=0
        )
        second_m = jnp.where(own_first, other_m, own_m)
        second_b = jnp.where(own_first, other_b, own_b)
        both_maps = mm(first, second_m)
        m_ref[at] = both_maps[:HDIM].astype(BF16)
        total = both_maps[HDIM:] + second_b
        b_ref[at] = total
        leaving_ref[at] = total.astype(BF16)


def chip_grads_kernel(core_ref, own_ref, other_ref, device_ref, other_map_ref, b_ref, leaving_ref):
    own_first = core_ref[0] == 1
    for at in range(b_ref.shape[0]):
        own, other = own_ref[0, at].astype(F32), other_ref[1, at].astype(F32)
        own_m, other_m = device_ref[0, 0, at].astype(F32), other_map_ref[1, 0, at].astype(F32)
        first = jnp.where(own_first, own, other)
        second = jnp.where(own_first, other, own)
        second_m = jnp.where(own_first, other_m, own_m)
        total = mm(first, second_m, (1, 1)) + second
        b_ref[at] = total
        leaving_ref[at] = total.astype(BF16)


def hop_kernel(over, core_ref, entering_ref, m_ref, b_ref, leaving_ref):
    for at in range(entering_ref.shape[0]):
        leaving_ref[at] = (mm(entering_ref[at], m_ref[at], over) + b_ref[at]).astype(BF16)


def last_kernel(over, first_core, core_ref, entering_ref, device_ref, other_ref, *refs):
    own_b, other_b = (refs[0], refs[1]) if len(refs) == 4 else (None, None)
    keep_ref, give_ref = refs[-2:]
    own_first = core_ref[0] == first_core
    for at in range(entering_ref.shape[0]):
        entering = entering_ref[at].astype(F32)
        first_m = jnp.where(
            own_first, device_ref[0, 0, at].astype(F32), other_ref[1, 0, at].astype(F32)
        )
        own = device_ref[0, 1, at] if own_b is None else own_b[0, at]
        other = other_ref[1, 1, at] if other_b is None else other_b[1, at]
        first_b = jnp.where(own_first, own.astype(F32), other.astype(F32))
        between = mm(entering, first_m, over) + first_b
        keep_ref[at] = jnp.where(own_first, entering, between).astype(BF16)
        give_ref[at] = jnp.where(own_first, between, entering).astype(BF16)


def carried(device, other, grads, chip_m, chip_b, leaving, step, order, meanwhile=()):
    over, first_core = ((1, 0), 0) if step > 0 else ((1, 1), 1)
    low = jax.ShapeDtypeStruct(leaving.shape, BF16)
    hops = lax.axis_size("seq") // 2 - 1
    for at in range(hops):
        entering = to_chip(leaving, step)
        if at < len(meanwhile):
            meanwhile[at]()
        if at + 1 < hops:
            (leaving,) = whole_call(
                partial(hop_kernel, over), [entering, chip_m, chip_b], [low], order, "hop"
            )
    keep, give = whole_call(
        partial(last_kernel, over, first_core),
        [entering, device, other, *grads],
        [low, low],
        order,
        "entering",
    )
    return keep, to_core(give)


def project_kernel(core_ref, x_ref, w_ref, out_ref):
    out_ref[...] = jnp.dot(x_ref[...], w_ref[...], preferred_element_type=F32).astype(BF16)


def project(x, w, order, tile=256):
    return call_with_core(
        project_kernel,
        (w.shape[1] // tile,),
        [
            pl.BlockSpec(x.shape, lambda t, c: (0, 0)),
            pl.BlockSpec((w.shape[0], tile), lambda t, c: (0, t)),
        ],
        pl.BlockSpec((x.shape[0], tile), lambda t, c: (0, t)),
        jax.ShapeDtypeStruct((x.shape[0], w.shape[1]), BF16),
        [x, w],
        order=order,
        name="project",
        cost=LONG,
    )


def weight_kernel(sides, per, core_ref, *refs):
    keep_ref, send_ref, turned_ref, ordered_ref, y_scratch = refs[-5:]
    chips, rows = keep_ref.shape[:2]
    half = chips * rows
    pairs = 1 if sides else (len(refs) - 5) // 2
    width = keep_ref.shape[2]
    step = 512 if width % 512 == 0 else width // 2 if width > 512 else width

    def product(y):
        for at in range(0, width, step):
            spot = slice(at, at + step)
            total = jnp.dot(ordered_ref[...], y[:, spot], preferred_element_type=F32).astype(BF16)
            keep_ref[:, :, spot] = total[:half].reshape(chips, rows, step)
            send_ref[:, :, spot] = total[half:].reshape(chips, rows, step)

    def turn(x_ref):
        turned_ref[...] = x_ref[...].T
        for chip in range(chips):
            for which in range(2):
                core = core_ref[0] if which == 0 else 1 - core_ref[0]
                at = pl.multiple_of((2 * chip + core) * rows, rows)
                ordered_ref[which * half + chip * rows : which * half + (chip + 1) * rows] = (
                    turned_ref[pl.ds(at, rows)]
                )

    for pair in range(pairs):
        pl.when(pl.program_id(0) == pair * per)(partial(turn, refs[pair]))
    if sides:
        mend(refs[1 : 1 + sides], refs[1 + sides], y_scratch)
        product(y_scratch)
    elif pairs == 1:
        product(refs[1].at[0])
    else:
        for pair in range(pairs):
            pl.when(pl.program_id(0) // per == pair)(partial(product, refs[pairs + pair].at[0]))


def down_blocks(rows):
    height, width = rows // 4, D // 4
    blocks = [
        ((down * height, across * width), (across * height, down * width))
        for down in range(FF // width)
        for across in range(4)
    ]
    return blocks, height, width


def down_kernel(core_ref, x_ref, y_ref, keep_ref, send_ref, turned_ref):
    chip = pl.program_id(0)
    rows = keep_ref.shape[1]
    share = turned_ref.shape[0] // (2 * pl.num_programs(0))
    blocks, height, width = down_blocks(rows)

    @pl.when(chip == 0)
    def _():
        turned_ref[...] = x_ref[...].T

    for core, out_ref in ((core_ref[0], keep_ref), (1 - core_ref[0], send_ref)):
        at = pl.multiple_of((2 * chip + core) * share, 16)
        total = jnp.dot(turned_ref[pl.ds(at, share)], y_ref[...], preferred_element_type=F32)
        total = total.astype(BF16)
        for (row, column), (to_row, to_column) in blocks:
            out_ref[0, to_row : to_row + height, to_column : to_column + width] = total[
                row : row + height, column : column + width
            ]


def down_grads(x, y, order):
    positions, inputs = x.shape
    chips = lax.axis_size("seq") // 2
    rows = y.shape[1] // (2 * chips)
    out = jax.ShapeDtypeStruct((chips, rows, inputs), BF16)
    out_spec = pl.BlockSpec((1, rows, inputs), lambda t, c: (t, 0, 0))
    return call_with_core(
        down_kernel,
        (chips,),
        [pl.BlockSpec(x.shape, lambda t, c: (0, 0)), pl.BlockSpec(y.shape, lambda t, c: (0, 0))],
        [out_spec, out_spec],
        [out, out],
        [x, y],
        [pltpu.VMEM((inputs, positions), BF16)],
        order,
        name="down_grads",
        cost=LONG,
    )


def copy_kernel(core_ref, x_ref, out_ref):
    out_ref[...] = x_ref[...]


def placed(array, order):
    shape = jax.ShapeDtypeStruct(array.shape, array.dtype)
    return whole_call(copy_kernel, [array], [shape], order, "placed")[0]


def mend(y_refs, fix_ref, y_scratch):
    at = 0
    for y_ref in y_refs:
        y_scratch[:, at : at + y_ref.shape[2]] = y_ref[0]
        at += y_ref.shape[2]
    parts = fix_ref.shape[1]
    length = y_scratch.shape[0] // parts
    for part in range(parts):
        end = (part + 1) * length
        y_scratch[end - 16 : end] = y_scratch[end - 16 : end] + fix_ref[0, part]


def weight_grads(xs, ys, order, fix=None, width=None, cost=LONG):
    positions, inputs = xs[0].shape
    tiles = ys[0].shape[0]
    columns = ys[0].shape[2] if fix is None else sum(member.shape[2] for member in ys)
    width = width or columns
    count = columns // width
    per = tiles * count
    chips = lax.axis_size("seq") // 2
    rows = inputs // (2 * chips)
    out = jax.ShapeDtypeStruct((chips, rows, len(xs) * tiles * columns), BF16)
    out_spec = pl.BlockSpec((chips, rows, width), lambda t, c: (0, 0, t))
    in_specs = [pl.BlockSpec((positions, inputs), lambda t, c: (0, 0)) for _ in xs]
    if fix is None:

        def place(pair, t, c):
            t = jnp.clip(t - pair * per, 0, per - 1)
            return (t // count, 0, t % count)

        in_specs += [
            pl.BlockSpec((1, positions, width), partial(place, pair)) for pair in range(len(xs))
        ]
    else:
        in_specs += [
            pl.BlockSpec((1, positions, member.shape[2]), lambda t, c: (t, 0, 0)) for member in ys
        ]
        in_specs.append(pl.BlockSpec((1,) + fix.shape[1:], lambda t, c: (t, 0, 0, 0)))
    return call_with_core(
        partial(weight_kernel, 0 if fix is None else len(ys), per),
        (len(xs) * per,),
        in_specs,
        [out_spec, out_spec],
        [out, out],
        [*xs, *ys] + ([] if fix is None else [fix]),
        [
            pltpu.VMEM((inputs, positions), BF16),
            pltpu.VMEM((inputs, positions), BF16),
            pltpu.VMEM((positions, width), BF16),
        ],
        order,
        name="weight_grads",
        cost=cost,
    )


def dense_kernel(
    core_ref, branch_ref, x_ref, w_out_ref, gain_ref, w_gate_ref, w_up_ref, w_down_ref, cot_ref,
    out_ref, normed_ref, act_ref, grad_up_ref, attended_ref, branch_out_ref,
    hidden_ref, out_total_ref, back_total_ref,
):
    step = pl.program_id(0)

    @pl.when(step == 0)
    def _():
        hidden = x_ref[...].astype(F32) + jnp.dot(
            branch_ref[...], w_out_ref[...], preferred_element_type=F32
        )
        hidden_ref[...] = hidden
        scale = lax.rsqrt(jnp.mean(hidden * hidden, axis=-1, keepdims=True) + EPSILON)
        normed_ref[...] = (hidden * scale * gain_ref[...].astype(F32)).astype(BF16)
        out_total_ref[...] = hidden
        back_total_ref[...] = jnp.zeros_like(back_total_ref)

    normed = normed_ref[...]
    gate = mm(normed, w_gate_ref[...])
    up = mm(normed, w_up_ref[...])
    grad_act = mm(cot_ref[...], w_down_ref[...], (1, 1))
    sig = sigmoid(gate)
    active = gate * sig
    act = (active * up).astype(BF16)
    grad_gate = (grad_act * up * (sig * (1.0 + gate * (1.0 - sig)))).astype(BF16)
    grad_up = (grad_act * active).astype(BF16)
    act_ref[...] = act
    grad_up_ref[0] = grad_gate
    grad_up_ref[1] = grad_up
    out_total_ref[...] += mm(act, w_down_ref[...])
    back_total_ref[...] += mm(
        jnp.concatenate([grad_gate, grad_up], axis=1),
        jnp.concatenate([w_gate_ref[...], w_up_ref[...]], axis=1),
        (1, 1),
    )

    @pl.when(step == pl.num_programs(0) - 1)
    def _():
        out_ref[...] = out_total_ref[...].astype(BF16)
        hidden = hidden_ref[...]
        scale = lax.rsqrt(jnp.mean(hidden * hidden, axis=-1, keepdims=True) + EPSILON)
        unit = hidden * scale
        weighted = gain_ref[...].astype(F32) * back_total_ref[...]
        back = scale * (weighted - unit * jnp.mean(unit * weighted, axis=-1, keepdims=True))
        attended = (cot_ref[...].astype(F32) + back).astype(BF16)
        attended_ref[...] = attended
        branch_out_ref[...] = mm(attended, w_out_ref[...], (1, 1)).astype(BF16)


def dense(branch, x, w_out, gain, w_up, w_down, cotangent, order, tile=256):
    positions = x.shape[0]
    steps = FF // tile
    full = lambda *shape: pl.BlockSpec(shape, lambda t, c: (0,) * len(shape))
    wide = full(positions, D)
    low = jax.ShapeDtypeStruct((positions, D), BF16)
    return call_with_core(
        dense_kernel,
        (steps,),
        [
            wide, wide, full(D, D), full(1, D),
            pl.BlockSpec((D, tile), lambda t, c: (0, t)),
            pl.BlockSpec((D, tile), lambda t, c: (0, steps + t)),
            pl.BlockSpec((tile, D), lambda t, c: (t, 0)),
            wide,
        ],
        [
            wide, wide,
            pl.BlockSpec((positions, tile), lambda t, c: (0, t)),
            pl.BlockSpec((2, positions, tile), lambda t, c: (0, 0, t)),
            wide, wide,
        ],
        [
            low, low,
            jax.ShapeDtypeStruct((positions, FF), BF16),
            jax.ShapeDtypeStruct((2, positions, FF), BF16),
            low, low,
        ],
        [branch, x, w_out, gain[None], w_up, w_up, w_down, cotangent],
        [pltpu.VMEM((positions, D), F32)] * 3,
        order,
        name="dense",
        cost=30.0,
    )


def input_kernel(count, first, last, core_ref, *refs):
    y_refs, fix_ref, w_ref = refs[:count], refs[count], refs[count + 1]
    rest, (out_ref, total_ref, y_scratch) = refs[count + 2 : -3], refs[-3:]
    step = pl.program_id(0)

    @pl.when(step == 0)
    def _():
        if not first:
            total_ref[...] = rest[0][...]
            return
        gate_ref, w_gate_ref, rates_ref, w_rates_ref = rest
        total_ref[...] = mm(gate_ref[...], w_gate_ref[...], (1, 1))
        length = rates_ref.shape[2]
        for part in range(rates_ref.shape[0]):
            spot = slice(part * length, (part + 1) * length)
            total_ref[spot] = total_ref[spot] + mm(rates_ref[part], w_rates_ref[...], (0, 1))

    mend(y_refs, fix_ref, y_scratch)
    total_ref[...] += mm(y_scratch[...], w_ref[...], (1, 1))

    @pl.when(step == pl.num_programs(0) - 1)
    def _():
        if not last:
            out_ref[...] = total_ref[...]
            return
        x_ref, gain_ref, hidden_ref = rest[1:]
        length = x_ref.shape[1]
        for part in range(x_ref.shape[0]):
            spot = slice(part * length, (part + 1) * length)
            x = x_ref[part].astype(F32)
            scale = lax.rsqrt(jnp.mean(x * x, axis=-1, keepdims=True) + EPSILON)
            unit = x * scale
            weighted = gain_ref[...].astype(F32) * total_ref[spot]
            back = scale * (weighted - unit * jnp.mean(unit * weighted, axis=-1, keepdims=True))
            out_ref[part] = (hidden_ref[spot].astype(F32) + back).astype(BF16)


def input_grad(ys, fix, w_qkv, begin, end, rest, x, order):
    groups, positions, width = ys[0].shape
    parts = x.shape[0]
    first, last = begin == 0, end == groups
    full = lambda array: pl.BlockSpec(array.shape, lambda t, c: (0,) * array.ndim)
    out = jax.ShapeDtypeStruct(x.shape, BF16) if last else jax.ShapeDtypeStruct((positions, D), F32)
    return call_with_core(
        partial(input_kernel, len(ys), first, last),
        (end - begin,),
        [pl.BlockSpec((1, positions, width), lambda t, c: (begin + t, 0, 0))] * len(ys)
        + [
            pl.BlockSpec((1, parts, 16, D), lambda t, c: (begin + t, 0, 0, 0)),
            pl.BlockSpec((D, D), lambda t, c: (0, begin + t)),
        ]
        + [full(member) for member in rest],
        full(out),
        out,
        [*ys, fix, w_qkv, *rest],
        [pltpu.VMEM((positions, D), F32), pltpu.VMEM((positions, D), BF16)],
        order,
        name="input_grad",
        cost=LONG,
    )


def bits(count):
    return range(count.bit_length() - 1)


def swap(value, axis, bit):
    count = lax.axis_size(axis)
    return lax.ppermute(value, axis, [(at, at ^ (1 << bit)) for at in range(count)])


def own_bit(axis, bit):
    return ((lax.axis_index(axis) >> bit) & 1).astype(jnp.int32).reshape(1)


def round_kernel(splits, count, fine, bit_ref, *refs):
    step = 4 if splits else 2
    outs = refs[step * count :]
    at = 0
    for member in range(count):
        blocks = refs[step * member : step * member + step]
        width = blocks[0].shape[-1]
        for half in range(step // 2):
            own, got = blocks[2 * half], blocks[2 * half + 1]
            total = own[...].astype(F32) + got[...].astype(F32)
            out = outs[half]
            total = total.reshape(out.shape[:2] + (width,))
            out[:, :, at : at + width] = total.astype(BF16)
            if fine is not None and at <= fine < at + width:
                spot = fine - at
                value = total[:, :, spot : spot + HDIM] + total[:, :, spot + HDIM : spot + 2 * HDIM]
                high = value.astype(BF16)
                out[:, :, fine : fine + HDIM] = high
                out[:, :, fine + HDIM : fine + 2 * HDIM] = (value - high.astype(F32)).astype(BF16)
        at += width


def added(members, split, order, name, fine=None):
    columns = sum(member[3] for member in members)
    lead = 1
    if split is not None:
        while split[1] % (4 * lead) == 0 and lead * split[2] * columns * 2 < 400000:
            lead *= 2
    size = members[0][0].shape[0] * members[0][0].shape[1]
    args, in_specs = [], []
    if split is None:
        bit, ahead, behind = jnp.zeros((1,), jnp.int32), 1, size
    else:
        bit, ahead, behind = split
    for own, got, at, width in members:
        for half in range(1 if split is None else 2):
            for array in (own, got):
                if split is None:
                    args.append(array.reshape(1, size, array.shape[2]))
                    spec = pl.BlockSpec((1, behind, width), lambda a, b, n=at // width: (0, 0, n))
                else:
                    args.append(array.reshape(ahead, 2, behind, array.shape[2]))
                    spec = pl.BlockSpec(
                        (lead, 1, behind, width),
                        lambda a, b, h=half, n=at // width: (a, b[0] ^ (1 - h), 0, n),
                    )
                in_specs.append(spec)
    out = jax.ShapeDtypeStruct((ahead, behind, columns), BF16)
    out_spec = pl.BlockSpec((lead, behind, columns), lambda a, b: (a, 0, 0))
    outs = 1 if split is None else 2
    return call_with_core(
        partial(round_kernel, split is not None, len(members), fine),
        (ahead // lead,),
        in_specs,
        [out_spec] * outs,
        [out] * outs,
        args,
        order=order,
        name=name,
        scalar=bit,
        limit=VMEM_SMALL if split is None else VMEM_LIMIT,
        cost=3.0,
    )


def sum_kernel(core_ref, own_ref, got_ref, out_ref):
    out_ref[...] = (own_ref[...].astype(F32) + got_ref[...].astype(F32)).astype(out_ref.dtype)


def summed_with(value, got, order, dtype):
    rows, columns = value.shape
    spec = pl.BlockSpec((rows // 2, columns), lambda t, c: (t, 0))
    return call_with_core(
        sum_kernel,
        (2,),
        [spec, spec],
        spec,
        jax.ShapeDtypeStruct(value.shape, dtype),
        [value, got],
        order=order,
        name="summed",
        cost=2.0,
    )


def pair_kernel(bit_ref, value_ref, got_ref, out_ref):
    out_ref[:, pl.ds(bit_ref[0], 1)] = value_ref[...][:, None]
    out_ref[:, pl.ds(1 - bit_ref[0], 1)] = got_ref[...][:, None]


class Stream:
    def __init__(self, order, parts, fine=None):
        self.order, self.fine = order, fine
        self.chips, self.rows = parts[0][0][0].shape[:2]
        self.count = lax.axis_size("row")
        self.share = self.rows // self.count
        self.parts = [list(part) for part in parts]
        row_bits = list(bits(self.count))
        self.row_plans = [row_bits, row_bits[::-1]]
        self.dims = [
            [("seq", bit + 1) for bit in bits(self.chips)][::-1]
            + [("row", bit) for bit in row_bits[::-1]]
            for _ in parts
        ]
        self.gathered = []

    def exchange(self, members, dims, name, fine=None):
        place = dims.index(name)
        ahead, behind = 1 << place, (1 << (len(dims) - 1 - place)) * self.share
        sent, kept = added(members, (own_bit(*name), ahead, behind), self.order, "exchange", fine)
        dims.remove(name)
        return (kept, swap(sent, *name), 0, kept.shape[2])

    def along_row_rest(self):
        for step in range(1, len(self.row_plans[0])):
            self.along_row(step)

    def along_seq_rest(self):
        for step in range(1, len(bits(self.chips))):
            self.along_seq(step)

    def gather_rest(self):
        for _ in range(1, len(self.row_plans[0])):
            self.gather()

    def along_row(self, step):
        for at, part in enumerate(self.parts):
            name = ("row", self.row_plans[at][step])
            self.parts[at] = [self.exchange(part, self.dims[at], name, None if at else self.fine)]

    def along_seq(self, step):
        if len(self.parts) > 1:
            self.parts = [[member for part in self.parts for member in part]]
        self.parts[0] = [
            self.exchange(self.parts[0], self.dims[0], ("seq", step + 1), self.fine)
        ]

    def finish_offloaded(self):
        members = [member for part in self.parts for member in part]
        (value,) = added(members, None, self.order, "share")
        groups = [[2 * chip + core for chip in range(self.chips)] for core in range(2)]
        self.share_value = lax.psum_scatter(
            value[0], "seq", scatter_dimension=0, axis_index_groups=groups, tiled=True
        )

    def share_found(self):
        members = [member for part in self.parts for member in part]
        (self.value,) = added(members, None, self.order, "share", self.fine)
        self.value = self.value.reshape(1, self.share, -1)
        self.have = []
        self.send_gathered()

    def send_gathered(self):
        if len(self.have) < len(self.row_plans[0]):
            self.bit = self.row_plans[0][::-1][len(self.have)]
            self.got = swap(self.value, "row", self.bit)

    def gather(self):
        self.have = sorted(self.have + [self.bit], reverse=True)
        place = self.have.index(self.bit)
        ahead = 1 << place
        width = self.value.shape[-1]
        size = self.value.shape[0] * self.value.shape[1]
        value = self.value.reshape(ahead, size // ahead, width)
        got = self.got.reshape(ahead, size // ahead, width)
        spec = pl.BlockSpec(value.shape, lambda t, b: (0, 0, 0))
        out = jax.ShapeDtypeStruct((ahead, 2, size // ahead, width), BF16)
        self.value = call_with_core(
            pair_kernel,
            (1,),
            [spec, spec],
            pl.BlockSpec(out.shape, lambda t, b: (0, 0, 0, 0)),
            out,
            [value, got],
            order=self.order,
            name="gather",
            limit=VMEM_SMALL,
            scalar=own_bit("row", self.bit),
        ).reshape(1, 2 * size, width)
        self.send_gathered()

    def total(self):
        return self.value[0]


def placed_gather(stream, order):
    return lax.all_gather(placed(stream.share_value, order), "row", axis=0, tiled=True)


def final_kernel(plan, seq_ref, *refs):
    results = len(plan)
    arrays = refs[: len(refs) - 2 * results - 1]
    weights, outs, sums_ref = refs[len(arrays) :][:results], refs[-results - 1 : -1], refs[-1]
    sums = jnp.zeros((sums_ref.shape[1], HDIM), F32)
    for pieces, w_ref, out_ref in zip(plan, weights, outs):
        for piece in pieces:
            if len(piece) > 4:
                array, row, height, at, width, to_row, to = piece
                out_ref[to_row : to_row + height, to : to + width] = arrays[array][
                    row : row + height, at : at + width
                ].astype(F32)
                continue
            array, at, width, to = piece
            total = arrays[array][:, at : at + width].astype(F32)
            out_ref[:, to : to + width] = total
            if w_ref.shape[1] < out_ref.shape[1]:
                continue
            weighted = total * w_ref[:, to : to + width].astype(F32)
            for lane in range(0, width, HDIM):
                sums = sums + weighted[:, lane : lane + HDIM]
    sums_ref[...] = mm(jnp.ones((8, 2 * HDIM), BF16), split(sums), (1, 1))


def final(arrays, plan, weights, order):
    rows = arrays[0].shape[0]
    full = lambda *shape: pl.BlockSpec(shape, lambda t, c: (0, 0))
    return call_with_core(
        partial(final_kernel, plan),
        (1,),
        [full(*array.shape) for array in arrays]
        + [pl.BlockSpec((rows, w.shape[1]), lambda t, c: (c[0], 0)) for w, _ in weights],
        [full(*shape) for _, shape in weights] + [full(8, rows)],
        [jax.ShapeDtypeStruct(shape, F32) for _, shape in weights]
        + [jax.ShapeDtypeStruct((8, rows), F32)],
        [*arrays, *[w for w, _ in weights]],
        order=order,
        name="final",
        cost=3.0,
        scalar=lax.axis_index("seq").astype(jnp.int32).reshape(1),
    )


def half_product(formula, former, latter):
    return jnp.einsum(formula, former, latter, preferred_element_type=F32)


def shortened(value):
    return jax.tree.map(lambda part: part.astype(BF16), value)


def rms_norm(tensor, gain):
    return tensor * lax.rsqrt(jnp.mean(tensor * tensor, axis=-1, keepdims=True) + EPSILON) * gain


def swiglu(gate_up):
    return jax.nn.silu(gate_up[..., :FF]) * gate_up[..., FF:]


def local(
    hidden_in, lengths, norm1_gain, w_qkv, conv_w, w_rates, a_log, dt_bias,
    w_gate, out_gain, w_out, norm2_gain, w_up, w_down, cotangent,
):
    row_count, length = hidden_in.shape[:2]
    level = levels()
    taps = conv_w.astype(F32).T
    norm_column = norm1_gain[:, None]
    positions = row_count * length
    flat = lambda tensor: tensor.reshape(positions, tensor.shape[-1])
    unflat = lambda tensor: tensor.reshape(row_count, length, tensor.shape[-1])
    order = Order()
    normed, col, row, keep, mask, projected = front(
        hidden_in, along(hidden_in[:, length - HALO :], 1), lengths, norm1_gain, w_rates, a_log,
        dt_bias, w_qkv, order,
    )
    q, k, v, t, wu, p, m, device = maps(projected, taps, keep, col, row, mask, level, order)
    maps_shape = (row_count // 2 * HEADS, HDIM, HDIM)
    device = device.reshape((2, 2) + maps_shape)
    other = to_core(device)
    low_maps = jax.ShapeDtypeStruct(maps_shape, BF16)
    high_maps = jax.ShapeDtypeStruct(maps_shape, F32)
    gate = unflat(project(flat(normed), w_gate, order))
    chip_m, chip_b, leaving = whole_call(
        chip_maps_kernel, [device, other], [low_maps, high_maps, low_maps], order, "chip_maps"
    )
    states_in = carried(device, other, (), chip_m, chip_b, leaving, 1, order)
    entering_shape = (row_count // 2, HEADS, HDIM, HDIM)
    states_in = [member.reshape(entering_shape) for member in states_in]
    branch, mixed, states, delta = mix(q, k, wu, p, col, states_in, gate, out_gain, order)
    layer_out, normed2, activated, grad_gate_up, grad_attended, grad_branch = dense(
        flat(branch), flat(hidden_in), w_out, norm2_gain, w_up, w_down, flat(cotangent), order
    )
    grad_mixed, grad_gate, gain_parts, grads = adjoint(
        unflat(grad_branch), mixed, gate, out_gain, q, wu, p, m, col, order
    )
    grad_out_gain = jnp.sum(gain_parts, axis=(0, 1, 2))
    grads = grads.reshape((2,) + maps_shape)
    other_grads = to_core(grads)
    with_other = lambda pair: (pair[0], to_core(pair[1]))
    chip_grad, leaving = whole_call(
        chip_grads_kernel,
        [grads, other_grads, device, other],
        [high_maps, low_maps],
        order,
        "chip_grads",
    )
    done = {}

    def first_hop():
        done["down"] = with_other(down_grads(activated, flat(cotangent), order))

    def second_hop():
        done["up"] = with_other(weight_grads([normed2], [grad_gate_up], order, width=1408))

    def third_hop():
        done["others"] = with_other(
            weight_grads(
                [flat(branch), flat(normed)],
                [grad_attended[None], flat(grad_gate)[None]],
                order,
                width=512,
            )
        )

    adjoints = carried(
        device, other, (grads, other_grads), chip_m, chip_grad, leaving, -1, order,
        [first_hop, second_hop, third_hop],
    )
    adjoints = [member.reshape(entering_shape) for member in adjoints]
    seq = lax.axis_size("seq")
    rows = D // seq
    core = lax.axis_index("seq") % 2
    width = HEADS // 2 * HDIM
    cut = GROUPS * width // 2

    def back_part(first):
        return back(
            first, 2, projected, taps, keep, col, row, mask,
            (q, k, v, t, wu, p, states, delta), grad_mixed, adjoints, order,
        )

    def fix_of(*members):
        gh = jnp.concatenate([member[1] for member in members], axis=3)
        return jnp.pad(along(gh, -1), ((0, 0), (0, 0), (8, 0), (0, 0)))

    tiles = lambda *members: [
        member[0].reshape(GROUPS, positions, member[0].shape[-1]) for member in members
    ]
    up, down, others = done["up"], done["down"], done["others"]
    ups = Stream(order, [[up + (0, 3 * FF // 2)], [up + (3 * FF // 2, FF // 2), down + (0, FF)]])
    ups.along_row(0)
    first = back_part(0)
    second = back_part(2)
    fix_low = fix_of(first, second)
    low = with_other(weight_grads([flat(normed)], tiles(first, second), order, fix_low, cost=1.0))
    ups.along_row_rest()
    third = back_part(4)
    low = Stream(order, [[low + (0, cut), others + (0, D)], [low + (cut, cut), others + (D, D)]])
    low.along_row(0)
    ups.finish_offloaded()
    fourth = back_part(6)
    fix_high = fix_of(third, fourth)
    high = with_other(weight_grads([flat(normed)], tiles(third, fourth), order, fix_high, cost=1.0))
    low.along_row_rest()
    parts = (first, second, third, fourth)
    grad_rates, rate_sums = rates_back([member[3] for member in parts], row, a_log, order)
    grad_w_rates = half_product("rel,rld->ed", grad_rates[:, :24], normed)
    small = jnp.pad(rate_sums[:, :2].T.reshape(1, 2 * HEADS), ((0, 0), (0, HDIM - 2 * HEADS)))
    small = jnp.concatenate([small, grad_out_gain[None]], axis=0)
    grad_conv = jnp.sum(jnp.concatenate([member[2] for member in parts], axis=2), axis=0)[:, :, :4]
    extra = jnp.concatenate(
        [
            jnp.moveaxis(grad_conv, 2, 0).reshape(4, seq, -1).swapaxes(0, 1).reshape(seq, -1, HDIM),
            grad_w_rates.reshape(24, seq, -1).swapaxes(0, 1).reshape(seq, -1, HDIM),
            jnp.broadcast_to(small, (seq, 2, HDIM)),
        ],
        axis=1,
    )
    extra_high = extra.astype(BF16)
    extra = jnp.concatenate([extra_high, (extra - extra_high.astype(F32)).astype(BF16)], axis=2)
    extra_rows = extra.shape[1]
    extra = jnp.pad(extra, ((0, 0), (0, rows - extra_rows), (0, 0)))
    extra = extra.reshape(seq // 2, 2, rows, 2 * HDIM)
    take = lambda index: lax.dynamic_index_in_dim(extra, index, 1, keepdims=False)
    extra = with_other((take(core), take(1 - core)))
    high = Stream(
        order, [[high + (0, cut), extra + (0, 2 * HDIM)], [high + (cut, cut)]], fine=cut
    )
    high.along_row(0)
    low.along_seq(0)
    up_total = placed_gather(ups, order)
    fix = jnp.concatenate([fix_low, fix_high], axis=3)
    w_rates_wide = jnp.pad(w_rates, ((0, 0), (0, grad_rates.shape[1] - w_rates.shape[1])))
    part = input_grad(
        tiles(*parts), fix, w_qkv, 0, 3, [flat(grad_gate), w_gate, grad_rates, w_rates_wide],
        hidden_in, order,
    )
    high.along_row_rest()
    grad_x = input_grad(
        tiles(*parts), fix, w_qkv, 3, GROUPS, [part, hidden_in, norm1_gain[None], grad_attended],
        hidden_in, order,
    )
    low.along_seq_rest()
    high.along_seq(0)
    low.share_found()
    high.along_seq_rest()
    low.gather()
    high.share_found()
    low.gather_rest()
    blocks, height, block = down_blocks(rows)
    up_total, down_total, up_sums = final(
        [up_total],
        [
            [(0, 0, 2 * FF, 0)],
            [
                (0, there[0], height, 2 * FF + there[1], block, here[0], here[1])
                for here, there in blocks
            ],
        ],
        [(w_up, (rows, 2 * FF)), (norm_column, (FF // seq, D))],
        order,
    )
    high.gather()
    high.gather_rest()
    low_total, high_total = low.total(), high.total()
    pieces = []
    for group in range(GROUPS):
        at = group * width
        for begin, end in ((at, min(at + width, cut)), (max(at, cut), at + width)):
            if begin < end:
                to = group * D + begin - at
                past = begin >= cut
                pieces.append((0, begin + D * past, end - begin, to))
                pieces.append((1, begin + 2 * HDIM * past, end - begin, to + width))
    qkv_total, out_total, gate_total, qkv_sums = final(
        [low_total, high_total],
        [pieces, [(0, cut, D, 0)], [(0, 2 * cut + D, D, 0)]],
        [(w_qkv, (rows, GROUPS * D)), (norm_column, (rows, D)), (w_gate, (rows, D))],
        order,
    )
    extra = high_total[:extra_rows, cut : cut + 2 * HDIM].astype(F32)
    extra = extra[:, :HDIM] + extra[:, HDIM:]
    conv_rows = GROUPS * D * 4 // (seq * HDIM)
    conv_total = extra[:conv_rows].reshape(4, -1).T
    rates_total = extra[conv_rows:-2].reshape(24, -1)
    small = extra[-2:]
    layer_out = unflat(layer_out)
    at = lax.axis_index("seq") * rows
    mine = lambda tensor: lax.dynamic_slice_in_dim(tensor, at, rows, 0).astype(F32)
    norm1_total = (
        qkv_sums[0] + jnp.sum(rates_total * mine(w_rates).T, axis=0)
    ) / mine(norm1_gain)
    norm2_total = up_sums[0] / mine(norm2_gain)
    return (
        layer_out,
        grad_x,
        norm1_total,
        qkv_total,
        conv_total,
        rates_total.T,
        small[0, :HEADS],
        small[0, HEADS : 2 * HEADS],
        gate_total,
        small[1],
        out_total,
        norm2_total,
        up_total,
        down_total,
    )


def solution(mesh):
    return jax.shard_map(
        local,
        mesh=mesh,
        in_specs=(
            P("row", "seq", None),
            P("row", None),
            P(),
            P(),
            P(),
            P(),
            P(),
            P(),
            P(),
            P(),
            P(),
            P(),
            P(),
            P(),
            P("row", "seq", None),
        ),
        out_specs=(
            P("row", "seq", None),
            P("row", "seq", None),
            P("seq"),
            P("seq", None),
            P("seq", None),
            P("seq", None),
            P(),
            P(),
            P("seq", None),
            P(),
            P("seq", None),
            P("seq"),
            P("seq", None),
            P("seq", None),
        ),
        check_vma=False,
    )
```
